32 devices in a mesh: groups: 2 (over x), outer: 4 (over z), inner: 4 (over y, core).
Axes of the slice: x: 2, y: 2, z: 4, core: 2. Of those that a mesh axis runs over, the one named last changes fastest.
Arguments:
- q_proj: bfloat16 [16384, 2048], P(('groups', 'outer', 'inner')), parts along dimension 0, may hold values from -4 to 4
- k_proj: bfloat16 [16384, 512], P(('groups', 'outer', 'inner')), parts along dimension 0, may hold values from -4 to 4
- v_proj: bfloat16 [16384, 512], P(('groups', 'outer', 'inner')), parts along dimension 0, may hold values from -6 to 6
- q_taps: float32 [3, 2048], replicated, may hold values from 0.5 to 1.5
- k_taps: float32 [3, 512], replicated, may hold values from 0.5 to 1.5
- v_taps: float32 [3, 512], replicated, may hold values from 0.5 to 1.5
- block_list: int32 [128, 3], P(('groups', 'outer', 'inner')), parts along dimension 0, may hold values from -1 to 63, as said below
Outputs:
- attn_out: bfloat16 [16384, 2048], P(('groups', 'outer', 'inner')), parts along dimension 0
The draws below stay inside these ranges and needn't reach their ends.
There are 2 independent parts, one for each index of `groups`. The reference program is written for one: setup_inputs(seed, part) draws one part's arguments, and reference() takes and returns one part's arrays. A program takes and returns all parts, laid end to end along the dimension named above; an argument that names none is the same for every part. Nothing has to cross between parts.
Inputs may be any that keep to these rules, and one draw needn't show every extreme that they name: `block_list`: row a holds block a and the 1 block before it that exist, then every block b <= a - 2 with b % 64 equal to a phase shared by all rows of a part, the phase below 62; all other entries are -1, and the last row has none.
All inputs are finite; a program needn't handle non-finite values.
Results may differ from the reference program's by a relative error of at most 0.002.
The reference program's roundings to bfloat16 on the way (of `q_conv` and `rounded`) count: a program that leaves them out, or rounds other values in their place, can miss the bound.
Values may be sent and summed in bfloat16 or wider, within the bound.
A program may use at most 64 MiB of HBM per device.

```python
import math
import jax
import jax.numpy as jnp
from jax import lax

HEADS = 16
KV_HEADS = 4
HEAD_DIM = 128
BLOCK = 128
LOCAL = 2
STRIDE = 64
KERNEL = 3
TOKENS = 8192
QW = 2048
KVW = 512
NQB = 64
NLIST = 3


def draw_q_proj(key, part):
    noise = jnp.clip(jax.random.normal(jax.random.fold_in(key, 11), (TOKENS, HEADS, HEAD_DIM), jnp.float32), -4.0, 4.0)
    field = 0.6 * noise
    return field.reshape(TOKENS, HEADS * HEAD_DIM).astype(jnp.bfloat16)


def draw_k_proj(key, part):
    noise = jnp.clip(jax.random.normal(jax.random.fold_in(key, 21), (TOKENS, KV_HEADS, HEAD_DIM), jnp.float32), -4.0, 4.0)
    field = 0.6 * noise
    return field.reshape(TOKENS, KV_HEADS * HEAD_DIM).astype(jnp.bfloat16)


def draw_block_list(key, part):
    phase_id = jax.random.randint(jax.random.fold_in(key, 31), (), 0, STRIDE - LOCAL).astype(jnp.int32)
    row_ids = jnp.arange(NQB, dtype=jnp.int32)[:, None]
    near_ids = row_ids - jnp.arange(LOCAL, dtype=jnp.int32)[None, :]
    near_ids = jnp.where(near_ids >= 0, near_ids, -1)
    far_ids = phase_id + STRIDE * jnp.arange(NQB // STRIDE, dtype=jnp.int32)[None, :]
    far_ids = jnp.where(far_ids <= row_ids - LOCAL, far_ids, -1)
    return jnp.concatenate([near_ids, far_ids], 1).astype(jnp.int32)


def block_scale(stream_key, shape, split, least, high):
    def one(dim, blocks):
        draws = jax.random.uniform(jax.random.fold_in(jax.random.fold_in(stream_key, 6), dim), (blocks,), jnp.float32, least / len(split), high / len(split))
        return jnp.repeat(jnp.exp(draws), shape[dim] // blocks).reshape((-1,) + (1,) * (len(shape) - dim - 1))

    level = one(*split[0])
    for cut in split[1:]:
        level = level * one(*cut)
    return level


def centred(rng, dims, deviation, reach, pieces=(), held_as=jnp.bfloat16):
    drawn = deviation * jax.random.normal(rng, dims, jnp.float32)
    if pieces:
        drawn = drawn * block_scale(rng, dims, pieces, -0.22, 0.18)
    return jnp.clip(drawn, -reach, reach).astype(held_as)


def setup_inputs(seed: int = 0, part: int = 0) -> dict:
    seeds = jax.random.split(jax.random.key(seed), 8)
    own_keys = jax.random.split(jax.random.fold_in(seeds[7], part), 8)
    return {
        "q_proj": draw_q_proj(jax.random.fold_in(jax.random.fold_in(seeds[7], part), 71), part),
        "k_proj": draw_k_proj(jax.random.fold_in(jax.random.fold_in(seeds[7], part), 71), part),
        "v_proj": centred(own_keys[2], (TOKENS, KVW), 1.0, 6.0, ((0, 16),)),
        "q_taps": jnp.clip(1.0 + 0.1 * jax.random.normal(seeds[3], (KERNEL, QW), jnp.float32), 0.5, 1.5),
        "k_taps": jnp.clip(1.0 + 0.1 * jax.random.normal(seeds[4], (KERNEL, KVW), jnp.float32), 0.5, 1.5),
        "v_taps": jnp.clip(1.0 + 0.1 * jax.random.normal(seeds[5], (KERNEL, KVW), jnp.float32), 0.5, 1.5),
        "block_list": draw_block_list(jax.random.fold_in(jax.random.fold_in(seeds[7], part), 71), part),
    }


def conv_rows(source, kernel_taps):
    width = kernel_taps.shape[0]
    row_count = source.shape[0]
    padded = jnp.concatenate([jnp.zeros((width - 1, source.shape[1]), source.dtype), source], 0)
    summed = jnp.zeros((row_count, source.shape[1]), jnp.float32)
    for offset in range(width):
        start = width - 1 - offset
        summed = summed + kernel_taps[offset][None, :] * padded[start:start + row_count].astype(jnp.float32)
    return summed.astype(jnp.bfloat16)

def reference(q_proj, k_proj, v_proj, q_taps, k_taps, v_taps, block_list):
    q_conv = conv_rows(q_proj, q_taps)
    k_conv = conv_rows(k_proj, k_taps)
    v_conv = conv_rows(v_proj, v_taps)
    per_group = HEADS // KV_HEADS
    inv_scale = 1.0 / math.sqrt(HEAD_DIM)
    key_blocks = k_conv.reshape(NQB, BLOCK, KVW)
    value_blocks = v_conv.reshape(NQB, BLOCK, KVW)

    def one_block(block_id):
        entries = block_list[block_id]
        usable = entries >= 0
        clamped = jnp.where(usable, entries, 0).astype(jnp.int32)
        key_block = key_blocks[clamped].reshape(NLIST * BLOCK, KV_HEADS, HEAD_DIM).astype(jnp.float32)
        value_block = value_blocks[clamped].reshape(NLIST * BLOCK, KV_HEADS, HEAD_DIM).astype(jnp.float32)
        query_block = lax.dynamic_slice_in_dim(q_conv, block_id * BLOCK, BLOCK, 0)
        query_block = query_block.reshape(BLOCK, KV_HEADS, per_group, HEAD_DIM).astype(jnp.float32)
        scores = jnp.einsum('qgrd,kgd->grqk', query_block, key_block) * inv_scale
        key_pos = (clamped[:, None] * BLOCK + jnp.arange(BLOCK, dtype=jnp.int32)[None, :]).reshape(-1)
        key_usable = jnp.repeat(usable, BLOCK)
        query_pos = block_id * BLOCK + jnp.arange(BLOCK, dtype=jnp.int32)
        visible = key_usable[None, :] & (key_pos[None, :] <= query_pos[:, None])
        scores = jnp.where(visible, scores, -1e+30)
        peak = lax.optimization_barrier(jnp.max(scores, axis=-1, keepdims=True))
        terms = jnp.where(visible, jnp.exp(scores - peak), 0.0)
        totals = lax.optimization_barrier(jnp.sum(terms, axis=-1))
        rounded = lax.optimization_barrier(terms.astype(jnp.bfloat16)).astype(jnp.float32)
        mixed = jnp.einsum('grqk,kgd->qgrd', rounded, value_block)
        result = mixed / jnp.transpose(totals, (2, 0, 1))[..., None]
        return result.reshape(BLOCK, QW).astype(jnp.bfloat16)
    blocks = lax.map(one_block, jnp.arange(NQB, dtype=jnp.int32))
    return blocks.reshape(TOKENS, QW)
```

```python
import functools
import math

import jax
import jax.numpy as jnp
from jax import lax
from jax.experimental import pallas as pl
from jax.experimental.pallas import tpu as pltpu
from jax.sharding import PartitionSpec as P

HEAD_DIM = 128
BLOCK = 128
LOCAL = 2
STRIDE = 64
HALO = 16
NEG = -1e30
MESH = pl.DeviceIdType.MESH
SCALE = math.log2(math.e) / math.sqrt(HEAD_DIM)
NT = (((1,), (1,)), ((), ()))


def conv(padded, taps):
    wide = padded.astype(jnp.float32)
    total = taps[0:1] * wide[HALO:]
    for j in (1, 2):
        total = total + taps[j : j + 1] * pltpu.roll(wide, j, 0)[HALO:]
    return total.astype(jnp.bfloat16)


def kernel(
    ni, no, list_hbm, q_hbm, k_hbm, v_hbm, qt_hbm, kt_hbm, vt_hbm, outb,
    list_ref, qt_ref, kt_ref, vt_ref, qpad, kvpad, kvc, qs, acc_ref, max_ref, pbuf, wout, win, cand, rbuf, zpiece, zbuf,
    fsum, far, in_sem, tail_s, tail_r, w_s, w_r, sc_s, sc_r, z_s, z_r,
    g_s, g_r,
):
    tokens, qw = q_hbm.shape
    kvw = k_hbm.shape[1]
    groups = kvw // HEAD_DIM
    per_group = qw // kvw
    nb = tokens // BLOCK
    slots = far.shape[1]
    piece_rows, piece_cols = zpiece.shape[1:]
    col_parts = kvw // piece_cols
    before = BLOCK + HALO
    entries = list_ref.shape[1]
    o = lax.axis_index("outer")
    i = lax.axis_index("inner")
    d = o * ni + i
    last = ni * no - 1
    has_next = d < last
    has_prev = d > 0

    def chain(step):
        other = d + step
        return {"outer": other // ni, "inner": lax.rem(other, ni)}

    def inner_peer(r):
        return {"inner": lax.rem(i + r, ni)}

    loads = [
        pltpu.make_async_copy(q_hbm, qpad.at[pl.ds(HALO, tokens)], in_sem.at[0]),
        pltpu.make_async_copy(k_hbm, kvpad.at[0, pl.ds(before, tokens)], in_sem.at[1]),
        pltpu.make_async_copy(v_hbm, kvpad.at[1, pl.ds(before, tokens)], in_sem.at[2]),
        pltpu.make_async_copy(list_hbm, list_ref, in_sem.at[3]),
        pltpu.make_async_copy(qt_hbm, qt_ref, in_sem.at[4]),
        pltpu.make_async_copy(kt_hbm, kt_ref, in_sem.at[5]),
        pltpu.make_async_copy(vt_hbm, vt_ref, in_sem.at[6]),
    ]
    for n in (3, 1, 5, 2, 6, 0, 4):
        loads[n].start()

    barrier = pltpu.get_barrier_semaphore()
    for r in range(1, ni):
        pl.semaphore_signal(barrier, inc=1, device_id=inner_peer(r), device_id_type=MESH)
    for r in range(1, no):
        pl.semaphore_signal(
            barrier, inc=1, device_id={"outer": lax.rem(o + r, no)}, device_id_type=MESH
        )

    @pl.when(has_next)
    def _():
        pl.semaphore_signal(barrier, inc=1, device_id=chain(1), device_id_type=MESH)

    @pl.when(has_prev)
    def _():
        pl.semaphore_signal(barrier, inc=1, device_id=chain(-1), device_id_type=MESH)

    loads[3].wait()
    phase = jnp.int32(-1)
    for b in range(nb):
        for e in range(entries):
            entry = list_ref[b, e]
            distant = (entry >= 0) & (entry <= d * nb + b - LOCAL)
            phase = jnp.maximum(phase, jnp.where(distant, lax.rem(entry, STRIDE), -1))
    for b in range(nb):
        hit = lax.rem((d - 1) * nb + b + STRIDE, STRIDE) == phase
        wout[b : b + 1, :] = jnp.full((1, 128), jnp.where(hit, 1.0, 0.0), jnp.float32)
    if nb < wout.shape[0]:
        wout[nb:, :] = jnp.zeros((wout.shape[0] - nb, 128), jnp.float32)

    @pl.when(d == 0)
    def _():
        qpad[0:HALO, :] = jnp.zeros((HALO, qw), jnp.bfloat16)
        kvpad[:, 0:before, :] = jnp.zeros((2, before, kvw), jnp.bfloat16)

    @pl.when(d == last)
    def _():
        win[...] = jnp.zeros(win.shape, jnp.float32)

    fsum[...] = jnp.zeros(fsum.shape, jnp.bfloat16)

    w_copy = pltpu.make_async_remote_copy(
        wout, win, w_s, w_r, device_id=chain(-1), device_id_type=MESH
    )
    rim = pl.ds(tokens - HALO, HALO)
    body_rows = pl.ds(tokens - before, BLOCK)

    def to_next(src, dst, n):
        return pltpu.make_async_remote_copy(
            src, dst, tail_s.at[n], tail_r.at[n], device_id=chain(1), device_id_type=MESH
        )

    tails = [
        to_next(k_hbm.at[rim], kvpad.at[0, pl.ds(BLOCK, HALO)], 0),
        to_next(v_hbm.at[rim], kvpad.at[1, pl.ds(BLOCK, HALO)], 1),
        to_next(k_hbm.at[body_rows], kvpad.at[0, pl.ds(0, BLOCK)], 2),
        to_next(v_hbm.at[body_rows], kvpad.at[1, pl.ds(0, BLOCK)], 3),
        to_next(q_hbm.at[rim], qpad.at[pl.ds(0, HALO)], 4),
    ]

    def first_sends():
        pl.semaphore_wait(
            barrier,
            ni - 1 + no - 1 + jnp.where(has_next, 1, 0) + jnp.where(has_prev, 1, 0),
        )

        @pl.when(has_prev)
        def _():
            w_copy.start()

        @pl.when(has_next)
        def _():
            for copy in tails:
                copy.start()

    def kv_conv(b):
        rows = slice(b * BLOCK, b * BLOCK + before)
        dst = slice(b * BLOCK, (b + 1) * BLOCK)
        kvc[0, dst, :] = conv(kvpad[0, rows, :], kt_ref[...])
        kvc[1, dst, :] = conv(kvpad[1, rows, :], vt_ref[...])

    for n in (1, 5, 2, 6):
        loads[n].wait()
    for b in range(2, nb + 1):
        kv_conv(b)

    def candidate_step():
        @pl.when(has_prev)
        def _():
            tails[0].wait_recv()
            tails[1].wait_recv()

        kv_conv(1)

        @pl.when(has_next)
        def _():
            w_copy.wait_recv()

        for g in range(groups):
            cols = slice(g * HEAD_DIM, (g + 1) * HEAD_DIM)
            for half in range(2):
                total = jnp.zeros((BLOCK, HEAD_DIM), jnp.float32)
                for b in range(nb):
                    own = jnp.where(lax.rem(d * nb + b, STRIDE) == phase, 1.0, 0.0)
                    weight = jnp.maximum(win[b : b + 1, :], own)
                    rows = slice((b + 1) * BLOCK, (b + 2) * BLOCK)
                    total = total + weight * kvc[half, rows, cols].astype(jnp.float32)
                cand[half, :, cols] = total.astype(jnp.bfloat16)

        for half in range(2):
            for r in range(1, ni):
                scatter(half, r).start()

    def part(index):
        row = pl.multiple_of(index // col_parts * piece_rows, piece_rows)
        col = pl.multiple_of(lax.rem(index, col_parts) * piece_cols, piece_cols)
        return pl.ds(row, piece_rows), pl.ds(col, piece_cols)

    def scatter(half, r):
        return pltpu.make_async_remote_copy(
            cand.at[(half, *part(lax.rem(i + r, ni)))],
            rbuf.at[half, r],
            sc_s.at[half, r],
            sc_r.at[half, r],
            device_id=inner_peer(r),
            device_id_type=MESH,
        )

    def column(half, r):
        return pltpu.make_async_remote_copy(
            zpiece.at[half],
            zbuf.at[half, r],
            z_s.at[half, r],
            z_r.at[half, r],
            device_id={"outer": lax.rem(o + r, no)},
            device_id_type=MESH,
        )

    def gather(half, r):
        return pltpu.make_async_remote_copy(
            fsum.at[half],
            far.at[(half, slice(None), *part(i))],
            g_s.at[half, r],
            g_r.at[half, r],
            device_id=inner_peer(r),
            device_id_type=MESH,
        )

    def column_step(half):
        total = cand[(half, *part(i))].astype(jnp.float32)
        for r in range(1, ni):
            scatter(half, r).wait_recv()
            total = total + rbuf[half, r].astype(jnp.float32)
        zpiece[half] = total.astype(jnp.bfloat16)
        for r in range(1, no):
            pl.when(o + r < no)(column(half, r).start)

    def slot_of(row):
        return lax.rem(row * (ni * nb) // STRIDE, slots)

    def gather_step(half):
        fsum[half, slot_of(o)] = zpiece[half]
        for r in range(1, no):

            @pl.when(o >= r)
            def _():
                column(half, r).wait_recv()
                at = slot_of(o - r)
                fsum[half, at] = (
                    fsum[half, at].astype(jnp.float32) + zbuf[half, r].astype(jnp.float32)
                ).astype(jnp.bfloat16)

        for r in range(1, ni):
            gather(half, r).start()
        far[(half, slice(None), *part(i))] = fsum[half]

    def gather_wait(half):
        for r in range(1, ni):
            gather(half, r).wait_recv()

    loads[0].wait()
    loads[4].wait()

    row_ids = lax.broadcasted_iota(jnp.int32, (BLOCK, BLOCK), 0)
    col_ids = lax.broadcasted_iota(jnp.int32, (BLOCK, BLOCK), 1)
    causal = jnp.concatenate([row_ids >= col_ids] * per_group, 0)
    ones = jnp.ones((LOCAL * BLOCK, HEAD_DIM), jnp.bfloat16)

    def near(step, carry):
        b = jnp.where(step < nb - 2, step + 2, nb - 1 - step)

        @pl.when(b == 0)
        def _():
            @pl.when(has_prev)
            def _():
                tails[2].wait_recv()
                tails[3].wait_recv()
                tails[4].wait_recv()

            kv_conv(0)

        bias = jnp.where((b == 0) & (d == 0), NEG, 0.0)
        base = pl.multiple_of(b * BLOCK, BLOCK)
        for g in range(groups):
            wide = slice(g * per_group * HEAD_DIM, (g + 1) * per_group * HEAD_DIM)
            cols = slice(g * HEAD_DIM, (g + 1) * HEAD_DIM)
            q = conv(qpad[pl.ds(base, BLOCK + HALO), wide], qt_ref[:, wide])
            q = jnp.concatenate(
                [q[:, h * HEAD_DIM : (h + 1) * HEAD_DIM] for h in range(per_group)], 0
            )
            qs[b, g] = q
            k = kvc[0, pl.ds(base, LOCAL * BLOCK), cols]
            v = kvc[1, pl.ds(base, LOCAL * BLOCK), cols]
            s = lax.dot_general(q, k, NT, preferred_element_type=jnp.float32)
            prev = s[:, :BLOCK] + bias
            own = jnp.where(causal, s[:, BLOCK:], NEG)
            peak = jnp.max(jnp.maximum(prev, own), axis=1, keepdims=True)
            p = jnp.concatenate(
                [jnp.exp2((prev - peak) * SCALE), jnp.exp2((own - peak) * SCALE)], 1
            ).astype(jnp.bfloat16)
            acc_ref[b, g] = jnp.dot(
                p, jnp.concatenate([v, ones], 1), preferred_element_type=jnp.float32
            )
            max_ref[b, g] = jnp.broadcast_to(peak, (per_group * BLOCK, HEAD_DIM))

        pl.when(step == 0)(first_sends)
        pl.when(step == 1)(candidate_step)

        @pl.when(step == 2)
        def _():
            column_step(0)
            column_step(1)

        return carry

    lax.fori_loop(0, nb, near, 0)
    gather_step(0)
    gather_step(1)
    gather_wait(0)

    def distant_keys(b, carry):
        biases = []
        for n in range(slots):
            seen = jnp.int32(0)
            for e in range(entries):
                entry = list_ref[b, e]
                hit = (entry >= n * STRIDE) & (entry < (n + 1) * STRIDE)
                hit = hit & (entry <= d * nb + b - LOCAL)
                seen = jnp.where(hit, 1, seen)
            biases.append(jnp.where(seen > 0, 0.0, NEG))
        for g in range(groups):
            cols = slice(g * HEAD_DIM, (g + 1) * HEAD_DIM)
            q = qs[b, g]
            near_peak = max_ref[b, g]
            scores = []
            top = None
            for n in range(slots):
                s = lax.dot_general(q, far[0, n, :, cols], NT, preferred_element_type=jnp.float32)
                s = s + biases[n]
                scores.append(s)
                top = s if top is None else jnp.maximum(top, s)
            peak = jnp.maximum(near_peak, jnp.max(top, axis=1, keepdims=True))
            max_ref[b, g] = jnp.exp2((near_peak - peak) * SCALE)
            for n in range(slots):
                p = jnp.exp2((scores[n] - peak) * SCALE)
                pbuf[b, g, :, n * BLOCK : (n + 1) * BLOCK] = p.astype(jnp.bfloat16)
        return carry

    def distant_values(b, carry):
        base = pl.multiple_of(b * BLOCK, BLOCK)
        for g in range(groups):
            cols = slice(g * HEAD_DIM, (g + 1) * HEAD_DIM)
            both = acc_ref[b, g]
            shrink = max_ref[b, g]
            total = both[:, :HEAD_DIM] * shrink
            count = both[:, HEAD_DIM:] * shrink
            for n in range(slots):
                more = jnp.dot(
                    pbuf[b, g, :, n * BLOCK : (n + 1) * BLOCK],
                    jnp.concatenate([far[1, n, :, cols], ones[:BLOCK]], 1),
                    preferred_element_type=jnp.float32,
                )
                total = total + more[:, :HEAD_DIM]
                count = count + more[:, HEAD_DIM:]
            mixed = (total / count).astype(jnp.bfloat16)
            for h in range(per_group):
                head = g * per_group + h
                outb[pl.ds(base, BLOCK), head * HEAD_DIM : (head + 1) * HEAD_DIM] = mixed[
                    h * BLOCK : (h + 1) * BLOCK
                ]
        return carry

    lax.fori_loop(0, nb, distant_keys, 0)
    gather_wait(1)
    lax.fori_loop(0, nb, distant_values, 0)

    @pl.when(has_prev)
    def _():
        w_copy.wait_send()

    @pl.when(has_next)
    def _():
        for copy in tails:
            copy.wait_send()

    for half in range(2):
        for r in range(1, ni):
            scatter(half, r).wait_send()
            gather(half, r).wait_send()
        for r in range(1, no):
            pl.when(o + r < no)(column(half, r).wait_send)


def paired_kernel(
    no, list_hbm, q_hbm, k_hbm, v_hbm, qt_hbm, kt_hbm, vt_hbm, outb,
    list_ref, qt_ref, kt_ref, vt_ref, qpad, kvpad, kvc, qs, acc_ref, max_ref, pbuf,
    flag_out, flag_in, chip, cand, rrow, rprev, rsum, zrow, zfar, far,
    in_sem, own_sem, fl_s, fl_r, raw_s, raw_r, rim_s, rim_r, tail_s, tail_r,
    a_s, a_r, b_s, b_r, c_s, c_r, d_s, d_r, e_s, e_r,
):
    tokens, qw = q_hbm.shape
    kvw = k_hbm.shape[1]
    groups = kvw // HEAD_DIM
    hw = kvw // 2
    quarter = hw // 2
    per_group = qw // kvw
    nb = tokens // BLOCK
    before = BLOCK + HALO
    entries = list_ref.shape[1]
    o = lax.axis_index("outer")
    i = lax.axis_index("inner")
    y = i // 2
    c = lax.rem(i, 2)
    m = o * 2 + y
    last_chip = no * 2 - 1
    d = o * 4 + i
    has_next = d < 4 * no - 1
    has_prev = d > 0
    chip_next = m < last_chip
    chip_prev = m > 0
    first_core = c == 0
    second_core = c == 1
    odd = lax.rem(o, 2) == 1
    even = lax.rem(o, 2) == 0

    def chip_core(step, core):
        other = m + step
        return {"outer": other // 2, "inner": lax.rem(other, 2) * 2 + core}

    def at(row, col):
        return {"outer": row, "inner": col * 2 + c}

    peer_core = {"inner": i + 1 - 2 * c}
    peer_y = {"inner": lax.rem(i + 2, 4)}
    next_device = {"outer": (d + 1) // 4, "inner": lax.rem(d + 1, 4)}

    def greet(device):
        pl.semaphore_signal(barrier, inc=1, device_id=device, device_id_type=MESH)

    barrier = pltpu.get_barrier_semaphore()
    greet(peer_core)
    greet(peer_y)
    pl.when(chip_next)(lambda: greet(chip_core(1, 0)))
    pl.when(chip_prev)(lambda: greet(chip_core(-1, 1)))

    @pl.when(odd)
    def _():
        greet(at(o - 1, 0))
        greet(at(o - 1, 1))

    for p in range(1, no, 2):

        @pl.when(o > p)
        def _():
            greet(at(p, 0))
            greet(at(p, 1))

    loads = [
        pltpu.make_async_copy(q_hbm, qpad.at[pl.ds(HALO, tokens)], in_sem.at[0]),
        pltpu.make_async_copy(k_hbm, kvpad.at[0, pl.ds(before, tokens)], in_sem.at[1]),
        pltpu.make_async_copy(v_hbm, kvpad.at[1, pl.ds(before, tokens)], in_sem.at[2]),
        pltpu.make_async_copy(list_hbm, list_ref, in_sem.at[3]),
        pltpu.make_async_copy(qt_hbm, qt_ref, in_sem.at[4]),
        pltpu.make_async_copy(kt_hbm, kt_ref, in_sem.at[5]),
        pltpu.make_async_copy(vt_hbm, vt_ref, in_sem.at[6]),
    ]
    half_cols = pl.ds(pl.multiple_of(c * hw, hw), hw)
    peer_cols = pl.ds(pl.multiple_of((1 - c) * hw, hw), hw)
    chip_rows = pl.ds(pl.multiple_of(HALO + c * tokens, HALO), tokens)
    own = [
        pltpu.make_async_copy(x.at[:, half_cols], chip.at[h, chip_rows], own_sem.at[h])
        for h, x in enumerate((k_hbm, v_hbm))
    ]
    for n in (3, 1, 5, 2, 6, 0, 4):
        loads[n].start()
    for copy in own:
        copy.start()

    def remote(src, dst, send, recv, device):
        return pltpu.make_async_remote_copy(
            src, dst, send, recv, device_id=device, device_id_type=MESH
        )

    flag_back = [
        remote(flag_out, flag_in.at[0], fl_s.at[k], fl_r.at[0], chip_core(-1, k)) for k in range(2)
    ]
    flag_peer = remote(flag_out, flag_in.at[1], fl_s.at[2], fl_r.at[1], peer_core)
    raws = [
        remote(x.at[:, peer_cols], chip.at[h, chip_rows], raw_s.at[h], raw_r.at[h], peer_core)
        for h, x in enumerate((k_hbm, v_hbm))
    ]
    rim = pl.ds(tokens - HALO, HALO)
    rims = [
        [
            remote(
                x.at[rim, k * hw : (k + 1) * hw],
                chip.at[h, pl.ds(0, HALO)],
                rim_s.at[k, h],
                rim_r.at[h],
                chip_core(1, k),
            )
            for h, x in enumerate((k_hbm, v_hbm))
        ]
        for k in range(2)
    ]
    tail_rows = pl.ds(tokens - before, before)
    tails = [
        remote(k_hbm.at[tail_rows], kvpad.at[0, pl.ds(0, before)], tail_s.at[0], tail_r.at[0], next_device),
        remote(v_hbm.at[tail_rows], kvpad.at[1, pl.ds(0, before)], tail_s.at[1], tail_r.at[1], next_device),
        remote(q_hbm.at[rim], qpad.at[pl.ds(0, HALO)], tail_s.at[2], tail_r.at[2], next_device),
    ]

    @pl.when(jnp.logical_not(has_prev))
    def _():
        qpad[0:HALO, :] = jnp.zeros((HALO, qw), jnp.bfloat16)
        kvpad[:, 0:before, :] = jnp.zeros((2, before, kvw), jnp.bfloat16)

    @pl.when(jnp.logical_not(chip_prev))
    def _():
        chip[:, 0:HALO, :] = jnp.zeros((2, HALO, hw), jnp.bfloat16)

    @pl.when(jnp.logical_not(chip_next))
    def _():
        flag_in[0] = jnp.full(flag_in.shape[1:], -1, jnp.int32)

    @pl.when(second_core)
    def _():
        flag_in[1] = jnp.full(flag_in.shape[1:], -1, jnp.int32)

    loads[3].wait()
    phase = jnp.int32(-1)
    for b in range(nb):
        for e in range(entries):
            entry = list_ref[b, e]
            distant = (entry >= 0) & (entry <= d * nb + b - LOCAL)
            phase = jnp.maximum(phase, jnp.where(distant, lax.rem(entry, STRIDE), -1))
    flag_out[...] = jnp.full(flag_out.shape, phase, jnp.int32)

    expected = 2 + jnp.where(first_core & chip_prev, 2, 0) + jnp.where(second_core & chip_next, 2, 0)
    expected = expected + jnp.where(even, 2, 2 * (no - 1 - o))
    pl.semaphore_wait(barrier, expected)

    @pl.when(first_core & chip_prev)
    def _():
        for copy in flag_back:
            copy.start()

    @pl.when(second_core)
    def _():
        flag_peer.start()

        @pl.when(chip_next)
        def _():
            for h in range(2):
                for k in range(2):
                    rims[k][h].start()

    for copy in raws:
        copy.start()

    @pl.when(has_next)
    def _():
        for copy in tails:
            copy.start()

    def kv_conv(b):
        rows = slice(b * BLOCK, b * BLOCK + before)
        dst = slice(b * BLOCK, (b + 1) * BLOCK)
        kvc[0, dst, :] = conv(kvpad[0, rows, :], kt_ref[...])
        kvc[1, dst, :] = conv(kvpad[1, rows, :], vt_ref[...])

    def cols_of(col):
        return slice(col * quarter, (col + 1) * quarter)

    def to_peer_site(h):
        return remote(cand.at[h, 1 - y], rrow.at[h], a_s.at[h], a_r.at[h], peer_y)

    def to_odd_row(h, col):
        return remote(cand.at[h, col], rprev.at[h, y], b_s.at[h, col], b_r.at[h, y], at(o + 1, col))

    def to_peer_col(h):
        return remote(rsum.at[h], zrow.at[h], c_s.at[h], c_r.at[h], peer_y)

    def to_later(h, row, col):
        return remote(
            rsum.at[h],
            zfar.at[h, o // 2, y],
            d_s.at[h, row, col],
            d_r.at[h, o // 2, y],
            at(row, col),
        )

    def from_earlier(h, p, col):
        return remote(
            rsum.at[h],
            zfar.at[h, p, col],
            d_s.at[h, 0, 0],
            d_r.at[h, p, col],
            peer_y,
        )

    def to_peer_core(h):
        mine = pl.ds(2 * c, 2)
        return remote(far.at[h, mine], far.at[h, mine], e_s.at[h], e_r.at[h], peer_core)

    def from_peer_core(h):
        theirs = pl.ds(2 - 2 * c, 2)
        return remote(far.at[h, theirs], far.at[h, theirs], e_s.at[h], e_r.at[h], peer_core)

    def candidate_step():
        @pl.when(chip_next)
        def _():
            remote(flag_out, flag_in.at[0], fl_s.at[0], fl_r.at[0], peer_core).wait_recv()

        @pl.when(first_core)
        def _():
            flag_peer.wait_recv()

        known = jnp.maximum(jnp.maximum(flag_in[0, 0:1, :], flag_in[1, 0:1, :]), phase)
        first = m * 2 * nb
        weights = [
            jnp.where(known == first + b, 1.0, 0.0).astype(jnp.bfloat16) for b in range(2 * nb)
        ]
        for h, taps in enumerate((kt_ref, vt_ref)):
            own[h].wait()
            raws[h].wait_recv()

            @pl.when(chip_prev)
            def _():
                rims[0][h].wait_recv()

            raw = weights[0] * chip[h, 0:before, :]
            for b in range(1, 2 * nb):
                raw = raw + weights[b] * chip[h, b * BLOCK : b * BLOCK + before, :]
            total = conv(raw, taps[:, half_cols])
            for col in range(2):
                cand[h, col] = total[:, cols_of(col)]

            @pl.when(even)
            def _():
                for col in range(2):
                    to_odd_row(h, col).start()

            to_peer_site(h).start()

    def site_step(h):
        to_peer_site(h).wait_recv()
        rsum[h] = cand[h, y] + rrow[h]

        @pl.when(odd)
        def _():
            for col in range(2):
                remote(
                    cand.at[h, col], rprev.at[h, col], b_s.at[h, col], b_r.at[h, col], peer_y
                ).wait_recv()
            rsum[h] = rsum[h] + rprev[h, 0] + rprev[h, 1]
            for row in range(no - 1, 0, -1):

                @pl.when(row > o)
                def _():
                    for col in range(2):
                        to_later(h, row, col).start()

        to_peer_col(h).start()

    def final_step(h):
        to_peer_col(h).wait_recv()
        far[h, 2 * c + y] = rsum[h]
        far[h, 2 * c + 1 - y] = zrow[h]
        for p in range(no // 2):

            @pl.when(o > 2 * p + 1)
            def _():
                for col in range(2):
                    from_earlier(h, p, col).wait_recv()
                    far[h, 2 * c + col] = far[h, 2 * c + col] + zfar[h, p, col]

        to_peer_core(h).start()

    for n in (1, 5, 2, 6):
        loads[n].wait()
    for b in range(2, nb + 1):
        kv_conv(b)

    loads[0].wait()
    loads[4].wait()

    row_ids = lax.broadcasted_iota(jnp.int32, (BLOCK, BLOCK), 0)
    col_ids = lax.broadcasted_iota(jnp.int32, (BLOCK, BLOCK), 1)
    causal = jnp.concatenate([row_ids >= col_ids] * per_group, 0)
    ones = jnp.ones((LOCAL * BLOCK, HEAD_DIM), jnp.bfloat16)

    def near(step, carry):
        b = jnp.where(step < nb - 2, step + 2, nb - 1 - step)

        @pl.when(b == 1)
        def _():
            @pl.when(has_prev)
            def _():
                tails[0].wait_recv()
                tails[1].wait_recv()

            kv_conv(1)

        @pl.when(b == 0)
        def _():
            @pl.when(has_prev)
            def _():
                tails[2].wait_recv()

            kv_conv(0)

        bias = jnp.where((b == 0) & (d == 0), NEG, 0.0)
        base = pl.multiple_of(b * BLOCK, BLOCK)
        for g in range(groups):
            wide = slice(g * per_group * HEAD_DIM, (g + 1) * per_group * HEAD_DIM)
            cols = slice(g * HEAD_DIM, (g + 1) * HEAD_DIM)
            q = conv(qpad[pl.ds(base, BLOCK + HALO), wide], qt_ref[:, wide])
            q = jnp.concatenate(
                [q[:, h * HEAD_DIM : (h + 1) * HEAD_DIM] for h in range(per_group)], 0
            )
            qs[b, g] = q
            k = kvc[0, pl.ds(base, LOCAL * BLOCK), cols]
            v = kvc[1, pl.ds(base, LOCAL * BLOCK), cols]
            s = lax.dot_general(q, k, NT, preferred_element_type=jnp.float32)
            prev = s[:, :BLOCK] + bias
            mine = jnp.where(causal, s[:, BLOCK:], NEG)
            peak = jnp.max(jnp.maximum(prev, mine), axis=1, keepdims=True)
            p = jnp.concatenate(
                [jnp.exp2((prev - peak) * SCALE), jnp.exp2((mine - peak) * SCALE)], 1
            ).astype(jnp.bfloat16)
            acc_ref[b, g] = jnp.dot(
                p, jnp.concatenate([v, ones], 1), preferred_element_type=jnp.float32
            )
            max_ref[b, g] = jnp.broadcast_to(peak, (per_group * BLOCK, HEAD_DIM))
            for at_step, at_group, run in HOOKS(candidate_step, site_step, final_step):
                if at_group == g:
                    pl.when(step == at_step)(run)

        return carry

    lax.fori_loop(0, nb, near, 0)
    final_step(0)
    final_step(1)
    from_peer_core(0).wait_recv()

    def distant_keys(b, carry):
        seen = jnp.int32(0)
        for e in range(entries):
            entry = list_ref[b, e]
            seen = jnp.where((entry >= 0) & (entry <= d * nb + b - LOCAL), 1, seen)
        bias = jnp.where(seen > 0, 0.0, NEG)
        for g in range(groups):
            q = qs[b, g]
            near_peak = max_ref[b, g]
            s = lax.dot_general(q, far[0, g], NT, preferred_element_type=jnp.float32) + bias
            peak = jnp.maximum(near_peak, jnp.max(s, axis=1, keepdims=True))
            max_ref[b, g] = jnp.exp2((near_peak - peak) * SCALE)
            pbuf[b, g] = jnp.exp2((s - peak) * SCALE).astype(jnp.bfloat16)
        return carry

    def distant_values(b, carry):
        base = pl.multiple_of(b * BLOCK, BLOCK)
        for g in range(groups):
            both = acc_ref[b, g]
            shrink = max_ref[b, g]
            more = jnp.dot(
                pbuf[b, g],
                jnp.concatenate([far[1, g], ones[:BLOCK]], 1),
                preferred_element_type=jnp.float32,
            )
            total = both[:, :HEAD_DIM] * shrink + more[:, :HEAD_DIM]
            count = both[:, HEAD_DIM:] * shrink + more[:, HEAD_DIM:]
            mixed = (total / count).astype(jnp.bfloat16)
            for h in range(per_group):
                head = g * per_group + h
                outb[pl.ds(base, BLOCK), head * HEAD_DIM : (head + 1) * HEAD_DIM] = mixed[
                    h * BLOCK : (h + 1) * BLOCK
                ]
        return carry

    lax.fori_loop(0, nb, distant_keys, 0)
    from_peer_core(1).wait_recv()
    lax.fori_loop(0, nb, distant_values, 0)

    @pl.when(first_core & chip_prev)
    def _():
        for copy in flag_back:
            copy.wait_send()

    @pl.when(second_core)
    def _():
        flag_peer.wait_send()

        @pl.when(chip_next)
        def _():
            for k in range(2):
                for copy in rims[k]:
                    copy.wait_send()

    @pl.when(has_next)
    def _():
        for copy in tails:
            copy.wait_send()

    for h in range(2):
        raws[h].wait_send()
        to_peer_site(h).wait_send()
        to_peer_col(h).wait_send()
        to_peer_core(h).wait_send()

        @pl.when(even)
        def _():
            for col in range(2):
                to_odd_row(h, col).wait_send()

        @pl.when(odd)
        def _():
            for row in range(1, no):

                @pl.when(row > o)
                def _():
                    for col in range(2):
                        to_later(h, row, col).wait_send()


def HOOKS(candidate_step, site_step, final_step):
    return [
        (0, 2, candidate_step),
        (2, 2, lambda: site_step(0)),
        (3, 1, lambda: site_step(1)),
    ]


def paired_call(arrays, no):
    block_list, q_proj, k_proj = arrays[:3]
    q_taps, k_taps, v_taps = arrays[4:]
    tokens, qw = q_proj.shape
    kvw = k_proj.shape[1]
    nb = tokens // BLOCK
    groups = kvw // HEAD_DIM
    rows = qw // kvw * BLOCK
    hw = kvw // 2
    piece = (BLOCK, hw // 2)
    dma = pltpu.SemaphoreType.DMA
    bf16, f32 = jnp.bfloat16, jnp.float32
    hbm_spec = pl.BlockSpec(memory_space=pltpu.HBM)
    scores = nb * groups * rows * (LOCAL + 1) * BLOCK
    return pl.pallas_call(
        functools.partial(paired_kernel, no),
        out_shape=jax.ShapeDtypeStruct((tokens, qw), bf16),
        in_specs=[hbm_spec] * 7,
        out_specs=pl.BlockSpec(memory_space=pltpu.VMEM),
        scratch_shapes=[
            pltpu.SMEM(block_list.shape, jnp.int32),
            pltpu.VMEM(q_taps.shape, f32),
            pltpu.VMEM(k_taps.shape, f32),
            pltpu.VMEM(v_taps.shape, f32),
            pltpu.VMEM((tokens + HALO, qw), bf16),
            pltpu.VMEM((2, tokens + BLOCK + HALO, kvw), bf16),
            pltpu.VMEM((2, tokens + BLOCK, kvw), bf16),
            pltpu.VMEM((nb, groups, rows, HEAD_DIM), bf16),
            pltpu.VMEM((nb, groups, rows, 2 * HEAD_DIM), f32),
            pltpu.VMEM((nb, groups, rows, HEAD_DIM), f32),
            pltpu.VMEM((nb, groups, rows, BLOCK), bf16),
            pltpu.VMEM((8, hw), jnp.int32),
            pltpu.VMEM((2, 8, hw), jnp.int32),
            pltpu.VMEM((2, 2 * tokens + HALO, hw), bf16),
            pltpu.VMEM((2, 2, *piece), bf16),
            pltpu.VMEM((2, *piece), bf16),
            pltpu.VMEM((2, 2, *piece), bf16),
            pltpu.VMEM((2, *piece), bf16),
            pltpu.VMEM((2, *piece), bf16),
            pltpu.VMEM((2, no // 2, 2, *piece), bf16),
            pltpu.VMEM((2, groups, BLOCK, HEAD_DIM), bf16),
            dma((7,)),
            dma((2,)),
            dma((3,)),
            dma((2,)),
            dma((2,)),
            dma((2,)),
            dma((2, 2)),
            dma((2,)),
            dma((3,)),
            dma((3,)),
            dma((2,)),
            dma((2,)),
            dma((2, 2)),
            dma((2, 2)),
            dma((2,)),
            dma((2,)),
            dma((2, no, 2)),
            dma((2, no // 2, 2)),
            dma((2,)),
            dma((2,)),
        ],
        compiler_params=pltpu.CompilerParams(
            collective_id=0, has_side_effects=True, vmem_limit_bytes=48 * 1024 * 1024
        ),
        cost_estimate=pl.CostEstimate(
            flops=4 * scores * HEAD_DIM,
            bytes_accessed=4 * tokens * qw + 4 * tokens * kvw,
            transcendentals=scores,
        ),
    )(*arrays)


def body(q_proj, k_proj, v_proj, q_taps, k_taps, v_taps, block_list):
    tokens, qw = q_proj.shape
    kvw = k_proj.shape[1]
    ni = lax.axis_size("inner")
    no = lax.axis_size("outer")
    nb = tokens // BLOCK
    groups = kvw // HEAD_DIM
    rows = qw // kvw * BLOCK
    slots = max(1, nb * ni * no // STRIDE)
    piece_rows = max(HALO, BLOCK // ni)
    piece_cols = BLOCK * kvw // (ni * piece_rows)
    piece = (piece_rows, piece_cols)
    dma = pltpu.SemaphoreType.DMA
    bf16, f32 = jnp.bfloat16, jnp.float32
    hbm_spec = pl.BlockSpec(memory_space=pltpu.HBM)
    scores = nb * groups * rows * (LOCAL + slots) * BLOCK
    arrays = [
        pltpu.with_memory_space_constraint(x, pltpu.HBM)
        for x in (block_list, q_proj, k_proj, v_proj, q_taps, k_taps, v_taps)
    ]
    paired = ni == 4 and no % 2 == 0 and nb * ni * no == STRIDE and groups == 4 and nb >= 2
    if paired:
        return paired_call(arrays, no)
    return pl.pallas_call(
        functools.partial(kernel, ni, no),
        out_shape=jax.ShapeDtypeStruct((tokens, qw), bf16),
        in_specs=[hbm_spec] * 7,
        out_specs=pl.BlockSpec(memory_space=pltpu.VMEM),
        scratch_shapes=[
            pltpu.SMEM(block_list.shape, jnp.int32),
            pltpu.VMEM(q_taps.shape, f32),
            pltpu.VMEM(k_taps.shape, f32),
            pltpu.VMEM(v_taps.shape, f32),
            pltpu.VMEM((tokens + HALO, qw), bf16),
            pltpu.VMEM((2, tokens + BLOCK + HALO, kvw), bf16),
            pltpu.VMEM((2, tokens + BLOCK, kvw), bf16),
            pltpu.VMEM((nb, groups, rows, HEAD_DIM), bf16),
            pltpu.VMEM((nb, groups, rows, 2 * HEAD_DIM), f32),
            pltpu.VMEM((nb, groups, rows, HEAD_DIM), f32),
            pltpu.VMEM((nb, groups, rows, slots * BLOCK), bf16),
            pltpu.VMEM((max(8, nb), 128), f32),
            pltpu.VMEM((max(8, nb), 128), f32),
            pltpu.VMEM((2, BLOCK, kvw), bf16),
            pltpu.VMEM((2, ni, *piece), bf16),
            pltpu.VMEM((2, *piece), bf16),
            pltpu.VMEM((2, no, *piece), bf16),
            pltpu.VMEM((2, slots, *piece), bf16),
            pltpu.VMEM((2, slots, BLOCK, kvw), bf16),
            dma((7,)),
            dma((5,)),
            dma((5,)),
            dma,
            dma,
            dma((2, ni)),
            dma((2, ni)),
            dma((2, no)),
            dma((2, no)),
            dma((2, ni)),
            dma((2, ni)),
        ],
        compiler_params=pltpu.CompilerParams(
            collective_id=0, has_side_effects=True, vmem_limit_bytes=48 * 1024 * 1024
        ),
        cost_estimate=pl.CostEstimate(
            flops=4 * scores * HEAD_DIM,
            bytes_accessed=4 * tokens * qw + 4 * tokens * kvw,
            transcendentals=scores,
        ),
    )(*arrays)


def solution(mesh):
    rows = P(("groups", "outer", "inner"), None)
    return jax.shard_map(
        body,
        mesh=mesh,
        in_specs=(rows, rows, rows, P(), P(), P(), rows),
        out_specs=rows,
        check_vma=False,
    )
```

```python
import functools
import math

import jax
import jax.numpy as jnp
from jax import lax
from jax.experimental import pallas as pl
from jax.experimental.pallas import tpu as pltpu
from jax.sharding import PartitionSpec as P

HEAD_DIM = 128
BLOCK = 128
LOCAL = 2
STRIDE = 64
HALO = 16
NEG = -1e30
MESH = pl.DeviceIdType.MESH
SCALE = math.log2(math.e) / math.sqrt(HEAD_DIM)
NT = (((1,), (1,)), ((), ()))


def conv(padded, taps):
    wide = padded.astype(jnp.float32)
    total = taps[0:1] * wide[HALO:]
    for j in (1, 2):
        total = total + taps[j : j + 1] * pltpu.roll(wide, j, 0)[HALO:]
    return total.astype(jnp.bfloat16)


def kernel(
    ni, no, list_hbm, q_hbm, k_hbm, v_hbm, qt_hbm, kt_hbm, vt_hbm, outb,
    list_ref, qt_ref, kt_ref, vt_ref, qpad, kvpad, kvc, qs, acc_ref, max_ref, pbuf, wout, win, cand, rbuf, zpiece, zbuf,
    fsum, far, in_sem, tail_s, tail_r, w_s, w_r, sc_s, sc_r, z_s, z_r,
    g_s, g_r,
):
    tokens, qw = q_hbm.shape
    kvw = k_hbm.shape[1]
    groups = kvw // HEAD_DIM
    per_group = qw // kvw
    nb = tokens // BLOCK
    slots = far.shape[1]
    piece_rows, piece_cols = zpiece.shape[1:]
    col_parts = kvw // piece_cols
    before = BLOCK + HALO
    entries = list_ref.shape[1]
    o = lax.axis_index("outer")
    i = lax.axis_index("inner")
    d = o * ni + i
    last = ni * no - 1
    has_next = d < last
    has_prev = d > 0

    def chain(step):
        other = d + step
        return {"outer": other // ni, "inner": lax.rem(other, ni)}

    def inner_peer(r):
        return {"inner": lax.rem(i + r, ni)}

    loads = [
        pltpu.make_async_copy(q_hbm, qpad.at[pl.ds(HALO, tokens)], in_sem.at[0]),
        pltpu.make_async_copy(k_hbm, kvpad.at[0, pl.ds(before, tokens)], in_sem.at[1]),
        pltpu.make_async_copy(v_hbm, kvpad.at[1, pl.ds(before, tokens)], in_sem.at[2]),
        pltpu.make_async_copy(list_hbm, list_ref, in_sem.at[3]),
        pltpu.make_async_copy(qt_hbm, qt_ref, in_sem.at[4]),
        pltpu.make_async_copy(kt_hbm, kt_ref, in_sem.at[5]),
        pltpu.make_async_copy(vt_hbm, vt_ref, in_sem.at[6]),
    ]
    for n in (3, 1, 5, 2, 6, 0, 4):
        loads[n].start()

    barrier = pltpu.get_barrier_semaphore()
    for r in range(1, ni):
        pl.semaphore_signal(barrier, inc=1, device_id=inner_peer(r), device_id_type=MESH)
    for r in range(1, no):
        pl.semaphore_signal(
            barrier, inc=1, device_id={"outer": lax.rem(o + r, no)}, device_id_type=MESH
        )

    @pl.when(has_next)
    def _():
        pl.semaphore_signal(barrier, inc=1, device_id=chain(1), device_id_type=MESH)

    @pl.when(has_prev)
    def _():
        pl.semaphore_signal(barrier, inc=1, device_id=chain(-1), device_id_type=MESH)

    loads[3].wait()
    phase = jnp.int32(-1)
    for b in range(nb):
        for e in range(entries):
            entry = list_ref[b, e]
            distant = (entry >= 0) & (entry <= d * nb + b - LOCAL)
            phase = jnp.maximum(phase, jnp.where(distant, lax.rem(entry, STRIDE), -1))
    for b in range(nb):
        hit = lax.rem((d - 1) * nb + b + STRIDE, STRIDE) == phase
        wout[b : b + 1, :] = jnp.full((1, 128), jnp.where(hit, 1.0, 0.0), jnp.float32)
    if nb < wout.shape[0]:
        wout[nb:, :] = jnp.zeros((wout.shape[0] - nb, 128), jnp.float32)

    @pl.when(d == 0)
    def _():
        qpad[0:HALO, :] = jnp.zeros((HALO, qw), jnp.bfloat16)
        kvpad[:, 0:before, :] = jnp.zeros((2, before, kvw), jnp.bfloat16)

    @pl.when(d == last)
    def _():
        win[...] = jnp.zeros(win.shape, jnp.float32)

    fsum[...] = jnp.zeros(fsum.shape, jnp.bfloat16)

    w_copy = pltpu.make_async_remote_copy(
        wout, win, w_s, w_r, device_id=chain(-1), device_id_type=MESH
    )
    rim = pl.ds(tokens - HALO, HALO)
    body_rows = pl.ds(tokens - before, BLOCK)

    def to_next(src, dst, n):
        return pltpu.make_async_remote_copy(
            src, dst, tail_s.at[n], tail_r.at[n], device_id=chain(1), device_id_type=MESH
        )

    tails = [
        to_next(k_hbm.at[rim], kvpad.at[0, pl.ds(BLOCK, HALO)], 0),
        to_next(v_hbm.at[rim], kvpad.at[1, pl.ds(BLOCK, HALO)], 1),
        to_next(k_hbm.at[body_rows], kvpad.at[0, pl.ds(0, BLOCK)], 2),
        to_next(v_hbm.at[body_rows], kvpad.at[1, pl.ds(0, BLOCK)], 3),
        to_next(q_hbm.at[rim], qpad.at[pl.ds(0, HALO)], 4),
    ]

    def first_sends():
        pl.semaphore_wait(
            barrier,
            ni - 1 + no - 1 + jnp.where(has_next, 1, 0) + jnp.where(has_prev, 1, 0),
        )

        @pl.when(has_prev)
        def _():
            w_copy.start()

        @pl.when(has_next)
        def _():
            for copy in tails:
                copy.start()

    def kv_conv(b):
        rows = slice(b * BLOCK, b * BLOCK + before)
        dst = slice(b * BLOCK, (b + 1) * BLOCK)
        kvc[0, dst, :] = conv(kvpad[0, rows, :], kt_ref[...])
        kvc[1, dst, :] = conv(kvpad[1, rows, :], vt_ref[...])

    for n in (1, 5, 2, 6):
        loads[n].wait()
    for b in range(2, nb + 1):
        kv_conv(b)

    def candidate_step():
        @pl.when(has_prev)
        def _():
            tails[0].wait_recv()
            tails[1].wait_recv()

        kv_conv(1)

        @pl.when(has_next)
        def _():
            w_copy.wait_recv()

        for g in range(groups):
            cols = slice(g * HEAD_DIM, (g + 1) * HEAD_DIM)
            for half in range(2):
                total = jnp.zeros((BLOCK, HEAD_DIM), jnp.float32)
                for b in range(nb):
                    own = jnp.where(lax.rem(d * nb + b, STRIDE) == phase, 1.0, 0.0)
                    weight = jnp.maximum(win[b : b + 1, :], own)
                    rows = slice((b + 1) * BLOCK, (b + 2) * BLOCK)
                    total = total + weight * kvc[half, rows, cols].astype(jnp.float32)
                cand[half, :, cols] = total.astype(jnp.bfloat16)

        for half in range(2):
            for r in range(1, ni):
                scatter(half, r).start()

    def part(index):
        row = pl.multiple_of(index // col_parts * piece_rows, piece_rows)
        col = pl.multiple_of(lax.rem(index, col_parts) * piece_cols, piece_cols)
        return pl.ds(row, piece_rows), pl.ds(col, piece_cols)

    def scatter(half, r):
        return pltpu.make_async_remote_copy(
            cand.at[(half, *part(lax.rem(i + r, ni)))],
            rbuf.at[half, r],
            sc_s.at[half, r],
            sc_r.at[half, r],
            device_id=inner_peer(r),
            device_id_type=MESH,
        )

    def column(half, r):
        return pltpu.make_async_remote_copy(
            zpiece.at[half],
            zbuf.at[half, r],
            z_s.at[half, r],
            z_r.at[half, r],
            device_id={"outer": lax.rem(o + r, no)},
            device_id_type=MESH,
        )

    def gather(half, r):
        return pltpu.make_async_remote_copy(
            fsum.at[half],
            far.at[(half, slice(None), *part(i))],
            g_s.at[half, r],
            g_r.at[half, r],
            device_id=inner_peer(r),
            device_id_type=MESH,
        )

    def column_step(half):
        total = cand[(half, *part(i))].astype(jnp.float32)
        for r in range(1, ni):
            scatter(half, r).wait_recv()
            total = total + rbuf[half, r].astype(jnp.float32)
        zpiece[half] = total.astype(jnp.bfloat16)
        for r in range(1, no):
            pl.when(o + r < no)(column(half, r).start)

    def slot_of(row):
        return lax.rem(row * (ni * nb) // STRIDE, slots)

    def gather_step(half):
        fsum[half, slot_of(o)] = zpiece[half]
        for r in range(1, no):

            @pl.when(o >= r)
            def _():
                column(half, r).wait_recv()
                at = slot_of(o - r)
                fsum[half, at] = (
                    fsum[half, at].astype(jnp.float32) + zbuf[half, r].astype(jnp.float32)
                ).astype(jnp.bfloat16)

        for r in range(1, ni):
            gather(half, r).start()
        far[(half, slice(None), *part(i))] = fsum[half]

    def gather_wait(half):
        for r in range(1, ni):
            gather(half, r).wait_recv()

    loads[0].wait()
    loads[4].wait()

    row_ids = lax.broadcasted_iota(jnp.int32, (BLOCK, BLOCK), 0)
    col_ids = lax.broadcasted_iota(jnp.int32, (BLOCK, BLOCK), 1)
    causal = jnp.concatenate([row_ids >= col_ids] * per_group, 0)
    ones = jnp.ones((LOCAL * BLOCK, HEAD_DIM), jnp.bfloat16)

    def near(step, carry):
        b = jnp.where(step < nb - 2, step + 2, nb - 1 - step)

        @pl.when(b == 0)
        def _():
            @pl.when(has_prev)
            def _():
                tails[2].wait_recv()
                tails[3].wait_recv()
                tails[4].wait_recv()

            kv_conv(0)

        bias = jnp.where((b == 0) & (d == 0), NEG, 0.0)
        base = pl.multiple_of(b * BLOCK, BLOCK)
        for g in range(groups):
            wide = slice(g * per_group * HEAD_DIM, (g + 1) * per_group * HEAD_DIM)
            cols = slice(g * HEAD_DIM, (g + 1) * HEAD_DIM)
            q = conv(qpad[pl.ds(base, BLOCK + HALO), wide], qt_ref[:, wide])
            q = jnp.concatenate(
                [q[:, h * HEAD_DIM : (h + 1) * HEAD_DIM] for h in range(per_group)], 0
            )
            qs[b, g] = q
            k = kvc[0, pl.ds(base, LOCAL * BLOCK), cols]
            v = kvc[1, pl.ds(base, LOCAL * BLOCK), cols]
            s = lax.dot_general(q, k, NT, preferred_element_type=jnp.float32)
            prev = s[:, :BLOCK] + bias
            own = jnp.where(causal, s[:, BLOCK:], NEG)
            peak = jnp.max(jnp.maximum(prev, own), axis=1, keepdims=True)
            p = jnp.concatenate(
                [jnp.exp2((prev - peak) * SCALE), jnp.exp2((own - peak) * SCALE)], 1
            ).astype(jnp.bfloat16)
            acc_ref[b, g] = jnp.dot(
                p, jnp.concatenate([v, ones], 1), preferred_element_type=jnp.float32
            )
            max_ref[b, g] = jnp.broadcast_to(peak, (per_group * BLOCK, HEAD_DIM))

        pl.when(step == 0)(first_sends)
        pl.when(step == 1)(candidate_step)

        @pl.when(step == 2)
        def _():
            column_step(0)
            column_step(1)

        return carry

    lax.fori_loop(0, nb, near, 0)
    gather_step(0)
    gather_step(1)
    gather_wait(0)

    def distant_keys(b, carry):
        biases = []
        for n in range(slots):
            seen = jnp.int32(0)
            for e in range(entries):
                entry = list_ref[b, e]
                hit = (entry >= n * STRIDE) & (entry < (n + 1) * STRIDE)
                hit = hit & (entry <= d * nb + b - LOCAL)
                seen = jnp.where(hit, 1, seen)
            biases.append(jnp.where(seen > 0, 0.0, NEG))
        for g in range(groups):
            cols = slice(g * HEAD_DIM, (g + 1) * HEAD_DIM)
            q = qs[b, g]
            near_peak = max_ref[b, g]
            scores = []
            top = None
            for n in range(slots):
                s = lax.dot_general(q, far[0, n, :, cols], NT, preferred_element_type=jnp.float32)
                s = s + biases[n]
                scores.append(s)
                top = s if top is None else jnp.maximum(top, s)
            peak = jnp.maximum(near_peak, jnp.max(top, axis=1, keepdims=True))
            max_ref[b, g] = jnp.exp2((near_peak - peak) * SCALE)
            for n in range(slots):
                p = jnp.exp2((scores[n] - peak) * SCALE)
                pbuf[b, g, :, n * BLOCK : (n + 1) * BLOCK] = p.astype(jnp.bfloat16)
        return carry

    def distant_values(b, carry):
        base = pl.multiple_of(b * BLOCK, BLOCK)
        for g in range(groups):
            cols = slice(g * HEAD_DIM, (g + 1) * HEAD_DIM)
            both = acc_ref[b, g]
            shrink = max_ref[b, g]
            total = both[:, :HEAD_DIM] * shrink
            count = both[:, HEAD_DIM:] * shrink
            for n in range(slots):
                more = jnp.dot(
                    pbuf[b, g, :, n * BLOCK : (n + 1) * BLOCK],
                    jnp.concatenate([far[1, n, :, cols], ones[:BLOCK]], 1),
                    preferred_element_type=jnp.float32,
                )
                total = total + more[:, :HEAD_DIM]
                count = count + more[:, HEAD_DIM:]
            mixed = (total / count).astype(jnp.bfloat16)
            for h in range(per_group):
                head = g * per_group + h
                outb[pl.ds(base, BLOCK), head * HEAD_DIM : (head + 1) * HEAD_DIM] = mixed[
                    h * BLOCK : (h + 1) * BLOCK
                ]
        return carry

    lax.fori_loop(0, nb, distant_keys, 0)
    gather_wait(1)
    lax.fori_loop(0, nb, distant_values, 0)

    @pl.when(has_prev)
    def _():
        w_copy.wait_send()

    @pl.when(has_next)
    def _():
        for copy in tails:
            copy.wait_send()

    for half in range(2):
        for r in range(1, ni):
            scatter(half, r).wait_send()
            gather(half, r).wait_send()
        for r in range(1, no):
            pl.when(o + r < no)(column(half, r).wait_send)


ROWS = 4
SUMS = ({0: (1,), 2: (3,)}, {0: (1, 2), 1: (2,)})
SPREADS = ({1: (3, 2)}, {2: (3,)})
SITE_STEPS = ((2, 2), (3, 3))
TAILS_EARLY = True


def dests(row):
    return sorted({r for table in (*SUMS, *SPREADS) for r in table.get(row, ())})


def origins(row):
    return sorted({s for table in (*SUMS, *SPREADS) for s, rows in table.items() if row in rows})


def paired_kernel(
    list_hbm, q_hbm, k_hbm, v_hbm, qt_hbm, kt_hbm, vt_hbm, outb,
    list_ref, qt_ref, kt_ref, vt_ref, qpad, kvpad, kvc, qs, acc_ref, max_ref, pbuf,
    flag_out, flag_in, chip, cand, rrow, rother, rsum, zrow, zfar, far,
    in_sem, own_sem, fl_s, fl_r, raw_s, raw_r, rim_s, rim_r, tail_s, tail_r,
    a_s, a_r, b_s, b_r, c_s, c_r, d_s, d_r, e_s, e_r, ready,
):
    tokens, qw = q_hbm.shape
    kvw = k_hbm.shape[1]
    groups = kvw // HEAD_DIM
    hw = kvw // 2
    quarter = hw // 2
    per_group = qw // kvw
    nb = tokens // BLOCK
    before = BLOCK + HALO
    entries = list_ref.shape[1]
    o = lax.axis_index("outer")
    i = lax.axis_index("inner")
    y = i // 2
    c = lax.rem(i, 2)
    m = o * 2 + y
    no = ROWS
    last_chip = no * 2 - 1
    d = o * 4 + i
    has_next = d < 4 * no - 1
    has_prev = d > 0
    chip_next = m < last_chip
    chip_prev = m > 0
    first_core = c == 0
    second_core = c == 1

    def chip_core(step, core):
        other = m + step
        return {"outer": other // 2, "inner": lax.rem(other, 2) * 2 + core}

    def at(row, col):
        return {"outer": row, "inner": col * 2 + c}

    peer_core = {"inner": i + 1 - 2 * c}
    peer_y = {"inner": lax.rem(i + 2, 4)}
    next_device = {"outer": (d + 1) // 4, "inner": lax.rem(d + 1, 4)}

    barrier = pltpu.get_barrier_semaphore()

    def greet(device):
        pl.semaphore_signal(barrier, inc=1, device_id=device, device_id_type=MESH)

    def call(device):
        pl.semaphore_signal(ready, inc=1, device_id=device, device_id_type=MESH)

    loads = [
        pltpu.make_async_copy(q_hbm, qpad.at[pl.ds(HALO, tokens)], in_sem.at[0]),
        pltpu.make_async_copy(k_hbm, kvpad.at[0, pl.ds(before, tokens)], in_sem.at[1]),
        pltpu.make_async_copy(v_hbm, kvpad.at[1, pl.ds(before, tokens)], in_sem.at[2]),
        pltpu.make_async_copy(list_hbm, list_ref, in_sem.at[3]),
        pltpu.make_async_copy(qt_hbm, qt_ref, in_sem.at[4]),
        pltpu.make_async_copy(kt_hbm, kt_ref, in_sem.at[5]),
        pltpu.make_async_copy(vt_hbm, vt_ref, in_sem.at[6]),
    ]
    half_cols = pl.ds(pl.multiple_of(c * hw, hw), hw)
    peer_cols = pl.ds(pl.multiple_of((1 - c) * hw, hw), hw)
    chip_rows = pl.ds(pl.multiple_of(HALO + c * tokens, HALO), tokens)
    own = [
        pltpu.make_async_copy(x.at[:, half_cols], chip.at[h, chip_rows], own_sem.at[h])
        for h, x in enumerate((k_hbm, v_hbm))
    ]
    loads[3].start()
    greet(peer_core)
    greet(peer_y)

    @pl.when(chip_next)
    def _():
        greet(chip_core(1, 0))
        pl.when(second_core)(lambda: greet(chip_core(1, 1)))

    for row in range(no):
        if dests(row):

            @pl.when(o == row)
            def _():
                for dst in dests(row):
                    greet(at(dst, 0))
                    greet(at(dst, 1))

    for n in (1, 5, 2, 6):
        loads[n].start()
    for copy in own:
        copy.start()
    for n in (0, 4):
        loads[n].start()

    def remote(src, dst, send, recv, device):
        return pltpu.make_async_remote_copy(
            src, dst, send, recv, device_id=device, device_id_type=MESH
        )

    flag_back = [
        remote(flag_out, flag_in.at[0], fl_s.at[k], fl_r.at[0], chip_core(-1, k)) for k in range(2)
    ]
    flag_peer = remote(flag_out, flag_in.at[1], fl_s.at[2], fl_r.at[1], peer_core)
    raws = [
        remote(x.at[:, peer_cols], chip.at[h, chip_rows], raw_s.at[h], raw_r.at[h], peer_core)
        for h, x in enumerate((k_hbm, v_hbm))
    ]
    rim = pl.ds(tokens - HALO, HALO)
    rims = [
        [
            remote(
                x.at[rim, k * hw : (k + 1) * hw],
                chip.at[h, pl.ds(0, HALO)],
                rim_s.at[k, h],
                rim_r.at[h],
                chip_core(1, k),
            )
            for h, x in enumerate((k_hbm, v_hbm))
        ]
        for k in range(2)
    ]
    tail_rows = pl.ds(tokens - before, before)
    tails = [
        remote(k_hbm.at[tail_rows], kvpad.at[0, pl.ds(0, before)], tail_s.at[0], tail_r.at[0], next_device),
        remote(v_hbm.at[tail_rows], kvpad.at[1, pl.ds(0, before)], tail_s.at[1], tail_r.at[1], next_device),
        remote(q_hbm.at[rim], qpad.at[pl.ds(0, HALO)], tail_s.at[2], tail_r.at[2], next_device),
    ]

    @pl.when(jnp.logical_not(has_prev))
    def _():
        qpad[0:HALO, :] = jnp.zeros((HALO, qw), jnp.bfloat16)
        kvpad[:, 0:before, :] = jnp.zeros((2, before, kvw), jnp.bfloat16)

    @pl.when(jnp.logical_not(chip_prev))
    def _():
        chip[:, 0:HALO, :] = jnp.zeros((2, HALO, hw), jnp.bfloat16)

    @pl.when(jnp.logical_not(chip_next))
    def _():
        flag_in[0] = jnp.full(flag_in.shape[1:], -1, jnp.int32)

    @pl.when(second_core)
    def _():
        flag_in[1] = jnp.full(flag_in.shape[1:], -1, jnp.int32)

    expected = 2 + jnp.where(chip_prev, jnp.where(first_core, 2, 1), 0)
    awaited = jnp.where(second_core & chip_next, 2, 0)
    for row in range(no):
        expected = expected + jnp.where(o == row, 2 * len(origins(row)), 0)
        awaited = awaited + jnp.where(o == row, 2 * len(dests(row)), 0)
    pl.semaphore_wait(barrier, expected)
    pl.when(chip_prev)(lambda: call(chip_core(-1, 1)))
    for row in range(no):
        if origins(row):

            @pl.when(o == row)
            def _():
                for src in origins(row):
                    call(at(src, 0))
                    call(at(src, 1))

    for copy in raws:
        copy.start()

    loads[3].wait()
    phase = jnp.int32(-1)
    for b in range(nb):
        for e in range(entries):
            entry = list_ref[b, e]
            distant = (entry >= 0) & (entry <= d * nb + b - LOCAL)
            phase = jnp.maximum(phase, jnp.where(distant, lax.rem(entry, STRIDE), -1))
    flag_out[...] = jnp.full(flag_out.shape, phase, jnp.int32)

    @pl.when(first_core & chip_prev)
    def _():
        for copy in flag_back:
            copy.start()

    pl.when(second_core)(flag_peer.start)
    pl.when(awaited > 0)(lambda: pl.semaphore_wait(ready, awaited))

    @pl.when(second_core & chip_next)
    def _():
        for h in range(2):
            for k in range(2):
                rims[k][h].start()

    def tail_sends():
        @pl.when(has_next)
        def _():
            for copy in tails:
                copy.start()

    if TAILS_EARLY:
        tail_sends()

    def kv_conv(b):
        rows = slice(b * BLOCK, b * BLOCK + before)
        dst = slice(b * BLOCK, (b + 1) * BLOCK)
        kvc[0, dst, :] = conv(kvpad[0, rows, :], kt_ref[...])
        kvc[1, dst, :] = conv(kvpad[1, rows, :], vt_ref[...])

    def cols_of(col):
        return slice(col * quarter, (col + 1) * quarter)

    def to_peer_site(h):
        return remote(cand.at[h, 1 - y], rrow.at[h], a_s.at[h], a_r.at[h], peer_y)

    def to_site(h, row, col):
        return remote(
            cand.at[h, col], rother.at[h, o, y], b_s.at[h, row, col], b_r.at[h, o, y], at(row, col)
        )

    def at_site(h, src, col):
        return remote(
            cand.at[h, col], rother.at[h, src, col], b_s.at[h, 0, col], b_r.at[h, src, col], peer_y
        )

    def to_peer_col(h):
        return remote(rsum.at[h], zrow.at[h], c_s.at[h], c_r.at[h], peer_y)

    def to_later(h, row, col):
        return remote(
            rsum.at[h], zfar.at[h, o, y], d_s.at[h, row, col], d_r.at[h, o, y], at(row, col)
        )

    def from_earlier(h, src, col):
        return remote(
            rsum.at[h], zfar.at[h, src, col], d_s.at[h, 0, 0], d_r.at[h, src, col], peer_y
        )

    def to_peer_core(h):
        mine = pl.ds(2 * c, 2)
        return remote(far.at[h, mine], far.at[h, mine], e_s.at[h], e_r.at[h], peer_core)

    def from_peer_core(h):
        theirs = pl.ds(2 - 2 * c, 2)
        return remote(far.at[h, theirs], far.at[h, theirs], e_s.at[h], e_r.at[h], peer_core)

    def candidate_step():
        @pl.when(chip_next)
        def _():
            remote(flag_out, flag_in.at[0], fl_s.at[0], fl_r.at[0], peer_core).wait_recv()

        @pl.when(first_core)
        def _():
            flag_peer.wait_recv()

        known = jnp.maximum(jnp.maximum(flag_in[0, 0:1, :], flag_in[1, 0:1, :]), phase)
        first = m * 2 * nb
        weights = [
            jnp.where(known == first + b, 1.0, 0.0).astype(jnp.bfloat16) for b in range(2 * nb)
        ]
        for h, taps in enumerate((kt_ref, vt_ref)):
            own[h].wait()
            raws[h].wait_recv()

            @pl.when(chip_prev)
            def _():
                rims[0][h].wait_recv()

            raw = weights[0] * chip[h, 0:before, :]
            for b in range(1, 2 * nb):
                raw = raw + weights[b] * chip[h, b * BLOCK : b * BLOCK + before, :]
            total = conv(raw, taps[:, half_cols])
            for col in range(2):
                cand[h, col] = total[:, cols_of(col)]

            for src, rows in SUMS[h].items():

                @pl.when(o == src)
                def _():
                    for row in rows:
                        for col in range(2):
                            to_site(h, row, col).start()

            to_peer_site(h).start()

        if not TAILS_EARLY:
            tail_sends()

    def site_step(h):
        to_peer_site(h).wait_recv()
        rsum[h] = cand[h, y] + rrow[h]
        for row in range(no):
            sources = [src for src, rows in SUMS[h].items() if row in rows]
            if sources:

                @pl.when(o == row)
                def _():
                    for src in sources:
                        for col in range(2):
                            at_site(h, src, col).wait_recv()
                            rsum[h] = rsum[h] + rother[h, src, col]

        for src, rows in SPREADS[h].items():

            @pl.when(o == src)
            def _():
                for row in rows:
                    for col in range(2):
                        to_later(h, row, col).start()

        to_peer_col(h).start()

    def final_step(h):
        to_peer_col(h).wait_recv()
        far[h, 2 * c + y] = rsum[h]
        far[h, 2 * c + 1 - y] = zrow[h]
        for src, rows in SPREADS[h].items():
            for row in rows:

                @pl.when(o == row)
                def _():
                    for col in range(2):
                        from_earlier(h, src, col).wait_recv()
                        far[h, 2 * c + col] = far[h, 2 * c + col] + zfar[h, src, col]

        to_peer_core(h).start()

    for n in (1, 5, 2, 6):
        loads[n].wait()
    for b in range(2, nb + 1):
        kv_conv(b)
    candidate_step()

    loads[0].wait()
    loads[4].wait()

    row_ids = lax.broadcasted_iota(jnp.int32, (BLOCK, BLOCK), 0)
    col_ids = lax.broadcasted_iota(jnp.int32, (BLOCK, BLOCK), 1)
    causal = jnp.concatenate([row_ids >= col_ids] * per_group, 0)
    ones = jnp.ones((LOCAL * BLOCK, HEAD_DIM), jnp.bfloat16)

    def near(step, carry):
        b = jnp.where(step < nb - 2, step + 2, nb - 1 - step)

        @pl.when(b == 1)
        def _():
            @pl.when(has_prev)
            def _():
                tails[0].wait_recv()
                tails[1].wait_recv()

            kv_conv(1)

        @pl.when(b == 0)
        def _():
            @pl.when(has_prev)
            def _():
                tails[2].wait_recv()

            kv_conv(0)

        bias = jnp.where((b == 0) & (d == 0), NEG, 0.0)
        base = pl.multiple_of(b * BLOCK, BLOCK)
        for g in range(groups):
            wide = slice(g * per_group * HEAD_DIM, (g + 1) * per_group * HEAD_DIM)
            cols = slice(g * HEAD_DIM, (g + 1) * HEAD_DIM)
            q = conv(qpad[pl.ds(base, BLOCK + HALO), wide], qt_ref[:, wide])
            q = jnp.concatenate(
                [q[:, h * HEAD_DIM : (h + 1) * HEAD_DIM] for h in range(per_group)], 0
            )
            qs[b, g] = q
            k = kvc[0, pl.ds(base, LOCAL * BLOCK), cols]
            v = kvc[1, pl.ds(base, LOCAL * BLOCK), cols]
            s = lax.dot_general(q, k, NT, preferred_element_type=jnp.float32)
            prev = s[:, :BLOCK] + bias
            mine = jnp.where(causal, s[:, BLOCK:], NEG)
            peak = jnp.max(jnp.maximum(prev, mine), axis=1, keepdims=True)
            p = jnp.concatenate(
                [jnp.exp2((prev - peak) * SCALE), jnp.exp2((mine - peak) * SCALE)], 1
            ).astype(jnp.bfloat16)
            acc_ref[b, g] = jnp.dot(
                p, jnp.concatenate([v, ones], 1), preferred_element_type=jnp.float32
            )
            max_ref[b, g] = jnp.broadcast_to(peak, (per_group * BLOCK, HEAD_DIM))
            for (at_step, at_group), h in zip(SITE_STEPS, range(2)):
                if at_group == g:
                    pl.when(step == at_step)(functools.partial(site_step, h))

        return carry

    lax.fori_loop(0, nb, near, 0)
    final_step(0)

    def distant_keys(first, b, carry):
        seen = jnp.int32(0)
        for e in range(entries):
            entry = list_ref[b, e]
            seen = jnp.where((entry >= 0) & (entry <= d * nb + b - LOCAL), 1, seen)
        bias = jnp.where(seen > 0, 0.0, NEG)
        for n in range(2):
            g = first + n
            q = qs[b, g]
            near_peak = max_ref[b, g]
            s = lax.dot_general(q, far[0, g], NT, preferred_element_type=jnp.float32) + bias
            peak = jnp.maximum(near_peak, jnp.max(s, axis=1, keepdims=True))
            max_ref[b, g] = jnp.exp2((near_peak - peak) * SCALE)
            pbuf[b, g] = jnp.exp2((s - peak) * SCALE).astype(jnp.bfloat16)
        return carry

    def distant_values(first, b, carry):
        base = pl.multiple_of(b * BLOCK, BLOCK)
        for n in range(2):
            g = first + n
            both = acc_ref[b, g]
            shrink = max_ref[b, g]
            more = jnp.dot(
                pbuf[b, g],
                jnp.concatenate([far[1, g], ones[:BLOCK]], 1),
                preferred_element_type=jnp.float32,
            )
            total = both[:, :HEAD_DIM] * shrink + more[:, :HEAD_DIM]
            count = both[:, HEAD_DIM:] * shrink + more[:, HEAD_DIM:]
            mixed = (total / count).astype(jnp.bfloat16)
            for h in range(per_group):
                col = pl.multiple_of((g * per_group + h) * HEAD_DIM, HEAD_DIM)
                outb[pl.ds(base, BLOCK), pl.ds(col, HEAD_DIM)] = mixed[
                    h * BLOCK : (h + 1) * BLOCK
                ]
        return carry

    mine = 2 * c
    theirs = 2 - 2 * c
    lax.fori_loop(0, nb, functools.partial(distant_keys, mine), 0, unroll=2)
    from_peer_core(0).wait_recv()
    lax.fori_loop(0, nb, functools.partial(distant_keys, theirs), 0, unroll=2)
    final_step(1)
    lax.fori_loop(0, nb, functools.partial(distant_values, mine), 0, unroll=2)
    from_peer_core(1).wait_recv()
    lax.fori_loop(0, nb, functools.partial(distant_values, theirs), 0, unroll=2)

    @pl.when(first_core & chip_prev)
    def _():
        for copy in flag_back:
            copy.wait_send()

    @pl.when(second_core)
    def _():
        flag_peer.wait_send()

        @pl.when(chip_next)
        def _():
            for k in range(2):
                for copy in rims[k]:
                    copy.wait_send()

    @pl.when(has_next)
    def _():
        for copy in tails:
            copy.wait_send()

    for h in range(2):
        raws[h].wait_send()
        to_peer_site(h).wait_send()
        to_peer_col(h).wait_send()
        to_peer_core(h).wait_send()

        for table, copy in ((SUMS, to_site), (SPREADS, to_later)):
            for src, rows in table[h].items():

                @pl.when(o == src)
                def _():
                    for row in rows:
                        for col in range(2):
                            copy(h, row, col).wait_send()


def paired_call(arrays):
    block_list, q_proj, k_proj = arrays[:3]
    q_taps, k_taps, v_taps = arrays[4:]
    tokens, qw = q_proj.shape
    kvw = k_proj.shape[1]
    nb = tokens // BLOCK
    groups = kvw // HEAD_DIM
    rows = qw // kvw * BLOCK
    hw = kvw // 2
    piece = (BLOCK, hw // 2)
    dma = pltpu.SemaphoreType.DMA
    bf16, f32 = jnp.bfloat16, jnp.float32
    hbm_spec = pl.BlockSpec(memory_space=pltpu.HBM)
    scores = nb * groups * rows * (LOCAL + 1) * BLOCK
    return pl.pallas_call(
        paired_kernel,
        out_shape=jax.ShapeDtypeStruct((tokens, qw), bf16),
        in_specs=[hbm_spec] * 7,
        out_specs=pl.BlockSpec(memory_space=pltpu.VMEM),
        scratch_shapes=[
            pltpu.SMEM(block_list.shape, jnp.int32),
            pltpu.VMEM(q_taps.shape, f32),
            pltpu.VMEM(k_taps.shape, f32),
            pltpu.VMEM(v_taps.shape, f32),
            pltpu.VMEM((tokens + HALO, qw), bf16),
            pltpu.VMEM((2, tokens + BLOCK + HALO, kvw), bf16),
            pltpu.VMEM((2, tokens + BLOCK, kvw), bf16),
            pltpu.VMEM((nb, groups, rows, HEAD_DIM), bf16),
            pltpu.VMEM((nb, groups, rows, 2 * HEAD_DIM), f32),
            pltpu.VMEM((nb, groups, rows, HEAD_DIM), f32),
            pltpu.VMEM((nb, groups, rows, BLOCK), bf16),
            pltpu.VMEM((8, hw), jnp.int32),
            pltpu.VMEM((2, 8, hw), jnp.int32),
            pltpu.VMEM((2, 2 * tokens + HALO, hw), bf16),
            pltpu.VMEM((2, 2, *piece), bf16),
            pltpu.VMEM((2, *piece), bf16),
            pltpu.VMEM((2, ROWS, 2, *piece), bf16),
            pltpu.VMEM((2, *piece), bf16),
            pltpu.VMEM((2, *piece), bf16),
            pltpu.VMEM((2, ROWS, 2, *piece), bf16),
            pltpu.VMEM((2, groups, BLOCK, HEAD_DIM), bf16),
            dma((7,)),
            dma((2,)),
            dma((3,)),
            dma((2,)),
            dma((2,)),
            dma((2,)),
            dma((2, 2)),
            dma((2,)),
            dma((3,)),
            dma((3,)),
            dma((2,)),
            dma((2,)),
            dma((2, ROWS, 2)),
            dma((2, ROWS, 2)),
            dma((2,)),
            dma((2,)),
            dma((2, ROWS, 2)),
            dma((2, ROWS, 2)),
            dma((2,)),
            dma((2,)),
            pltpu.SemaphoreType.REGULAR,
        ],
        compiler_params=pltpu.CompilerParams(
            collective_id=0, has_side_effects=True, vmem_limit_bytes=48 * 1024 * 1024
        ),
        cost_estimate=pl.CostEstimate(
            flops=4 * scores * HEAD_DIM,
            bytes_accessed=4 * tokens * qw + 4 * tokens * kvw,
            transcendentals=scores,
        ),
    )(*arrays)


def body(q_proj, k_proj, v_proj, q_taps, k_taps, v_taps, block_list):
    tokens, qw = q_proj.shape
    kvw = k_proj.shape[1]
    ni = lax.axis_size("inner")
    no = lax.axis_size("outer")
    nb = tokens // BLOCK
    groups = kvw // HEAD_DIM
    rows = qw // kvw * BLOCK
    slots = max(1, nb * ni * no // STRIDE)
    piece_rows = max(HALO, BLOCK // ni)
    piece_cols = BLOCK * kvw // (ni * piece_rows)
    piece = (piece_rows, piece_cols)
    dma = pltpu.SemaphoreType.DMA
    bf16, f32 = jnp.bfloat16, jnp.float32
    hbm_spec = pl.BlockSpec(memory_space=pltpu.HBM)
    scores = nb * groups * rows * (LOCAL + slots) * BLOCK
    arrays = [
        pltpu.with_memory_space_constraint(x, pltpu.HBM)
        for x in (block_list, q_proj, k_proj, v_proj, q_taps, k_taps, v_taps)
    ]
    paired = ni == 4 and no == ROWS and nb * ni * no == STRIDE and groups == 4 and nb >= 2
    if paired:
        return paired_call(arrays)
    return pl.pallas_call(
        functools.partial(kernel, ni, no),
        out_shape=jax.ShapeDtypeStruct((tokens, qw), bf16),
        in_specs=[hbm_spec] * 7,
        out_specs=pl.BlockSpec(memory_space=pltpu.VMEM),
        scratch_shapes=[
            pltpu.SMEM(block_list.shape, jnp.int32),
            pltpu.VMEM(q_taps.shape, f32),
            pltpu.VMEM(k_taps.shape, f32),
            pltpu.VMEM(v_taps.shape, f32),
            pltpu.VMEM((tokens + HALO, qw), bf16),
            pltpu.VMEM((2, tokens + BLOCK + HALO, kvw), bf16),
            pltpu.VMEM((2, tokens + BLOCK, kvw), bf16),
            pltpu.VMEM((nb, groups, rows, HEAD_DIM), bf16),
            pltpu.VMEM((nb, groups, rows, 2 * HEAD_DIM), f32),
            pltpu.VMEM((nb, groups, rows, HEAD_DIM), f32),
            pltpu.VMEM((nb, groups, rows, slots * BLOCK), bf16),
            pltpu.VMEM((max(8, nb), 128), f32),
            pltpu.VMEM((max(8, nb), 128), f32),
            pltpu.VMEM((2, BLOCK, kvw), bf16),
            pltpu.VMEM((2, ni, *piece), bf16),
            pltpu.VMEM((2, *piece), bf16),
            pltpu.VMEM((2, no, *piece), bf16),
            pltpu.VMEM((2, slots, *piece), bf16),
            pltpu.VMEM((2, slots, BLOCK, kvw), bf16),
            dma((7,)),
            dma((5,)),
            dma((5,)),
            dma,
            dma,
            dma((2, ni)),
            dma((2, ni)),
            dma((2, no)),
            dma((2, no)),
            dma((2, ni)),
            dma((2, ni)),
        ],
        compiler_params=pltpu.CompilerParams(
            collective_id=0, has_side_effects=True, vmem_limit_bytes=48 * 1024 * 1024
        ),
        cost_estimate=pl.CostEstimate(
            flops=4 * scores * HEAD_DIM,
            bytes_accessed=4 * tokens * qw + 4 * tokens * kvw,
            transcendentals=scores,
        ),
    )(*arrays)


def solution(mesh):
    rows = P(("groups", "outer", "inner"), None)
    return jax.shard_map(
        body,
        mesh=mesh,
        in_specs=(rows, rows, rows, P(), P(), P(), rows),
        out_specs=rows,
        check_vma=False,
    )
```

```python
import functools
import math

import jax
import jax.numpy as jnp
from jax import lax
from jax.experimental import pallas as pl
from jax.experimental.pallas import tpu as pltpu
from jax.sharding import PartitionSpec as P

HEAD_DIM = 128
BLOCK = 128
LOCAL = 2
STRIDE = 64
HALO = 16
NEG = -1e30
MESH = pl.DeviceIdType.MESH
SCALE = math.log2(math.e) / math.sqrt(HEAD_DIM)
NT = (((1,), (1,)), ((), ()))


def conv(padded, taps):
    wide = padded.astype(jnp.float32)
    total = taps[0:1] * wide[HALO:]
    for j in (1, 2):
        total = total + taps[j : j + 1] * pltpu.roll(wide, j, 0)[HALO:]
    return total.astype(jnp.bfloat16)


def kernel(
    ni, no, list_hbm, q_hbm, k_hbm, v_hbm, qt_hbm, kt_hbm, vt_hbm, outb,
    list_ref, qt_ref, kt_ref, vt_ref, qpad, kvpad, kvc, qs, acc_ref, max_ref, pbuf, wout, win, cand, rbuf, zpiece, zbuf,
    fsum, far, in_sem, tail_s, tail_r, w_s, w_r, sc_s, sc_r, z_s, z_r,
    g_s, g_r,
):
    tokens, qw = q_hbm.shape
    kvw = k_hbm.shape[1]
    groups = kvw // HEAD_DIM
    per_group = qw // kvw
    nb = tokens // BLOCK
    slots = far.shape[1]
    piece_rows, piece_cols = zpiece.shape[1:]
    col_parts = kvw // piece_cols
    before = BLOCK + HALO
    entries = list_ref.shape[1]
    o = lax.axis_index("outer")
    i = lax.axis_index("inner")
    d = o * ni + i
    last = ni * no - 1
    has_next = d < last
    has_prev = d > 0

    def chain(step):
        other = d + step
        return {"outer": other // ni, "inner": lax.rem(other, ni)}

    def inner_peer(r):
        return {"inner": lax.rem(i + r, ni)}

    loads = [
        pltpu.make_async_copy(q_hbm, qpad.at[pl.ds(HALO, tokens)], in_sem.at[0]),
        pltpu.make_async_copy(k_hbm, kvpad.at[0, pl.ds(before, tokens)], in_sem.at[1]),
        pltpu.make_async_copy(v_hbm, kvpad.at[1, pl.ds(before, tokens)], in_sem.at[2]),
        pltpu.make_async_copy(list_hbm, list_ref, in_sem.at[3]),
        pltpu.make_async_copy(qt_hbm, qt_ref, in_sem.at[4]),
        pltpu.make_async_copy(kt_hbm, kt_ref, in_sem.at[5]),
        pltpu.make_async_copy(vt_hbm, vt_ref, in_sem.at[6]),
    ]
    for n in (3, 1, 5, 2, 6, 0, 4):
        loads[n].start()

    barrier = pltpu.get_barrier_semaphore()
    for r in range(1, ni):
        pl.semaphore_signal(barrier, inc=1, device_id=inner_peer(r), device_id_type=MESH)
    for r in range(1, no):
        pl.semaphore_signal(
            barrier, inc=1, device_id={"outer": lax.rem(o + r, no)}, device_id_type=MESH
        )

    @pl.when(has_next)
    def _():
        pl.semaphore_signal(barrier, inc=1, device_id=chain(1), device_id_type=MESH)

    @pl.when(has_prev)
    def _():
        pl.semaphore_signal(barrier, inc=1, device_id=chain(-1), device_id_type=MESH)

    loads[3].wait()
    phase = jnp.int32(-1)
    for b in range(nb):
        for e in range(entries):
            entry = list_ref[b, e]
            distant = (entry >= 0) & (entry <= d * nb + b - LOCAL)
            phase = jnp.maximum(phase, jnp.where(distant, lax.rem(entry, STRIDE), -1))
    for b in range(nb):
        hit = lax.rem((d - 1) * nb + b + STRIDE, STRIDE) == phase
        wout[b : b + 1, :] = jnp.full((1, 128), jnp.where(hit, 1.0, 0.0), jnp.float32)
    if nb < wout.shape[0]:
        wout[nb:, :] = jnp.zeros((wout.shape[0] - nb, 128), jnp.float32)

    @pl.when(d == 0)
    def _():
        qpad[0:HALO, :] = jnp.zeros((HALO, qw), jnp.bfloat16)
        kvpad[:, 0:before, :] = jnp.zeros((2, before, kvw), jnp.bfloat16)

    @pl.when(d == last)
    def _():
        win[...] = jnp.zeros(win.shape, jnp.float32)

    fsum[...] = jnp.zeros(fsum.shape, jnp.bfloat16)

    w_copy = pltpu.make_async_remote_copy(
        wout, win, w_s, w_r, device_id=chain(-1), device_id_type=MESH
    )
    rim = pl.ds(tokens - HALO, HALO)
    body_rows = pl.ds(tokens - before, BLOCK)

    def to_next(src, dst, n):
        return pltpu.make_async_remote_copy(
            src, dst, tail_s.at[n], tail_r.at[n], device_id=chain(1), device_id_type=MESH
        )

    tails = [
        to_next(k_hbm.at[rim], kvpad.at[0, pl.ds(BLOCK, HALO)], 0),
        to_next(v_hbm.at[rim], kvpad.at[1, pl.ds(BLOCK, HALO)], 1),
        to_next(k_hbm.at[body_rows], kvpad.at[0, pl.ds(0, BLOCK)], 2),
        to_next(v_hbm.at[body_rows], kvpad.at[1, pl.ds(0, BLOCK)], 3),
        to_next(q_hbm.at[rim], qpad.at[pl.ds(0, HALO)], 4),
    ]

    def first_sends():
        pl.semaphore_wait(
            barrier,
            ni - 1 + no - 1 + jnp.where(has_next, 1, 0) + jnp.where(has_prev, 1, 0),
        )

        @pl.when(has_prev)
        def _():
            w_copy.start()

        @pl.when(has_next)
        def _():
            for copy in tails:
                copy.start()

    def kv_conv(b):
        rows = slice(b * BLOCK, b * BLOCK + before)
        dst = slice(b * BLOCK, (b + 1) * BLOCK)
        kvc[0, dst, :] = conv(kvpad[0, rows, :], kt_ref[...])
        kvc[1, dst, :] = conv(kvpad[1, rows, :], vt_ref[...])

    for n in (1, 5, 2, 6):
        loads[n].wait()
    for b in range(2, nb + 1):
        kv_conv(b)

    def candidate_step():
        @pl.when(has_prev)
        def _():
            tails[0].wait_recv()
            tails[1].wait_recv()

        kv_conv(1)

        @pl.when(has_next)
        def _():
            w_copy.wait_recv()

        for g in range(groups):
            cols = slice(g * HEAD_DIM, (g + 1) * HEAD_DIM)
            for half in range(2):
                total = jnp.zeros((BLOCK, HEAD_DIM), jnp.float32)
                for b in range(nb):
                    own = jnp.where(lax.rem(d * nb + b, STRIDE) == phase, 1.0, 0.0)
                    weight = jnp.maximum(win[b : b + 1, :], own)
                    rows = slice((b + 1) * BLOCK, (b + 2) * BLOCK)
                    total = total + weight * kvc[half, rows, cols].astype(jnp.float32)
                cand[half, :, cols] = total.astype(jnp.bfloat16)

        for half in range(2):
            for r in range(1, ni):
                scatter(half, r).start()

    def part(index):
        row = pl.multiple_of(index // col_parts * piece_rows, piece_rows)
        col = pl.multiple_of(lax.rem(index, col_parts) * piece_cols, piece_cols)
        return pl.ds(row, piece_rows), pl.ds(col, piece_cols)

    def scatter(half, r):
        return pltpu.make_async_remote_copy(
            cand.at[(half, *part(lax.rem(i + r, ni)))],
            rbuf.at[half, r],
            sc_s.at[half, r],
            sc_r.at[half, r],
            device_id=inner_peer(r),
            device_id_type=MESH,
        )

    def column(half, r):
        return pltpu.make_async_remote_copy(
            zpiece.at[half],
            zbuf.at[half, r],
            z_s.at[half, r],
            z_r.at[half, r],
            device_id={"outer": lax.rem(o + r, no)},
            device_id_type=MESH,
        )

    def gather(half, r):
        return pltpu.make_async_remote_copy(
            fsum.at[half],
            far.at[(half, slice(None), *part(i))],
            g_s.at[half, r],
            g_r.at[half, r],
            device_id=inner_peer(r),
            device_id_type=MESH,
        )

    def column_step(half):
        total = cand[(half, *part(i))].astype(jnp.float32)
        for r in range(1, ni):
            scatter(half, r).wait_recv()
            total = total + rbuf[half, r].astype(jnp.float32)
        zpiece[half] = total.astype(jnp.bfloat16)
        for r in range(1, no):
            pl.when(o + r < no)(column(half, r).start)

    def slot_of(row):
        return lax.rem(row * (ni * nb) // STRIDE, slots)

    def gather_step(half):
        fsum[half, slot_of(o)] = zpiece[half]
        for r in range(1, no):

            @pl.when(o >= r)
            def _():
                column(half, r).wait_recv()
                at = slot_of(o - r)
                fsum[half, at] = (
                    fsum[half, at].astype(jnp.float32) + zbuf[half, r].astype(jnp.float32)
                ).astype(jnp.bfloat16)

        for r in range(1, ni):
            gather(half, r).start()
        far[(half, slice(None), *part(i))] = fsum[half]

    def gather_wait(half):
        for r in range(1, ni):
            gather(half, r).wait_recv()

    loads[0].wait()
    loads[4].wait()

    row_ids = lax.broadcasted_iota(jnp.int32, (BLOCK, BLOCK), 0)
    col_ids = lax.broadcasted_iota(jnp.int32, (BLOCK, BLOCK), 1)
    causal = jnp.concatenate([row_ids >= col_ids] * per_group, 0)
    ones = jnp.ones((LOCAL * BLOCK, HEAD_DIM), jnp.bfloat16)

    def near(step, carry):
        b = jnp.where(step < nb - 2, step + 2, nb - 1 - step)

        @pl.when(b == 0)
        def _():
            @pl.when(has_prev)
            def _():
                tails[2].wait_recv()
                tails[3].wait_recv()
                tails[4].wait_recv()

            kv_conv(0)

        bias = jnp.where((b == 0) & (d == 0), NEG, 0.0)
        base = pl.multiple_of(b * BLOCK, BLOCK)
        for g in range(groups):
            wide = slice(g * per_group * HEAD_DIM, (g + 1) * per_group * HEAD_DIM)
            cols = slice(g * HEAD_DIM, (g + 1) * HEAD_DIM)
            q = conv(qpad[pl.ds(base, BLOCK + HALO), wide], qt_ref[:, wide])
            q = jnp.concatenate(
                [q[:, h * HEAD_DIM : (h + 1) * HEAD_DIM] for h in range(per_group)], 0
            )
            qs[b, g] = q
            k = kvc[0, pl.ds(base, LOCAL * BLOCK), cols]
            v = kvc[1, pl.ds(base, LOCAL * BLOCK), cols]
            s = lax.dot_general(q, k, NT, preferred_element_type=jnp.float32)
            prev = s[:, :BLOCK] + bias
            own = jnp.where(causal, s[:, BLOCK:], NEG)
            peak = jnp.max(jnp.maximum(prev, own), axis=1, keepdims=True)
            p = jnp.concatenate(
                [jnp.exp2((prev - peak) * SCALE), jnp.exp2((own - peak) * SCALE)], 1
            ).astype(jnp.bfloat16)
            acc_ref[b, g] = jnp.dot(
                p, jnp.concatenate([v, ones], 1), preferred_element_type=jnp.float32
            )
            max_ref[b, g] = jnp.broadcast_to(peak, (per_group * BLOCK, HEAD_DIM))

        pl.when(step == 0)(first_sends)
        pl.when(step == 1)(candidate_step)

        @pl.when(step == 2)
        def _():
            column_step(0)
            column_step(1)

        return carry

    lax.fori_loop(0, nb, near, 0)
    gather_step(0)
    gather_step(1)
    gather_wait(0)

    def distant_keys(b, carry):
        biases = []
        for n in range(slots):
            seen = jnp.int32(0)
            for e in range(entries):
                entry = list_ref[b, e]
                hit = (entry >= n * STRIDE) & (entry < (n + 1) * STRIDE)
                hit = hit & (entry <= d * nb + b - LOCAL)
                seen = jnp.where(hit, 1, seen)
            biases.append(jnp.where(seen > 0, 0.0, NEG))
        for g in range(groups):
            cols = slice(g * HEAD_DIM, (g + 1) * HEAD_DIM)
            q = qs[b, g]
            near_peak = max_ref[b, g]
            scores = []
            top = None
            for n in range(slots):
                s = lax.dot_general(q, far[0, n, :, cols], NT, preferred_element_type=jnp.float32)
                s = s + biases[n]
                scores.append(s)
                top = s if top is None else jnp.maximum(top, s)
            peak = jnp.maximum(near_peak, jnp.max(top, axis=1, keepdims=True))
            max_ref[b, g] = jnp.exp2((near_peak - peak) * SCALE)
            for n in range(slots):
                p = jnp.exp2((scores[n] - peak) * SCALE)
                pbuf[b, g, :, n * BLOCK : (n + 1) * BLOCK] = p.astype(jnp.bfloat16)
        return carry

    def distant_values(b, carry):
        base = pl.multiple_of(b * BLOCK, BLOCK)
        for g in range(groups):
            cols = slice(g * HEAD_DIM, (g + 1) * HEAD_DIM)
            both = acc_ref[b, g]
            shrink = max_ref[b, g]
            total = both[:, :HEAD_DIM] * shrink
            count = both[:, HEAD_DIM:] * shrink
            for n in range(slots):
                more = jnp.dot(
                    pbuf[b, g, :, n * BLOCK : (n + 1) * BLOCK],
                    jnp.concatenate([far[1, n, :, cols], ones[:BLOCK]], 1),
                    preferred_element_type=jnp.float32,
                )
                total = total + more[:, :HEAD_DIM]
                count = count + more[:, HEAD_DIM:]
            mixed = (total / count).astype(jnp.bfloat16)
            for h in range(per_group):
                head = g * per_group + h
                outb[pl.ds(base, BLOCK), head * HEAD_DIM : (head + 1) * HEAD_DIM] = mixed[
                    h * BLOCK : (h + 1) * BLOCK
                ]
        return carry

    lax.fori_loop(0, nb, distant_keys, 0)
    gather_wait(1)
    lax.fori_loop(0, nb, distant_values, 0)

    @pl.when(has_prev)
    def _():
        w_copy.wait_send()

    @pl.when(has_next)
    def _():
        for copy in tails:
            copy.wait_send()

    for half in range(2):
        for r in range(1, ni):
            scatter(half, r).wait_send()
            gather(half, r).wait_send()
        for r in range(1, no):
            pl.when(o + r < no)(column(half, r).wait_send)


ROWS = 4
SUMS = ({0: (1,), 2: (3,)}, {0: (2, 1), 1: (2,)})
SPREADS = ({1: (3, 2)}, {2: (3,)})
SITE_STEPS = ((2, 2), (3, 3))
LATE = ((2, 3), (1, 3), (0, 2))


def dests(row, late):
    rows = {r for table in (*SUMS, *SPREADS) for r in table.get(row, ())}
    return sorted(r for r in rows if ((row, r) in LATE) == late)


def origins(row, late):
    return [r for r in range(ROWS) if row in dests(r, late)]


def paired_kernel(
    list_hbm, q_hbm, k_hbm, v_hbm, qt_hbm, kt_hbm, vt_hbm, outb,
    list_ref, qt_ref, kt_ref, vt_ref, qpad, kvpad, kvc, qs, acc_ref, max_ref, pbuf,
    flag_out, flag_in, chip, cand, rrow, rother, rsum, zrow, zfar, far,
    in_sem, own_sem, fl_s, fl_r, raw_s, raw_r, rim_s, rim_r, tail_s, tail_r,
    a_s, a_r, b_s, b_r, c_s, c_r, d_s, d_r, e_s, e_r, ready,
):
    tokens, qw = q_hbm.shape
    kvw = k_hbm.shape[1]
    groups = kvw // HEAD_DIM
    hw = kvw // 2
    quarter = hw // 2
    per_group = qw // kvw
    nb = tokens // BLOCK
    before = BLOCK + HALO
    entries = list_ref.shape[1]
    o = lax.axis_index("outer")
    i = lax.axis_index("inner")
    y = i // 2
    c = lax.rem(i, 2)
    m = o * 2 + y
    no = ROWS
    last_chip = no * 2 - 1
    d = o * 4 + i
    has_next = d < 4 * no - 1
    has_prev = d > 0
    chip_next = m < last_chip
    chip_prev = m > 0
    first_core = c == 0
    second_core = c == 1

    def chip_core(step, core):
        other = m + step
        return {"outer": other // 2, "inner": lax.rem(other, 2) * 2 + core}

    def at(row, col):
        return {"outer": row, "inner": col * 2 + c}

    peer_core = {"inner": i + 1 - 2 * c}
    peer_y = {"inner": lax.rem(i + 2, 4)}
    next_device = {"outer": (d + 1) // 4, "inner": lax.rem(d + 1, 4)}

    barrier = pltpu.get_barrier_semaphore()

    def greet(device):
        pl.semaphore_signal(barrier, inc=1, device_id=device, device_id_type=MESH)

    def call(device):
        pl.semaphore_signal(ready, inc=1, device_id=device, device_id_type=MESH)

    loads = [
        pltpu.make_async_copy(q_hbm, qpad.at[pl.ds(HALO, tokens)], in_sem.at[0]),
        pltpu.make_async_copy(k_hbm, kvpad.at[0, pl.ds(before, tokens)], in_sem.at[1]),
        pltpu.make_async_copy(v_hbm, kvpad.at[1, pl.ds(before, tokens)], in_sem.at[2]),
        pltpu.make_async_copy(list_hbm, list_ref, in_sem.at[3]),
        pltpu.make_async_copy(qt_hbm, qt_ref, in_sem.at[4]),
        pltpu.make_async_copy(kt_hbm, kt_ref, in_sem.at[5]),
        pltpu.make_async_copy(vt_hbm, vt_ref, in_sem.at[6]),
    ]
    half_cols = pl.ds(pl.multiple_of(c * hw, hw), hw)
    peer_cols = pl.ds(pl.multiple_of((1 - c) * hw, hw), hw)
    chip_rows = pl.ds(pl.multiple_of(HALO + c * tokens, HALO), tokens)
    own = [
        pltpu.make_async_copy(x.at[:, half_cols], chip.at[h, chip_rows], own_sem.at[h])
        for h, x in enumerate((k_hbm, v_hbm))
    ]
    loads[3].start()
    greet(peer_core)
    greet(peer_y)

    late_next = (y == 1) & functools.reduce(
        jnp.logical_or, [o == row for row in range(no - 1) if (row, row + 1) in LATE]
    )
    late_prev = (y == 0) & functools.reduce(
        jnp.logical_or, [o == row + 1 for row in range(no - 1) if (row, row + 1) in LATE]
    )

    @pl.when(chip_next)
    def _():
        greet(chip_core(1, 0))
        pl.when(second_core & late_next)(lambda: greet(chip_core(1, 1)))

    pl.when(chip_prev & jnp.logical_not(late_prev))(lambda: greet(chip_core(-1, 1)))
    for row in range(no):

        @pl.when(o == row)
        def _():
            for other in origins(row, False) + dests(row, True):
                greet(at(other, 0))
                greet(at(other, 1))

    for n in (1, 5, 2, 6):
        loads[n].start()
    for copy in own:
        copy.start()
    for n in (0, 4):
        loads[n].start()

    def remote(src, dst, send, recv, device):
        return pltpu.make_async_remote_copy(
            src, dst, send, recv, device_id=device, device_id_type=MESH
        )

    flag_back = [
        remote(flag_out, flag_in.at[0], fl_s.at[k], fl_r.at[0], chip_core(-1, k)) for k in range(2)
    ]
    flag_peer = remote(flag_out, flag_in.at[1], fl_s.at[2], fl_r.at[1], peer_core)
    raws = [
        remote(x.at[:, peer_cols], chip.at[h, chip_rows], raw_s.at[h], raw_r.at[h], peer_core)
        for h, x in enumerate((k_hbm, v_hbm))
    ]
    rim = pl.ds(tokens - HALO, HALO)
    rims = [
        [
            remote(
                x.at[rim, k * hw : (k + 1) * hw],
                chip.at[h, pl.ds(0, HALO)],
                rim_s.at[k, h],
                rim_r.at[h],
                chip_core(1, k),
            )
            for h, x in enumerate((k_hbm, v_hbm))
        ]
        for k in range(2)
    ]
    tail_rows = pl.ds(tokens - before, before)
    tails = [
        remote(k_hbm.at[tail_rows], kvpad.at[0, pl.ds(0, before)], tail_s.at[0], tail_r.at[0], next_device),
        remote(v_hbm.at[tail_rows], kvpad.at[1, pl.ds(0, before)], tail_s.at[1], tail_r.at[1], next_device),
        remote(q_hbm.at[rim], qpad.at[pl.ds(0, HALO)], tail_s.at[2], tail_r.at[2], next_device),
    ]

    @pl.when(jnp.logical_not(has_prev))
    def _():
        qpad[0:HALO, :] = jnp.zeros((HALO, qw), jnp.bfloat16)
        kvpad[:, 0:before, :] = jnp.zeros((2, before, kvw), jnp.bfloat16)

    @pl.when(jnp.logical_not(chip_prev))
    def _():
        chip[:, 0:HALO, :] = jnp.zeros((2, HALO, hw), jnp.bfloat16)

    @pl.when(jnp.logical_not(chip_next))
    def _():
        flag_in[0] = jnp.full(flag_in.shape[1:], -1, jnp.int32)

    @pl.when(second_core)
    def _():
        flag_in[1] = jnp.full(flag_in.shape[1:], -1, jnp.int32)

    expected = 2 + jnp.where(chip_prev & first_core, 2, 0)
    expected = expected + jnp.where(chip_prev & late_prev & second_core, 1, 0)
    sends_on = second_core & chip_next
    expected = expected + jnp.where(sends_on & jnp.logical_not(late_next), 2, 0)
    awaited = jnp.where(sends_on & late_next, 2, 0)
    for row in range(no):
        met = 2 * len(dests(row, False) + origins(row, True))
        expected = expected + jnp.where(o == row, met, 0)
        awaited = awaited + jnp.where(o == row, 2 * len(dests(row, True)), 0)
    pl.semaphore_wait(barrier, expected)
    pl.when(chip_prev & late_prev)(lambda: call(chip_core(-1, 1)))
    for row in range(no):
        if origins(row, True):

            @pl.when(o == row)
            def _():
                for src in origins(row, True):
                    call(at(src, 0))
                    call(at(src, 1))

    for copy in raws:
        copy.start()

    loads[3].wait()
    phase = jnp.int32(-1)
    for b in range(nb):
        for e in range(entries):
            entry = list_ref[b, e]
            distant = (entry >= 0) & (entry <= d * nb + b - LOCAL)
            phase = jnp.maximum(phase, jnp.where(distant, lax.rem(entry, STRIDE), -1))
    flag_out[...] = jnp.full(flag_out.shape, phase, jnp.int32)

    @pl.when(first_core & chip_prev)
    def _():
        for copy in flag_back:
            copy.start()

    pl.when(second_core)(flag_peer.start)
    def next_sends():
        @pl.when(sends_on)
        def _():
            for h in range(2):
                for k in range(2):
                    rims[k][h].start()

        @pl.when(has_next)
        def _():
            for copy in tails:
                copy.start()

    held_back = sends_on & late_next
    pl.when(jnp.logical_not(held_back))(next_sends)

    def kv_conv(b):
        rows = slice(b * BLOCK, b * BLOCK + before)
        dst = slice(b * BLOCK, (b + 1) * BLOCK)
        kvc[0, dst, :] = conv(kvpad[0, rows, :], kt_ref[...])
        kvc[1, dst, :] = conv(kvpad[1, rows, :], vt_ref[...])

    def cols_of(col):
        return slice(col * quarter, (col + 1) * quarter)

    def to_peer_site(h):
        return remote(cand.at[h, 1 - y], rrow.at[h], a_s.at[h], a_r.at[h], peer_y)

    def to_site(h, row, col):
        return remote(
            cand.at[h, col], rother.at[h, o, y], b_s.at[h, row, col], b_r.at[h, o, y], at(row, col)
        )

    def at_site(h, src, col):
        return remote(
            cand.at[h, col], rother.at[h, src, col], b_s.at[h, 0, col], b_r.at[h, src, col], peer_y
        )

    def to_peer_col(h):
        return remote(rsum.at[h], zrow.at[h], c_s.at[h], c_r.at[h], peer_y)

    def to_later(h, row, col):
        return remote(
            rsum.at[h], zfar.at[h, o, y], d_s.at[h, row, col], d_r.at[h, o, y], at(row, col)
        )

    def from_earlier(h, src, col):
        return remote(
            rsum.at[h], zfar.at[h, src, col], d_s.at[h, 0, 0], d_r.at[h, src, col], peer_y
        )

    def to_peer_core(h):
        mine = pl.ds(2 * c, 2)
        return remote(far.at[h, mine], far.at[h, mine], e_s.at[h], e_r.at[h], peer_core)

    def from_peer_core(h):
        theirs = pl.ds(2 - 2 * c, 2)
        return remote(far.at[h, theirs], far.at[h, theirs], e_s.at[h], e_r.at[h], peer_core)

    def candidate_step():
        pl.when(awaited > 0)(lambda: pl.semaphore_wait(ready, awaited))
        pl.when(held_back)(next_sends)

        @pl.when(chip_next)
        def _():
            remote(flag_out, flag_in.at[0], fl_s.at[0], fl_r.at[0], peer_core).wait_recv()

        @pl.when(first_core)
        def _():
            flag_peer.wait_recv()

        known = jnp.maximum(jnp.maximum(flag_in[0, 0:1, :], flag_in[1, 0:1, :]), phase)
        first = m * 2 * nb
        weights = [
            jnp.where(known == first + b, 1.0, 0.0).astype(jnp.bfloat16) for b in range(2 * nb)
        ]
        for h, taps in enumerate((kt_ref, vt_ref)):
            own[h].wait()
            raws[h].wait_recv()

            @pl.when(chip_prev)
            def _():
                rims[0][h].wait_recv()

            raw = weights[0] * chip[h, 0:before, :]
            for b in range(1, 2 * nb):
                raw = raw + weights[b] * chip[h, b * BLOCK : b * BLOCK + before, :]
            total = conv(raw, taps[:, half_cols])
            for col in range(2):
                cand[h, col] = total[:, cols_of(col)]

            for src, rows in SUMS[h].items():

                @pl.when(o == src)
                def _():
                    for row in rows:
                        for col in range(2):
                            to_site(h, row, col).start()

            to_peer_site(h).start()

    def site_step(h):
        to_peer_site(h).wait_recv()
        rsum[h] = cand[h, y] + rrow[h]
        for row in range(no):
            sources = [src for src, rows in SUMS[h].items() if row in rows]
            if sources:

                @pl.when(o == row)
                def _():
                    for src in sources:
                        for col in range(2):
                            at_site(h, src, col).wait_recv()
                            rsum[h] = rsum[h] + rother[h, src, col]

        for src, rows in SPREADS[h].items():

            @pl.when(o == src)
            def _():
                for row in rows:
                    for col in range(2):
                        to_later(h, row, col).start()

        to_peer_col(h).start()

    def final_step(h):
        to_peer_col(h).wait_recv()
        far[h, 2 * c + y] = rsum[h]
        far[h, 2 * c + 1 - y] = zrow[h]
        for src, rows in SPREADS[h].items():
            for row in rows:

                @pl.when(o == row)
                def _():
                    for col in range(2):
                        from_earlier(h, src, col).wait_recv()
                        far[h, 2 * c + col] = far[h, 2 * c + col] + zfar[h, src, col]

        to_peer_core(h).start()

    for n in (1, 5, 2, 6):
        loads[n].wait()
    for b in range(2, nb + 1):
        kv_conv(b)
    candidate_step()

    loads[0].wait()
    loads[4].wait()

    row_ids = lax.broadcasted_iota(jnp.int32, (BLOCK, BLOCK), 0)
    col_ids = lax.broadcasted_iota(jnp.int32, (BLOCK, BLOCK), 1)
    causal = jnp.concatenate([row_ids >= col_ids] * per_group, 0)
    ones = jnp.ones((LOCAL * BLOCK, HEAD_DIM), jnp.bfloat16)

    def near(step, carry):
        b = jnp.where(step < nb - 2, step + 2, nb - 1 - step)

        @pl.when(b == 1)
        def _():
            @pl.when(has_prev)
            def _():
                tails[0].wait_recv()
                tails[1].wait_recv()

            kv_conv(1)

        @pl.when(b == 0)
        def _():
            @pl.when(has_prev)
            def _():
                tails[2].wait_recv()

            kv_conv(0)

        bias = jnp.where((b == 0) & (d == 0), NEG, 0.0)
        base = pl.multiple_of(b * BLOCK, BLOCK)
        for g in range(groups):
            wide = slice(g * per_group * HEAD_DIM, (g + 1) * per_group * HEAD_DIM)
            cols = slice(g * HEAD_DIM, (g + 1) * HEAD_DIM)
            q = conv(qpad[pl.ds(base, BLOCK + HALO), wide], qt_ref[:, wide])
            q = jnp.concatenate(
                [q[:, h * HEAD_DIM : (h + 1) * HEAD_DIM] for h in range(per_group)], 0
            )
            qs[b, g] = q
            k = kvc[0, pl.ds(base, LOCAL * BLOCK), cols]
            v = kvc[1, pl.ds(base, LOCAL * BLOCK), cols]
            s = lax.dot_general(q, k, NT, preferred_element_type=jnp.float32)
            prev = s[:, :BLOCK] + bias
            mine = jnp.where(causal, s[:, BLOCK:], NEG)
            peak = jnp.max(jnp.maximum(prev, mine), axis=1, keepdims=True)
            p = jnp.concatenate(
                [jnp.exp2((prev - peak) * SCALE), jnp.exp2((mine - peak) * SCALE)], 1
            ).astype(jnp.bfloat16)
            acc_ref[b, g] = jnp.dot(
                p, jnp.concatenate([v, ones], 1), preferred_element_type=jnp.float32
            )
            max_ref[b, g] = jnp.broadcast_to(peak, (per_group * BLOCK, HEAD_DIM))
            for (at_step, at_group), h in zip(SITE_STEPS, range(2)):
                if at_group == g:
                    pl.when(step == at_step)(functools.partial(site_step, h))

        return carry

    lax.fori_loop(0, nb, near, 0)
    final_step(0)

    def distant_keys(first, b, carry):
        seen = jnp.int32(0)
        for e in range(entries):
            entry = list_ref[b, e]
            seen = jnp.where((entry >= 0) & (entry <= d * nb + b - LOCAL), 1, seen)
        bias = jnp.where(seen > 0, 0.0, NEG)
        for n in range(2):
            g = first + n
            q = qs[b, g]
            near_peak = max_ref[b, g]
            s = lax.dot_general(q, far[0, g], NT, preferred_element_type=jnp.float32) + bias
            peak = jnp.maximum(near_peak, jnp.max(s, axis=1, keepdims=True))
            max_ref[b, g] = jnp.exp2((near_peak - peak) * SCALE)
            pbuf[b, g] = jnp.exp2((s - peak) * SCALE).astype(jnp.bfloat16)
        return carry

    def distant_values(first, b, carry):
        base = pl.multiple_of(b * BLOCK, BLOCK)
        for n in range(2):
            g = first + n
            both = acc_ref[b, g]
            shrink = max_ref[b, g]
            more = jnp.dot(
                pbuf[b, g],
                jnp.concatenate([far[1, g], ones[:BLOCK]], 1),
                preferred_element_type=jnp.float32,
            )
            total = both[:, :HEAD_DIM] * shrink + more[:, :HEAD_DIM]
            count = both[:, HEAD_DIM:] * shrink + more[:, HEAD_DIM:]
            mixed = (total / count).astype(jnp.bfloat16)
            for h in range(per_group):
                col = pl.multiple_of((g * per_group + h) * HEAD_DIM, HEAD_DIM)
                outb[pl.ds(base, BLOCK), pl.ds(col, HEAD_DIM)] = mixed[
                    h * BLOCK : (h + 1) * BLOCK
                ]
        return carry

    mine = 2 * c
    theirs = 2 - 2 * c
    lax.fori_loop(0, nb, functools.partial(distant_keys, mine), 0, unroll=2)
    from_peer_core(0).wait_recv()
    lax.fori_loop(0, nb, functools.partial(distant_keys, theirs), 0, unroll=2)
    final_step(1)
    lax.fori_loop(0, nb, functools.partial(distant_values, mine), 0, unroll=2)
    from_peer_core(1).wait_recv()
    lax.fori_loop(0, nb, functools.partial(distant_values, theirs), 0, unroll=2)

    @pl.when(first_core & chip_prev)
    def _():
        for copy in flag_back:
            copy.wait_send()

    @pl.when(second_core)
    def _():
        flag_peer.wait_send()

        @pl.when(chip_next)
        def _():
            for k in range(2):
                for copy in rims[k]:
                    copy.wait_send()

    @pl.when(has_next)
    def _():
        for copy in tails:
            copy.wait_send()

    for h in range(2):
        raws[h].wait_send()
        to_peer_site(h).wait_send()
        to_peer_col(h).wait_send()
        to_peer_core(h).wait_send()

        for table, copy in ((SUMS, to_site), (SPREADS, to_later)):
            for src, rows in table[h].items():

                @pl.when(o == src)
                def _():
                    for row in rows:
                        for col in range(2):
                            copy(h, row, col).wait_send()


def paired_call(arrays):
    block_list, q_proj, k_proj = arrays[:3]
    q_taps, k_taps, v_taps = arrays[4:]
    tokens, qw = q_proj.shape
    kvw = k_proj.shape[1]
    nb = tokens // BLOCK
    groups = kvw // HEAD_DIM
    rows = qw // kvw * BLOCK
    hw = kvw // 2
    piece = (BLOCK, hw // 2)
    dma = pltpu.SemaphoreType.DMA
    bf16, f32 = jnp.bfloat16, jnp.float32
    hbm_spec = pl.BlockSpec(memory_space=pltpu.HBM)
    scores = nb * groups * rows * (LOCAL + 1) * BLOCK
    return pl.pallas_call(
        paired_kernel,
        out_shape=jax.ShapeDtypeStruct((tokens, qw), bf16),
        in_specs=[hbm_spec] * 7,
        out_specs=pl.BlockSpec(memory_space=pltpu.VMEM),
        scratch_shapes=[
            pltpu.SMEM(block_list.shape, jnp.int32),
            pltpu.VMEM(q_taps.shape, f32),
            pltpu.VMEM(k_taps.shape, f32),
            pltpu.VMEM(v_taps.shape, f32),
            pltpu.VMEM((tokens + HALO, qw), bf16),
            pltpu.VMEM((2, tokens + BLOCK + HALO, kvw), bf16),
            pltpu.VMEM((2, tokens + BLOCK, kvw), bf16),
            pltpu.VMEM((nb, groups, rows, HEAD_DIM), bf16),
            pltpu.VMEM((nb, groups, rows, 2 * HEAD_DIM), f32),
            pltpu.VMEM((nb, groups, rows, HEAD_DIM), f32),
            pltpu.VMEM((nb, groups, rows, BLOCK), bf16),
            pltpu.VMEM((8, hw), jnp.int32),
            pltpu.VMEM((2, 8, hw), jnp.int32),
            pltpu.VMEM((2, 2 * tokens + HALO, hw), bf16),
            pltpu.VMEM((2, 2, *piece), bf16),
            pltpu.VMEM((2, *piece), bf16),
            pltpu.VMEM((2, ROWS, 2, *piece), bf16),
            pltpu.VMEM((2, *piece), bf16),
            pltpu.VMEM((2, *piece), bf16),
            pltpu.VMEM((2, ROWS, 2, *piece), bf16),
            pltpu.VMEM((2, groups, BLOCK, HEAD_DIM), bf16),
            dma((7,)),
            dma((2,)),
            dma((3,)),
            dma((2,)),
            dma((2,)),
            dma((2,)),
            dma((2, 2)),
            dma((2,)),
            dma((3,)),
            dma((3,)),
            dma((2,)),
            dma((2,)),
            dma((2, ROWS, 2)),
            dma((2, ROWS, 2)),
            dma((2,)),
            dma((2,)),
            dma((2, ROWS, 2)),
            dma((2, ROWS, 2)),
            dma((2,)),
            dma((2,)),
            pltpu.SemaphoreType.REGULAR,
        ],
        compiler_params=pltpu.CompilerParams(
            collective_id=0, has_side_effects=True, vmem_limit_bytes=48 * 1024 * 1024
        ),
        cost_estimate=pl.CostEstimate(
            flops=4 * scores * HEAD_DIM,
            bytes_accessed=4 * tokens * qw + 4 * tokens * kvw,
            transcendentals=scores,
        ),
    )(*arrays)


def body(q_proj, k_proj, v_proj, q_taps, k_taps, v_taps, block_list):
    tokens, qw = q_proj.shape
    kvw = k_proj.shape[1]
    ni = lax.axis_size("inner")
    no = lax.axis_size("outer")
    nb = tokens // BLOCK
    groups = kvw // HEAD_DIM
    rows = qw // kvw * BLOCK
    slots = max(1, nb * ni * no // STRIDE)
    piece_rows = max(HALO, BLOCK // ni)
    piece_cols = BLOCK * kvw // (ni * piece_rows)
    piece = (piece_rows, piece_cols)
    dma = pltpu.SemaphoreType.DMA
    bf16, f32 = jnp.bfloat16, jnp.float32
    hbm_spec = pl.BlockSpec(memory_space=pltpu.HBM)
    scores = nb * groups * rows * (LOCAL + slots) * BLOCK
    arrays = [
        pltpu.with_memory_space_constraint(x, pltpu.HBM)
        for x in (block_list, q_proj, k_proj, v_proj, q_taps, k_taps, v_taps)
    ]
    paired = ni == 4 and no == ROWS and nb * ni * no == STRIDE and groups == 4 and nb >= 2
    if paired:
        return paired_call(arrays)
    return pl.pallas_call(
        functools.partial(kernel, ni, no),
        out_shape=jax.ShapeDtypeStruct((tokens, qw), bf16),
        in_specs=[hbm_spec] * 7,
        out_specs=pl.BlockSpec(memory_space=pltpu.VMEM),
        scratch_shapes=[
            pltpu.SMEM(block_list.shape, jnp.int32),
            pltpu.VMEM(q_taps.shape, f32),
            pltpu.VMEM(k_taps.shape, f32),
            pltpu.VMEM(v_taps.shape, f32),
            pltpu.VMEM((tokens + HALO, qw), bf16),
            pltpu.VMEM((2, tokens + BLOCK + HALO, kvw), bf16),
            pltpu.VMEM((2, tokens + BLOCK, kvw), bf16),
            pltpu.VMEM((nb, groups, rows, HEAD_DIM), bf16),
            pltpu.VMEM((nb, groups, rows, 2 * HEAD_DIM), f32),
            pltpu.VMEM((nb, groups, rows, HEAD_DIM), f32),
            pltpu.VMEM((nb, groups, rows, slots * BLOCK), bf16),
            pltpu.VMEM((max(8, nb), 128), f32),
            pltpu.VMEM((max(8, nb), 128), f32),
            pltpu.VMEM((2, BLOCK, kvw), bf16),
            pltpu.VMEM((2, ni, *piece), bf16),
            pltpu.VMEM((2, *piece), bf16),
            pltpu.VMEM((2, no, *piece), bf16),
            pltpu.VMEM((2, slots, *piece), bf16),
            pltpu.VMEM((2, slots, BLOCK, kvw), bf16),
            dma((7,)),
            dma((5,)),
            dma((5,)),
            dma,
            dma,
            dma((2, ni)),
            dma((2, ni)),
            dma((2, no)),
            dma((2, no)),
            dma((2, ni)),
            dma((2, ni)),
        ],
        compiler_params=pltpu.CompilerParams(
            collective_id=0, has_side_effects=True, vmem_limit_bytes=48 * 1024 * 1024
        ),
        cost_estimate=pl.CostEstimate(
            flops=4 * scores * HEAD_DIM,
            bytes_accessed=4 * tokens * qw + 4 * tokens * kvw,
            transcendentals=scores,
        ),
    )(*arrays)


def solution(mesh):
    rows = P(("groups", "outer", "inner"), None)
    return jax.shard_map(
        body,
        mesh=mesh,
        in_specs=(rows, rows, rows, P(), P(), P(), rows),
        out_specs=rows,
        check_vma=False,
    )
```

```python
import functools
import math

import jax
import jax.numpy as jnp
from jax import lax
from jax.experimental import pallas as pl
from jax.experimental.pallas import tpu as pltpu
from jax.sharding import PartitionSpec as P

HEAD_DIM = 128
BLOCK = 128
LOCAL = 2
STRIDE = 64
HALO = 16
NEG = -1e30
MESH = pl.DeviceIdType.MESH
SCALE = math.log2(math.e) / math.sqrt(HEAD_DIM)
NT = (((1,), (1,)), ((), ()))


def conv(padded, taps):
    wide = padded.astype(jnp.float32)
    total = taps[0:1] * wide[HALO:]
    for j in (1, 2):
        total = total + taps[j : j + 1] * pltpu.roll(wide, j, 0)[HALO:]
    return total.astype(jnp.bfloat16)


def kernel(
    ni, no, list_hbm, q_hbm, k_hbm, v_hbm, qt_hbm, kt_hbm, vt_hbm, outb,
    list_ref, qt_ref, kt_ref, vt_ref, qpad, kvpad, kvc, qs, acc_ref, max_ref, pbuf, wout, win, cand, rbuf, zpiece, zbuf,
    fsum, far, in_sem, tail_s, tail_r, w_s, w_r, sc_s, sc_r, z_s, z_r,
    g_s, g_r,
):
    tokens, qw = q_hbm.shape
    kvw = k_hbm.shape[1]
    groups = kvw // HEAD_DIM
    per_group = qw // kvw
    nb = tokens // BLOCK
    slots = far.shape[1]
    piece_rows, piece_cols = zpiece.shape[1:]
    col_parts = kvw // piece_cols
    before = BLOCK + HALO
    entries = list_ref.shape[1]
    o = lax.axis_index("outer")
    i = lax.axis_index("inner")
    d = o * ni + i
    last = ni * no - 1
    has_next = d < last
    has_prev = d > 0

    def chain(step):
        other = d + step
        return {"outer": other // ni, "inner": lax.rem(other, ni)}

    def inner_peer(r):
        return {"inner": lax.rem(i + r, ni)}

    loads = [
        pltpu.make_async_copy(q_hbm, qpad.at[pl.ds(HALO, tokens)], in_sem.at[0]),
        pltpu.make_async_copy(k_hbm, kvpad.at[0, pl.ds(before, tokens)], in_sem.at[1]),
        pltpu.make_async_copy(v_hbm, kvpad.at[1, pl.ds(before, tokens)], in_sem.at[2]),
        pltpu.make_async_copy(list_hbm, list_ref, in_sem.at[3]),
        pltpu.make_async_copy(qt_hbm, qt_ref, in_sem.at[4]),
        pltpu.make_async_copy(kt_hbm, kt_ref, in_sem.at[5]),
        pltpu.make_async_copy(vt_hbm, vt_ref, in_sem.at[6]),
    ]
    for n in (3, 1, 5, 2, 6, 0, 4):
        loads[n].start()

    barrier = pltpu.get_barrier_semaphore()
    for r in range(1, ni):
        pl.semaphore_signal(barrier, inc=1, device_id=inner_peer(r), device_id_type=MESH)
    for r in range(1, no):
        pl.semaphore_signal(
            barrier, inc=1, device_id={"outer": lax.rem(o + r, no)}, device_id_type=MESH
        )

    @pl.when(has_next)
    def _():
        pl.semaphore_signal(barrier, inc=1, device_id=chain(1), device_id_type=MESH)

    @pl.when(has_prev)
    def _():
        pl.semaphore_signal(barrier, inc=1, device_id=chain(-1), device_id_type=MESH)

    loads[3].wait()
    phase = jnp.int32(-1)
    for b in range(nb):
        for e in range(entries):
            entry = list_ref[b, e]
            distant = (entry >= 0) & (entry <= d * nb + b - LOCAL)
            phase = jnp.maximum(phase, jnp.where(distant, lax.rem(entry, STRIDE), -1))
    for b in range(nb):
        hit = lax.rem((d - 1) * nb + b + STRIDE, STRIDE) == phase
        wout[b : b + 1, :] = jnp.full((1, 128), jnp.where(hit, 1.0, 0.0), jnp.float32)
    if nb < wout.shape[0]:
        wout[nb:, :] = jnp.zeros((wout.shape[0] - nb, 128), jnp.float32)

    @pl.when(d == 0)
    def _():
        qpad[0:HALO, :] = jnp.zeros((HALO, qw), jnp.bfloat16)
        kvpad[:, 0:before, :] = jnp.zeros((2, before, kvw), jnp.bfloat16)

    @pl.when(d == last)
    def _():
        win[...] = jnp.zeros(win.shape, jnp.float32)

    fsum[...] = jnp.zeros(fsum.shape, jnp.bfloat16)

    w_copy = pltpu.make_async_remote_copy(
        wout, win, w_s, w_r, device_id=chain(-1), device_id_type=MESH
    )
    rim = pl.ds(tokens - HALO, HALO)
    body_rows = pl.ds(tokens - before, BLOCK)

    def to_next(src, dst, n):
        return pltpu.make_async_remote_copy(
            src, dst, tail_s.at[n], tail_r.at[n], device_id=chain(1), device_id_type=MESH
        )

    tails = [
        to_next(k_hbm.at[rim], kvpad.at[0, pl.ds(BLOCK, HALO)], 0),
        to_next(v_hbm.at[rim], kvpad.at[1, pl.ds(BLOCK, HALO)], 1),
        to_next(k_hbm.at[body_rows], kvpad.at[0, pl.ds(0, BLOCK)], 2),
        to_next(v_hbm.at[body_rows], kvpad.at[1, pl.ds(0, BLOCK)], 3),
        to_next(q_hbm.at[rim], qpad.at[pl.ds(0, HALO)], 4),
    ]

    def first_sends():
        pl.semaphore_wait(
            barrier,
            ni - 1 + no - 1 + jnp.where(has_next, 1, 0) + jnp.where(has_prev, 1, 0),
        )

        @pl.when(has_prev)
        def _():
            w_copy.start()

        @pl.when(has_next)
        def _():
            for copy in tails:
                copy.start()

    def kv_conv(b):
        rows = slice(b * BLOCK, b * BLOCK + before)
        dst = slice(b * BLOCK, (b + 1) * BLOCK)
        kvc[0, dst, :] = conv(kvpad[0, rows, :], kt_ref[...])
        kvc[1, dst, :] = conv(kvpad[1, rows, :], vt_ref[...])

    for n in (1, 5, 2, 6):
        loads[n].wait()
    for b in range(2, nb + 1):
        kv_conv(b)

    def candidate_step():
        @pl.when(has_prev)
        def _():
            tails[0].wait_recv()
            tails[1].wait_recv()

        kv_conv(1)

        @pl.when(has_next)
        def _():
            w_copy.wait_recv()

        for g in range(groups):
            cols = slice(g * HEAD_DIM, (g + 1) * HEAD_DIM)
            for half in range(2):
                total = jnp.zeros((BLOCK, HEAD_DIM), jnp.float32)
                for b in range(nb):
                    own = jnp.where(lax.rem(d * nb + b, STRIDE) == phase, 1.0, 0.0)
                    weight = jnp.maximum(win[b : b + 1, :], own)
                    rows = slice((b + 1) * BLOCK, (b + 2) * BLOCK)
                    total = total + weight * kvc[half, rows, cols].astype(jnp.float32)
                cand[half, :, cols] = total.astype(jnp.bfloat16)

        for half in range(2):
            for r in range(1, ni):
                scatter(half, r).start()

    def part(index):
        row = pl.multiple_of(index // col_parts * piece_rows, piece_rows)
        col = pl.multiple_of(lax.rem(index, col_parts) * piece_cols, piece_cols)
        return pl.ds(row, piece_rows), pl.ds(col, piece_cols)

    def scatter(half, r):
        return pltpu.make_async_remote_copy(
            cand.at[(half, *part(lax.rem(i + r, ni)))],
            rbuf.at[half, r],
            sc_s.at[half, r],
            sc_r.at[half, r],
            device_id=inner_peer(r),
            device_id_type=MESH,
        )

    def column(half, r):
        return pltpu.make_async_remote_copy(
            zpiece.at[half],
            zbuf.at[half, r],
            z_s.at[half, r],
            z_r.at[half, r],
            device_id={"outer": lax.rem(o + r, no)},
            device_id_type=MESH,
        )

    def gather(half, r):
        return pltpu.make_async_remote_copy(
            fsum.at[half],
            far.at[(half, slice(None), *part(i))],
            g_s.at[half, r],
            g_r.at[half, r],
            device_id=inner_peer(r),
            device_id_type=MESH,
        )

    def column_step(half):
        total = cand[(half, *part(i))].astype(jnp.float32)
        for r in range(1, ni):
            scatter(half, r).wait_recv()
            total = total + rbuf[half, r].astype(jnp.float32)
        zpiece[half] = total.astype(jnp.bfloat16)
        for r in range(1, no):
            pl.when(o + r < no)(column(half, r).start)

    def slot_of(row):
        return lax.rem(row * (ni * nb) // STRIDE, slots)

    def gather_step(half):
        fsum[half, slot_of(o)] = zpiece[half]
        for r in range(1, no):

            @pl.when(o >= r)
            def _():
                column(half, r).wait_recv()
                at = slot_of(o - r)
                fsum[half, at] = (
                    fsum[half, at].astype(jnp.float32) + zbuf[half, r].astype(jnp.float32)
                ).astype(jnp.bfloat16)

        for r in range(1, ni):
            gather(half, r).start()
        far[(half, slice(None), *part(i))] = fsum[half]

    def gather_wait(half):
        for r in range(1, ni):
            gather(half, r).wait_recv()

    loads[0].wait()
    loads[4].wait()

    row_ids = lax.broadcasted_iota(jnp.int32, (BLOCK, BLOCK), 0)
    col_ids = lax.broadcasted_iota(jnp.int32, (BLOCK, BLOCK), 1)
    causal = jnp.concatenate([row_ids >= col_ids] * per_group, 0)
    ones = jnp.ones((LOCAL * BLOCK, HEAD_DIM), jnp.bfloat16)

    def near(step, carry):
        b = jnp.where(step < nb - 2, step + 2, nb - 1 - step)

        @pl.when(b == 0)
        def _():
            @pl.when(has_prev)
            def _():
                tails[2].wait_recv()
                tails[3].wait_recv()
                tails[4].wait_recv()

            kv_conv(0)

        bias = jnp.where((b == 0) & (d == 0), NEG, 0.0)
        base = pl.multiple_of(b * BLOCK, BLOCK)
        for g in range(groups):
            wide = slice(g * per_group * HEAD_DIM, (g + 1) * per_group * HEAD_DIM)
            cols = slice(g * HEAD_DIM, (g + 1) * HEAD_DIM)
            q = conv(qpad[pl.ds(base, BLOCK + HALO), wide], qt_ref[:, wide])
            q = jnp.concatenate(
                [q[:, h * HEAD_DIM : (h + 1) * HEAD_DIM] for h in range(per_group)], 0
            )
            qs[b, g] = q
            k = kvc[0, pl.ds(base, LOCAL * BLOCK), cols]
            v = kvc[1, pl.ds(base, LOCAL * BLOCK), cols]
            s = lax.dot_general(q, k, NT, preferred_element_type=jnp.float32)
            prev = s[:, :BLOCK] + bias
            own = jnp.where(causal, s[:, BLOCK:], NEG)
            peak = jnp.max(jnp.maximum(prev, own), axis=1, keepdims=True)
            p = jnp.concatenate(
                [jnp.exp2((prev - peak) * SCALE), jnp.exp2((own - peak) * SCALE)], 1
            ).astype(jnp.bfloat16)
            acc_ref[b, g] = jnp.dot(
                p, jnp.concatenate([v, ones], 1), preferred_element_type=jnp.float32
            )
            max_ref[b, g] = jnp.broadcast_to(peak, (per_group * BLOCK, HEAD_DIM))

        pl.when(step == 0)(first_sends)
        pl.when(step == 1)(candidate_step)

        @pl.when(step == 2)
        def _():
            column_step(0)
            column_step(1)

        return carry

    lax.fori_loop(0, nb, near, 0)
    gather_step(0)
    gather_step(1)
    gather_wait(0)

    def distant_keys(b, carry):
        biases = []
        for n in range(slots):
            seen = jnp.int32(0)
            for e in range(entries):
                entry = list_ref[b, e]
                hit = (entry >= n * STRIDE) & (entry < (n + 1) * STRIDE)
                hit = hit & (entry <= d * nb + b - LOCAL)
                seen = jnp.where(hit, 1, seen)
            biases.append(jnp.where(seen > 0, 0.0, NEG))
        for g in range(groups):
            cols = slice(g * HEAD_DIM, (g + 1) * HEAD_DIM)
            q = qs[b, g]
            near_peak = max_ref[b, g]
            scores = []
            top = None
            for n in range(slots):
                s = lax.dot_general(q, far[0, n, :, cols], NT, preferred_element_type=jnp.float32)
                s = s + biases[n]
                scores.append(s)
                top = s if top is None else jnp.maximum(top, s)
            peak = jnp.maximum(near_peak, jnp.max(top, axis=1, keepdims=True))
            max_ref[b, g] = jnp.exp2((near_peak - peak) * SCALE)
            for n in range(slots):
                p = jnp.exp2((scores[n] - peak) * SCALE)
                pbuf[b, g, :, n * BLOCK : (n + 1) * BLOCK] = p.astype(jnp.bfloat16)
        return carry

    def distant_values(b, carry):
        base = pl.multiple_of(b * BLOCK, BLOCK)
        for g in range(groups):
            cols = slice(g * HEAD_DIM, (g + 1) * HEAD_DIM)
            both = acc_ref[b, g]
            shrink = max_ref[b, g]
            total = both[:, :HEAD_DIM] * shrink
            count = both[:, HEAD_DIM:] * shrink
            for n in range(slots):
                more = jnp.dot(
                    pbuf[b, g, :, n * BLOCK : (n + 1) * BLOCK],
                    jnp.concatenate([far[1, n, :, cols], ones[:BLOCK]], 1),
                    preferred_element_type=jnp.float32,
                )
                total = total + more[:, :HEAD_DIM]
                count = count + more[:, HEAD_DIM:]
            mixed = (total / count).astype(jnp.bfloat16)
            for h in range(per_group):
                head = g * per_group + h
                outb[pl.ds(base, BLOCK), head * HEAD_DIM : (head + 1) * HEAD_DIM] = mixed[
                    h * BLOCK : (h + 1) * BLOCK
                ]
        return carry

    lax.fori_loop(0, nb, distant_keys, 0)
    gather_wait(1)
    lax.fori_loop(0, nb, distant_values, 0)

    @pl.when(has_prev)
    def _():
        w_copy.wait_send()

    @pl.when(has_next)
    def _():
        for copy in tails:
            copy.wait_send()

    for half in range(2):
        for r in range(1, ni):
            scatter(half, r).wait_send()
            gather(half, r).wait_send()
        for r in range(1, no):
            pl.when(o + r < no)(column(half, r).wait_send)


ROWS = 4
SUMS = ({0: (1,), 2: (3,)}, {0: (2, 1), 1: (2,)})
SPREADS = ({1: (3, 2)}, {2: (3,)})
FIRST_ROW_STEP = 1
UNROLL = 4
LATE = ((2, 3), (1, 3), (0, 2))


def dests(row, late):
    rows = {r for table in (*SUMS, *SPREADS) for r in table.get(row, ())}
    return sorted(r for r in rows if ((row, r) in LATE) == late)


def origins(row, late):
    return [r for r in range(ROWS) if row in dests(r, late)]


def paired_kernel(
    list_hbm, q_hbm, k_hbm, v_hbm, qt_hbm, kt_hbm, vt_hbm, outb,
    list_ref, qt_ref, kt_ref, vt_ref, qpad, kvpad, kvc, qs, acc_ref, max_ref, pbuf,
    flag_out, flag_in, chip, cand, rrow, rother, site, zfar, far_k, far_v,
    in_sem, own_sem, fl_s, fl_r, raw_s, raw_r, rim_s, rim_r, tail_s, tail_r,
    a_s, a_r, b_s, b_r, c_s, c_r, d_s, d_r, e_s, e_r, ready,
):
    tokens, qw = q_hbm.shape
    kvw = k_hbm.shape[1]
    groups = kvw // HEAD_DIM
    hw = kvw // 2
    quarter = hw // 2
    per_group = qw // kvw
    nb = tokens // BLOCK
    before = BLOCK + HALO
    entries = list_ref.shape[1]
    o = lax.axis_index("outer")
    i = lax.axis_index("inner")
    y = i // 2
    c = lax.rem(i, 2)
    m = o * 2 + y
    no = ROWS
    last_chip = no * 2 - 1
    d = o * 4 + i
    has_next = d < 4 * no - 1
    has_prev = d > 0
    chip_next = m < last_chip
    chip_prev = m > 0
    first_core = c == 0
    second_core = c == 1

    def chip_core(step, core):
        other = m + step
        return {"outer": other // 2, "inner": lax.rem(other, 2) * 2 + core}

    def at(row, col):
        return {"outer": row, "inner": col * 2 + c}

    peer_core = {"inner": i + 1 - 2 * c}
    peer_y = {"inner": lax.rem(i + 2, 4)}
    next_device = {"outer": (d + 1) // 4, "inner": lax.rem(d + 1, 4)}

    barrier = pltpu.get_barrier_semaphore()

    def greet(device):
        pl.semaphore_signal(barrier, inc=1, device_id=device, device_id_type=MESH)

    def call(device):
        pl.semaphore_signal(ready, inc=1, device_id=device, device_id_type=MESH)

    loads = [
        pltpu.make_async_copy(q_hbm, qpad.at[pl.ds(HALO, tokens)], in_sem.at[0]),
        pltpu.make_async_copy(k_hbm, kvpad.at[0, pl.ds(before, tokens)], in_sem.at[1]),
        pltpu.make_async_copy(v_hbm, kvpad.at[1, pl.ds(before, tokens)], in_sem.at[2]),
        pltpu.make_async_copy(list_hbm, list_ref, in_sem.at[3]),
        pltpu.make_async_copy(qt_hbm, qt_ref, in_sem.at[4]),
        pltpu.make_async_copy(kt_hbm, kt_ref, in_sem.at[5]),
        pltpu.make_async_copy(vt_hbm, vt_ref, in_sem.at[6]),
    ]
    half_cols = pl.ds(pl.multiple_of(c * hw, hw), hw)
    peer_cols = pl.ds(pl.multiple_of((1 - c) * hw, hw), hw)
    chip_rows = pl.ds(pl.multiple_of(HALO + c * tokens, HALO), tokens)
    own = [
        pltpu.make_async_copy(x.at[:, half_cols], chip.at[h, chip_rows], own_sem.at[h])
        for h, x in enumerate((k_hbm, v_hbm))
    ]
    loads[3].start()
    greet(peer_core)
    greet(peer_y)

    late_next = (y == 1) & functools.reduce(
        jnp.logical_or, [o == row for row in range(no - 1) if (row, row + 1) in LATE]
    )
    late_prev = (y == 0) & functools.reduce(
        jnp.logical_or, [o == row + 1 for row in range(no - 1) if (row, row + 1) in LATE]
    )

    @pl.when(chip_next)
    def _():
        greet(chip_core(1, 0))
        pl.when(second_core & late_next)(lambda: greet(chip_core(1, 1)))

    pl.when(chip_prev & jnp.logical_not(late_prev))(lambda: greet(chip_core(-1, 1)))
    for row in range(no):

        @pl.when(o == row)
        def _():
            for other in origins(row, False) + dests(row, True):
                greet(at(other, 0))
                greet(at(other, 1))

    for n in (1, 5, 2, 6):
        loads[n].start()
    for copy in own:
        copy.start()
    for n in (0, 4):
        loads[n].start()

    def remote(src, dst, send, recv, device):
        return pltpu.make_async_remote_copy(
            src, dst, send, recv, device_id=device, device_id_type=MESH
        )

    flag_back = [
        remote(flag_out, flag_in.at[0], fl_s.at[k], fl_r.at[0], chip_core(-1, k)) for k in range(2)
    ]
    flag_peer = remote(flag_out, flag_in.at[1], fl_s.at[2], fl_r.at[1], peer_core)
    raws = [
        remote(x.at[:, peer_cols], chip.at[h, chip_rows], raw_s.at[h], raw_r.at[h], peer_core)
        for h, x in enumerate((k_hbm, v_hbm))
    ]
    rim = pl.ds(tokens - HALO, HALO)
    rims = [
        [
            remote(
                x.at[rim, k * hw : (k + 1) * hw],
                chip.at[h, pl.ds(0, HALO)],
                rim_s.at[k, h],
                rim_r.at[h],
                chip_core(1, k),
            )
            for h, x in enumerate((k_hbm, v_hbm))
        ]
        for k in range(2)
    ]
    tail_rows = pl.ds(tokens - before, before)
    tails = [
        remote(k_hbm.at[tail_rows], kvpad.at[0, pl.ds(0, before)], tail_s.at[0], tail_r.at[0], next_device),
        remote(v_hbm.at[tail_rows], kvpad.at[1, pl.ds(0, before)], tail_s.at[1], tail_r.at[1], next_device),
        remote(q_hbm.at[rim], qpad.at[pl.ds(0, HALO)], tail_s.at[2], tail_r.at[2], next_device),
    ]

    @pl.when(jnp.logical_not(has_prev))
    def _():
        qpad[0:HALO, :] = jnp.zeros((HALO, qw), jnp.bfloat16)
        kvpad[:, 0:before, :] = jnp.zeros((2, before, kvw), jnp.bfloat16)

    @pl.when(jnp.logical_not(chip_prev))
    def _():
        chip[:, 0:HALO, :] = jnp.zeros((2, HALO, hw), jnp.bfloat16)

    far_k[...] = jnp.zeros(far_k.shape, jnp.bfloat16)

    @pl.when(jnp.logical_not(chip_next))
    def _():
        flag_in[0] = jnp.full(flag_in.shape[1:], -1, jnp.int32)

    @pl.when(second_core)
    def _():
        flag_in[1] = jnp.full(flag_in.shape[1:], -1, jnp.int32)

    expected = 2 + jnp.where(chip_prev & first_core, 2, 0)
    expected = expected + jnp.where(chip_prev & late_prev & second_core, 1, 0)
    sends_on = second_core & chip_next
    expected = expected + jnp.where(sends_on & jnp.logical_not(late_next), 2, 0)
    awaited = jnp.where(sends_on & late_next, 2, 0)
    for row in range(no):
        met = 2 * len(dests(row, False) + origins(row, True))
        expected = expected + jnp.where(o == row, met, 0)
        awaited = awaited + jnp.where(o == row, 2 * len(dests(row, True)), 0)
    pl.semaphore_wait(barrier, expected)
    pl.when(chip_prev & late_prev)(lambda: call(chip_core(-1, 1)))
    for row in range(no):
        if origins(row, True):

            @pl.when(o == row)
            def _():
                for src in origins(row, True):
                    call(at(src, 0))
                    call(at(src, 1))

    for copy in raws:
        copy.start()

    loads[3].wait()
    phase = jnp.int32(-1)
    for b in range(nb):
        for e in range(entries):
            entry = list_ref[b, e]
            distant = (entry >= 0) & (entry <= d * nb + b - LOCAL)
            phase = jnp.maximum(phase, jnp.where(distant, lax.rem(entry, STRIDE), -1))
    flag_out[...] = jnp.full(flag_out.shape, phase, jnp.int32)

    @pl.when(first_core & chip_prev)
    def _():
        for copy in flag_back:
            copy.start()

    pl.when(second_core)(flag_peer.start)
    def next_sends():
        @pl.when(sends_on)
        def _():
            for h in range(2):
                for k in range(2):
                    rims[k][h].start()

        @pl.when(has_next)
        def _():
            for copy in tails:
                copy.start()

    held_back = sends_on & late_next
    pl.when(jnp.logical_not(held_back))(next_sends)

    def kv_conv(b):
        rows = slice(b * BLOCK, b * BLOCK + before)
        dst = slice(b * BLOCK, (b + 1) * BLOCK)
        kvc[0, dst, :] = conv(kvpad[0, rows, :], kt_ref[...])
        kvc[1, dst, :] = conv(kvpad[1, rows, :], vt_ref[...])

    def cols_of(col):
        return slice(col * quarter, (col + 1) * quarter)

    def to_peer_site(h):
        return remote(cand.at[h, 1 - y], rrow.at[h], a_s.at[h], a_r.at[h], peer_y)

    def to_site(h, row, col):
        return remote(
            cand.at[h, col], rother.at[h, o, y], b_s.at[h, row, col], b_r.at[h, o, y], at(row, col)
        )

    def at_site(h, src, col):
        return remote(
            cand.at[h, col], rother.at[h, src, col], b_s.at[h, 0, col], b_r.at[h, src, col], peer_y
        )

    def to_peer_col(h):
        return remote(site.at[h, y], site.at[h, y], c_s.at[h], c_r.at[h], peer_y)

    def from_peer_col(h):
        return remote(site.at[h, 1 - y], site.at[h, 1 - y], c_s.at[h], c_r.at[h], peer_y)

    def to_later(h, row, col):
        return remote(
            site.at[h, y], zfar.at[h, o, y], d_s.at[h, row, col], d_r.at[h, o, y], at(row, col)
        )

    def from_earlier(h, src, col):
        return remote(
            site.at[h, y], zfar.at[h, src, col], d_s.at[h, 0, 0], d_r.at[h, src, col], peer_y
        )

    def core_swap(h, core):
        if h == 0:
            part = far_k.at[core]
        else:
            part = far_v.at[pl.ds(2 * core, 2)]
        return remote(part, part, e_s.at[h], e_r.at[h], peer_core)

    def to_peer_core(h):
        return core_swap(h, c)

    def from_peer_core(h):
        return core_swap(h, 1 - c)

    def candidate_step():
        pl.when(awaited > 0)(lambda: pl.semaphore_wait(ready, awaited))
        pl.when(held_back)(next_sends)

        @pl.when(chip_next)
        def _():
            remote(flag_out, flag_in.at[0], fl_s.at[0], fl_r.at[0], peer_core).wait_recv()

        @pl.when(first_core)
        def _():
            flag_peer.wait_recv()

        known = jnp.maximum(jnp.maximum(flag_in[0, 0:1, :], flag_in[1, 0:1, :]), phase)
        first = m * 2 * nb
        weights = [
            jnp.where(known == first + b, 1.0, 0.0).astype(jnp.bfloat16) for b in range(2 * nb)
        ]
        for h, taps in enumerate((kt_ref, vt_ref)):
            own[h].wait()
            raws[h].wait_recv()

            @pl.when(chip_prev)
            def _():
                rims[0][h].wait_recv()

            raw = weights[0] * chip[h, 0:before, :]
            for b in range(1, 2 * nb):
                raw = raw + weights[b] * chip[h, b * BLOCK : b * BLOCK + before, :]
            total = conv(raw, taps[:, half_cols])
            for col in range(2):
                cand[h, col] = total[:, cols_of(col)]

            for src, rows in SUMS[h].items():

                @pl.when(o == src)
                def _():
                    for row in rows:
                        for col in range(2):
                            to_site(h, row, col).start()

            to_peer_site(h).start()

    def site_step(h):
        to_peer_site(h).wait_recv()
        site[h, y] = cand[h, y] + rrow[h]
        for row in range(no):
            sources = [src for src, rows in SUMS[h].items() if row in rows]
            if sources:

                @pl.when(o == row)
                def _():
                    for src in sources:
                        for col in range(2):
                            at_site(h, src, col).wait_recv()
                            site[h, y] = site[h, y] + rother[h, src, col]

        for src, rows in SPREADS[h].items():

            @pl.when(o == src)
            def _():
                for row in rows:
                    for col in range(2):
                        to_later(h, row, col).start()

        to_peer_col(h).start()

    def final_step(h):
        from_peer_col(h).wait_recv()
        for src, rows in SPREADS[h].items():
            for row in rows:

                @pl.when(o == row)
                def _():
                    for col in range(2):
                        from_earlier(h, src, col).wait_recv()
                        zfar[h, o, col] = zfar[h, src, col] + site[h, col]

        gets = functools.reduce(
            jnp.logical_or, [o == row for rows in SPREADS[h].values() for row in rows]
        )

        def place(source):
            for col in range(2):
                if h == 0:
                    far_k[c, cols_of(col), cols_of(col)] = source(col)
                else:
                    far_v[2 * c + col] = source(col)

        pl.when(gets)(lambda: place(lambda col: zfar[h, o, col]))
        pl.when(jnp.logical_not(gets))(lambda: place(lambda col: site[h, col]))
        to_peer_core(h).start()

    for n in (1, 5, 2, 6):
        loads[n].wait()
    for b in range(2, nb + 1):
        kv_conv(b)
    loads[0].wait()
    loads[4].wait()

    row_ids = lax.broadcasted_iota(jnp.int32, (BLOCK, BLOCK), 0)
    col_ids = lax.broadcasted_iota(jnp.int32, (BLOCK, BLOCK), 1)
    causal = jnp.concatenate([row_ids >= col_ids] * per_group, 0)
    ones = jnp.ones((LOCAL * BLOCK, HEAD_DIM), jnp.bfloat16)

    def near(step, carry):
        b = jnp.where(step < nb - 2, step + 2, nb - 1 - step)

        @pl.when(b == 1)
        def _():
            @pl.when(has_prev)
            def _():
                tails[0].wait_recv()
                tails[1].wait_recv()

            kv_conv(1)

        @pl.when(b == 0)
        def _():
            @pl.when(has_prev)
            def _():
                tails[2].wait_recv()

            kv_conv(0)

        bias = jnp.where((b == 0) & (d == 0), NEG, 0.0)
        base = pl.multiple_of(b * BLOCK, BLOCK)
        for g in range(groups):
            wide = slice(g * per_group * HEAD_DIM, (g + 1) * per_group * HEAD_DIM)
            cols = slice(g * HEAD_DIM, (g + 1) * HEAD_DIM)
            q = conv(qpad[pl.ds(base, BLOCK + HALO), wide], qt_ref[:, wide])
            q = jnp.concatenate(
                [q[:, h * HEAD_DIM : (h + 1) * HEAD_DIM] for h in range(per_group)], 0
            )
            qs[b, g // 2, :, cols_of(g % 2)] = q
            k = kvc[0, pl.ds(base, LOCAL * BLOCK), cols]
            v = kvc[1, pl.ds(base, LOCAL * BLOCK), cols]
            s = lax.dot_general(q, k, NT, preferred_element_type=jnp.float32)
            prev = s[:, :BLOCK] + bias
            mine = jnp.where(causal, s[:, BLOCK:], NEG)
            peak = jnp.max(jnp.maximum(prev, mine), axis=1, keepdims=True)
            p = jnp.concatenate(
                [jnp.exp2((prev - peak) * SCALE), jnp.exp2((mine - peak) * SCALE)], 1
            ).astype(jnp.bfloat16)
            acc_ref[b, g] = jnp.dot(
                p, jnp.concatenate([v, ones], 1), preferred_element_type=jnp.float32
            )
            max_ref[b, g] = jnp.broadcast_to(peak, (per_group * BLOCK, HEAD_DIM))

        pl.when(step == jnp.where(o == 0, FIRST_ROW_STEP, 0))(candidate_step)
        return carry

    lax.fori_loop(0, nb, near, 0)
    site_step(0)
    site_step(1)
    final_step(0)

    def distant_keys(pair, b):
        seen = jnp.int32(0)
        for e in range(entries):
            entry = list_ref[b, e]
            seen = jnp.where((entry >= 0) & (entry <= d * nb + b - LOCAL), 1, seen)
        bias = jnp.where(seen > 0, 0.0, NEG)
        both = lax.dot_general(qs[b, pair], far_k[pair], NT, preferred_element_type=jnp.float32)
        for n in range(2):
            g = 2 * pair + n
            s = both[:, cols_of(n)] + bias
            near_peak = max_ref[b, g]
            peak = jnp.maximum(near_peak, jnp.max(s, axis=1, keepdims=True))
            max_ref[b, g] = jnp.exp2((near_peak - peak) * SCALE)
            pbuf[b, g] = jnp.exp2((s - peak) * SCALE).astype(jnp.bfloat16)

    def distant_values(pair, b):
        base = pl.multiple_of(b * BLOCK, BLOCK)
        for n in range(2):
            g = 2 * pair + n
            shrink = max_ref[b, g]
            more = jnp.dot(
                pbuf[b, g],
                jnp.concatenate([far_v[g], ones[:BLOCK]], 1),
                preferred_element_type=jnp.float32,
            )
            total = acc_ref[b, g, :, :HEAD_DIM] * shrink + more[:, :HEAD_DIM]
            count = acc_ref[b, g, :, HEAD_DIM:] * shrink + more[:, HEAD_DIM:]
            inverse = pl.reciprocal(count, approx=True)
            inverse = inverse * (2.0 - count * inverse)
            mixed = (total * inverse).astype(jnp.bfloat16)
            for h in range(per_group):
                head = g * per_group + h
                outb[pl.ds(base, BLOCK), head * HEAD_DIM : (head + 1) * HEAD_DIM] = mixed[
                    h * BLOCK : (h + 1) * BLOCK
                ]

    def loop(run, pair):
        def step(b, carry):
            run(pair, b)
            return carry

        lax.fori_loop(0, nb, step, 0, unroll=UNROLL)

    def far_stage(pair):
        loop(distant_keys, pair)
        loop(distant_values, pair)
        core_swap(0, 1 - pair).wait_recv()
        loop(distant_keys, 1 - pair)
        core_swap(1, 1 - pair).wait_recv()
        loop(distant_values, 1 - pair)

    final_step(1)
    pl.when(first_core)(functools.partial(far_stage, 0))
    pl.when(second_core)(functools.partial(far_stage, 1))

    @pl.when(first_core & chip_prev)
    def _():
        for copy in flag_back:
            copy.wait_send()

    @pl.when(second_core)
    def _():
        flag_peer.wait_send()

        @pl.when(chip_next)
        def _():
            for k in range(2):
                for copy in rims[k]:
                    copy.wait_send()

    @pl.when(has_next)
    def _():
        for copy in tails:
            copy.wait_send()

    for h in range(2):
        raws[h].wait_send()
        to_peer_site(h).wait_send()
        to_peer_col(h).wait_send()
        to_peer_core(h).wait_send()

        for table, copy in ((SUMS, to_site), (SPREADS, to_later)):
            for src, rows in table[h].items():

                @pl.when(o == src)
                def _():
                    for row in rows:
                        for col in range(2):
                            copy(h, row, col).wait_send()


def paired_call(arrays):
    block_list, q_proj, k_proj = arrays[:3]
    q_taps, k_taps, v_taps = arrays[4:]
    tokens, qw = q_proj.shape
    kvw = k_proj.shape[1]
    nb = tokens // BLOCK
    groups = kvw // HEAD_DIM
    rows = qw // kvw * BLOCK
    hw = kvw // 2
    piece = (BLOCK, hw // 2)
    dma = pltpu.SemaphoreType.DMA
    bf16, f32 = jnp.bfloat16, jnp.float32
    hbm_spec = pl.BlockSpec(memory_space=pltpu.HBM)
    scores = nb * groups * rows * (LOCAL + 1) * BLOCK
    return pl.pallas_call(
        paired_kernel,
        out_shape=jax.ShapeDtypeStruct((tokens, qw), bf16),
        in_specs=[hbm_spec] * 7,
        out_specs=pl.BlockSpec(memory_space=pltpu.VMEM),
        scratch_shapes=[
            pltpu.SMEM(block_list.shape, jnp.int32),
            pltpu.VMEM(q_taps.shape, f32),
            pltpu.VMEM(k_taps.shape, f32),
            pltpu.VMEM(v_taps.shape, f32),
            pltpu.VMEM((tokens + HALO, qw), bf16),
            pltpu.VMEM((2, tokens + BLOCK + HALO, kvw), bf16),
            pltpu.VMEM((2, tokens + BLOCK, kvw), bf16),
            pltpu.VMEM((nb, groups // 2, rows, 2 * HEAD_DIM), bf16),
            pltpu.VMEM((nb, groups, rows, 2 * HEAD_DIM), f32),
            pltpu.VMEM((nb, groups, rows, HEAD_DIM), f32),
            pltpu.VMEM((nb, groups, rows, BLOCK), bf16),
            pltpu.VMEM((8, hw), jnp.int32),
            pltpu.VMEM((2, 8, hw), jnp.int32),
            pltpu.VMEM((2, 2 * tokens + HALO, hw), bf16),
            pltpu.VMEM((2, 2, *piece), bf16),
            pltpu.VMEM((2, *piece), bf16),
            pltpu.VMEM((2, ROWS, 2, *piece), bf16),
            pltpu.VMEM((2, 2, *piece), bf16),
            pltpu.VMEM((2, ROWS, 2, *piece), bf16),
            pltpu.VMEM((groups // 2, 2 * BLOCK, hw), bf16),
            pltpu.VMEM((groups, BLOCK, HEAD_DIM), bf16),
            dma((7,)),
            dma((2,)),
            dma((3,)),
            dma((2,)),
            dma((2,)),
            dma((2,)),
            dma((2, 2)),
            dma((2,)),
            dma((3,)),
            dma((3,)),
            dma((2,)),
            dma((2,)),
            dma((2, ROWS, 2)),
            dma((2, ROWS, 2)),
            dma((2,)),
            dma((2,)),
            dma((2, ROWS, 2)),
            dma((2, ROWS, 2)),
            dma((2,)),
            dma((2,)),
            pltpu.SemaphoreType.REGULAR,
        ],
        compiler_params=pltpu.CompilerParams(
            collective_id=0, has_side_effects=True, vmem_limit_bytes=48 * 1024 * 1024
        ),
        cost_estimate=pl.CostEstimate(
            flops=4 * scores * HEAD_DIM,
            bytes_accessed=4 * tokens * qw + 4 * tokens * kvw,
            transcendentals=scores,
        ),
    )(*arrays)


def body(q_proj, k_proj, v_proj, q_taps, k_taps, v_taps, block_list):
    tokens, qw = q_proj.shape
    kvw = k_proj.shape[1]
    ni = lax.axis_size("inner")
    no = lax.axis_size("outer")
    nb = tokens // BLOCK
    groups = kvw // HEAD_DIM
    rows = qw // kvw * BLOCK
    slots = max(1, nb * ni * no // STRIDE)
    piece_rows = max(HALO, BLOCK // ni)
    piece_cols = BLOCK * kvw // (ni * piece_rows)
    piece = (piece_rows, piece_cols)
    dma = pltpu.SemaphoreType.DMA
    bf16, f32 = jnp.bfloat16, jnp.float32
    hbm_spec = pl.BlockSpec(memory_space=pltpu.HBM)
    scores = nb * groups * rows * (LOCAL + slots) * BLOCK
    arrays = [
        pltpu.with_memory_space_constraint(x, pltpu.HBM)
        for x in (block_list, q_proj, k_proj, v_proj, q_taps, k_taps, v_taps)
    ]
    paired = ni == 4 and no == ROWS and nb * ni * no == STRIDE and groups == 4 and nb >= 2
    if paired:
        return paired_call(arrays)
    return pl.pallas_call(
        functools.partial(kernel, ni, no),
        out_shape=jax.ShapeDtypeStruct((tokens, qw), bf16),
        in_specs=[hbm_spec] * 7,
        out_specs=pl.BlockSpec(memory_space=pltpu.VMEM),
        scratch_shapes=[
            pltpu.SMEM(block_list.shape, jnp.int32),
            pltpu.VMEM(q_taps.shape, f32),
            pltpu.VMEM(k_taps.shape, f32),
            pltpu.VMEM(v_taps.shape, f32),
            pltpu.VMEM((tokens + HALO, qw), bf16),
            pltpu.VMEM((2, tokens + BLOCK + HALO, kvw), bf16),
            pltpu.VMEM((2, tokens + BLOCK, kvw), bf16),
            pltpu.VMEM((nb, groups, rows, HEAD_DIM), bf16),
            pltpu.VMEM((nb, groups, rows, 2 * HEAD_DIM), f32),
            pltpu.VMEM((nb, groups, rows, HEAD_DIM), f32),
            pltpu.VMEM((nb, groups, rows, slots * BLOCK), bf16),
            pltpu.VMEM((max(8, nb), 128), f32),
            pltpu.VMEM((max(8, nb), 128), f32),
            pltpu.VMEM((2, BLOCK, kvw), bf16),
            pltpu.VMEM((2, ni, *piece), bf16),
            pltpu.VMEM((2, *piece), bf16),
            pltpu.VMEM((2, no, *piece), bf16),
            pltpu.VMEM((2, slots, *piece), bf16),
            pltpu.VMEM((2, slots, BLOCK, kvw), bf16),
            dma((7,)),
            dma((5,)),
            dma((5,)),
            dma,
            dma,
            dma((2, ni)),
            dma((2, ni)),
            dma((2, no)),
            dma((2, no)),
            dma((2, ni)),
            dma((2, ni)),
        ],
        compiler_params=pltpu.CompilerParams(
            collective_id=0, has_side_effects=True, vmem_limit_bytes=48 * 1024 * 1024
        ),
        cost_estimate=pl.CostEstimate(
            flops=4 * scores * HEAD_DIM,
            bytes_accessed=4 * tokens * qw + 4 * tokens * kvw,
            transcendentals=scores,
        ),
    )(*arrays)


def solution(mesh):
    rows = P(("groups", "outer", "inner"), None)
    return jax.shard_map(
        body,
        mesh=mesh,
        in_specs=(rows, rows, rows, P(), P(), P(), rows),
        out_specs=rows,
        check_vma=False,
    )
```

```python
import functools
import math

import jax
import jax.numpy as jnp
from jax import lax
from jax.experimental import pallas as pl
from jax.experimental.pallas import tpu as pltpu
from jax.sharding import PartitionSpec as P

HEAD_DIM = 128
BLOCK = 128
LOCAL = 2
STRIDE = 64
HALO = 16
NEG = -1e30
MESH = pl.DeviceIdType.MESH
SCALE = math.log2(math.e) / math.sqrt(HEAD_DIM)
NT = (((1,), (1,)), ((), ()))


def conv(padded, taps):
    wide = padded.astype(jnp.float32)
    total = taps[0:1] * wide[HALO:]
    for j in (1, 2):
        total = total + taps[j : j + 1] * pltpu.roll(wide, j, 0)[HALO:]
    return total.astype(jnp.bfloat16)


def kernel(
    ni, no, list_hbm, q_hbm, k_hbm, v_hbm, qt_hbm, kt_hbm, vt_hbm, outb,
    list_ref, qt_ref, kt_ref, vt_ref, qpad, kvpad, kvc, qs, acc_ref, max_ref, pbuf, wout, win, cand, rbuf, zpiece, zbuf,
    fsum, far, in_sem, tail_s, tail_r, w_s, w_r, sc_s, sc_r, z_s, z_r,
    g_s, g_r,
):
    tokens, qw = q_hbm.shape
    kvw = k_hbm.shape[1]
    groups = kvw // HEAD_DIM
    per_group = qw // kvw
    nb = tokens // BLOCK
    slots = far.shape[1]
    piece_rows, piece_cols = zpiece.shape[1:]
    col_parts = kvw // piece_cols
    before = BLOCK + HALO
    entries = list_ref.shape[1]
    o = lax.axis_index("outer")
    i = lax.axis_index("inner")
    d = o * ni + i
    last = ni * no - 1
    has_next = d < last
    has_prev = d > 0

    def chain(step):
        other = d + step
        return {"outer": other // ni, "inner": lax.rem(other, ni)}

    def inner_peer(r):
        return {"inner": lax.rem(i + r, ni)}

    loads = [
        pltpu.make_async_copy(q_hbm, qpad.at[pl.ds(HALO, tokens)], in_sem.at[0]),
        pltpu.make_async_copy(k_hbm, kvpad.at[0, pl.ds(before, tokens)], in_sem.at[1]),
        pltpu.make_async_copy(v_hbm, kvpad.at[1, pl.ds(before, tokens)], in_sem.at[2]),
        pltpu.make_async_copy(list_hbm, list_ref, in_sem.at[3]),
        pltpu.make_async_copy(qt_hbm, qt_ref, in_sem.at[4]),
        pltpu.make_async_copy(kt_hbm, kt_ref, in_sem.at[5]),
        pltpu.make_async_copy(vt_hbm, vt_ref, in_sem.at[6]),
    ]
    for n in (3, 1, 5, 2, 6, 0, 4):
        loads[n].start()

    barrier = pltpu.get_barrier_semaphore()
    for r in range(1, ni):
        pl.semaphore_signal(barrier, inc=1, device_id=inner_peer(r), device_id_type=MESH)
    for r in range(1, no):
        pl.semaphore_signal(
            barrier, inc=1, device_id={"outer": lax.rem(o + r, no)}, device_id_type=MESH
        )

    @pl.when(has_next)
    def _():
        pl.semaphore_signal(barrier, inc=1, device_id=chain(1), device_id_type=MESH)

    @pl.when(has_prev)
    def _():
        pl.semaphore_signal(barrier, inc=1, device_id=chain(-1), device_id_type=MESH)

    loads[3].wait()
    phase = jnp.int32(-1)
    for b in range(nb):
        for e in range(entries):
            entry = list_ref[b, e]
            distant = (entry >= 0) & (entry <= d * nb + b - LOCAL)
            phase = jnp.maximum(phase, jnp.where(distant, lax.rem(entry, STRIDE), -1))
    for b in range(nb):
        hit = lax.rem((d - 1) * nb + b + STRIDE, STRIDE) == phase
        wout[b : b + 1, :] = jnp.full((1, 128), jnp.where(hit, 1.0, 0.0), jnp.float32)
    if nb < wout.shape[0]:
        wout[nb:, :] = jnp.zeros((wout.shape[0] - nb, 128), jnp.float32)

    @pl.when(d == 0)
    def _():
        qpad[0:HALO, :] = jnp.zeros((HALO, qw), jnp.bfloat16)
        kvpad[:, 0:before, :] = jnp.zeros((2, before, kvw), jnp.bfloat16)

    @pl.when(d == last)
    def _():
        win[...] = jnp.zeros(win.shape, jnp.float32)

    fsum[...] = jnp.zeros(fsum.shape, jnp.bfloat16)

    w_copy = pltpu.make_async_remote_copy(
        wout, win, w_s, w_r, device_id=chain(-1), device_id_type=MESH
    )
    rim = pl.ds(tokens - HALO, HALO)
    body_rows = pl.ds(tokens - before, BLOCK)

    def to_next(src, dst, n):
        return pltpu.make_async_remote_copy(
            src, dst, tail_s.at[n], tail_r.at[n], device_id=chain(1), device_id_type=MESH
        )

    tails = [
        to_next(k_hbm.at[rim], kvpad.at[0, pl.ds(BLOCK, HALO)], 0),
        to_next(v_hbm.at[rim], kvpad.at[1, pl.ds(BLOCK, HALO)], 1),
        to_next(k_hbm.at[body_rows], kvpad.at[0, pl.ds(0, BLOCK)], 2),
        to_next(v_hbm.at[body_rows], kvpad.at[1, pl.ds(0, BLOCK)], 3),
        to_next(q_hbm.at[rim], qpad.at[pl.ds(0, HALO)], 4),
    ]

    def first_sends():
        pl.semaphore_wait(
            barrier,
            ni - 1 + no - 1 + jnp.where(has_next, 1, 0) + jnp.where(has_prev, 1, 0),
        )

        @pl.when(has_prev)
        def _():
            w_copy.start()

        @pl.when(has_next)
        def _():
            for copy in tails:
                copy.start()

    def kv_conv(b):
        rows = slice(b * BLOCK, b * BLOCK + before)
        dst = slice(b * BLOCK, (b + 1) * BLOCK)
        kvc[0, dst, :] = conv(kvpad[0, rows, :], kt_ref[...])
        kvc[1, dst, :] = conv(kvpad[1, rows, :], vt_ref[...])

    for n in (1, 5, 2, 6):
        loads[n].wait()
    for b in range(2, nb + 1):
        kv_conv(b)

    def candidate_step():
        @pl.when(has_prev)
        def _():
            tails[0].wait_recv()
            tails[1].wait_recv()

        kv_conv(1)

        @pl.when(has_next)
        def _():
            w_copy.wait_recv()

        for g in range(groups):
            cols = slice(g * HEAD_DIM, (g + 1) * HEAD_DIM)
            for half in range(2):
                total = jnp.zeros((BLOCK, HEAD_DIM), jnp.float32)
                for b in range(nb):
                    own = jnp.where(lax.rem(d * nb + b, STRIDE) == phase, 1.0, 0.0)
                    weight = jnp.maximum(win[b : b + 1, :], own)
                    rows = slice((b + 1) * BLOCK, (b + 2) * BLOCK)
                    total = total + weight * kvc[half, rows, cols].astype(jnp.float32)
                cand[half, :, cols] = total.astype(jnp.bfloat16)

        for half in range(2):
            for r in range(1, ni):
                scatter(half, r).start()

    def part(index):
        row = pl.multiple_of(index // col_parts * piece_rows, piece_rows)
        col = pl.multiple_of(lax.rem(index, col_parts) * piece_cols, piece_cols)
        return pl.ds(row, piece_rows), pl.ds(col, piece_cols)

    def scatter(half, r):
        return pltpu.make_async_remote_copy(
            cand.at[(half, *part(lax.rem(i + r, ni)))],
            rbuf.at[half, r],
            sc_s.at[half, r],
            sc_r.at[half, r],
            device_id=inner_peer(r),
            device_id_type=MESH,
        )

    def column(half, r):
        return pltpu.make_async_remote_copy(
            zpiece.at[half],
            zbuf.at[half, r],
            z_s.at[half, r],
            z_r.at[half, r],
            device_id={"outer": lax.rem(o + r, no)},
            device_id_type=MESH,
        )

    def gather(half, r):
        return pltpu.make_async_remote_copy(
            fsum.at[half],
            far.at[(half, slice(None), *part(i))],
            g_s.at[half, r],
            g_r.at[half, r],
            device_id=inner_peer(r),
            device_id_type=MESH,
        )

    def column_step(half):
        total = cand[(half, *part(i))].astype(jnp.float32)
        for r in range(1, ni):
            scatter(half, r).wait_recv()
            total = total + rbuf[half, r].astype(jnp.float32)
        zpiece[half] = total.astype(jnp.bfloat16)
        for r in range(1, no):
            pl.when(o + r < no)(column(half, r).start)

    def slot_of(row):
        return lax.rem(row * (ni * nb) // STRIDE, slots)

    def gather_step(half):
        fsum[half, slot_of(o)] = zpiece[half]
        for r in range(1, no):

            @pl.when(o >= r)
            def _():
                column(half, r).wait_recv()
                at = slot_of(o - r)
                fsum[half, at] = (
                    fsum[half, at].astype(jnp.float32) + zbuf[half, r].astype(jnp.float32)
                ).astype(jnp.bfloat16)

        for r in range(1, ni):
            gather(half, r).start()
        far[(half, slice(None), *part(i))] = fsum[half]

    def gather_wait(half):
        for r in range(1, ni):
            gather(half, r).wait_recv()

    loads[0].wait()
    loads[4].wait()

    row_ids = lax.broadcasted_iota(jnp.int32, (BLOCK, BLOCK), 0)
    col_ids = lax.broadcasted_iota(jnp.int32, (BLOCK, BLOCK), 1)
    causal = jnp.concatenate([row_ids >= col_ids] * per_group, 0)
    ones = jnp.ones((LOCAL * BLOCK, HEAD_DIM), jnp.bfloat16)

    def near(step, carry):
        b = jnp.where(step < nb - 2, step + 2, nb - 1 - step)

        @pl.when(b == 0)
        def _():
            @pl.when(has_prev)
            def _():
                tails[2].wait_recv()
                tails[3].wait_recv()
                tails[4].wait_recv()

            kv_conv(0)

        bias = jnp.where((b == 0) & (d == 0), NEG, 0.0)
        base = pl.multiple_of(b * BLOCK, BLOCK)
        for g in range(groups):
            wide = slice(g * per_group * HEAD_DIM, (g + 1) * per_group * HEAD_DIM)
            cols = slice(g * HEAD_DIM, (g + 1) * HEAD_DIM)
            q = conv(qpad[pl.ds(base, BLOCK + HALO), wide], qt_ref[:, wide])
            q = jnp.concatenate(
                [q[:, h * HEAD_DIM : (h + 1) * HEAD_DIM] for h in range(per_group)], 0
            )
            qs[b, g] = q
            k = kvc[0, pl.ds(base, LOCAL * BLOCK), cols]
            v = kvc[1, pl.ds(base, LOCAL * BLOCK), cols]
            s = lax.dot_general(q, k, NT, preferred_element_type=jnp.float32)
            prev = s[:, :BLOCK] + bias
            own = jnp.where(causal, s[:, BLOCK:], NEG)
            peak = jnp.max(jnp.maximum(prev, own), axis=1, keepdims=True)
            p = jnp.concatenate(
                [jnp.exp2((prev - peak) * SCALE), jnp.exp2((own - peak) * SCALE)], 1
            ).astype(jnp.bfloat16)
            acc_ref[b, g] = jnp.dot(
                p, jnp.concatenate([v, ones], 1), preferred_element_type=jnp.float32
            )
            max_ref[b, g] = jnp.broadcast_to(peak, (per_group * BLOCK, HEAD_DIM))

        pl.when(step == 0)(first_sends)
        pl.when(step == 1)(candidate_step)

        @pl.when(step == 2)
        def _():
            column_step(0)
            column_step(1)

        return carry

    lax.fori_loop(0, nb, near, 0)
    gather_step(0)
    gather_step(1)
    gather_wait(0)

    def distant_keys(b, carry):
        biases = []
        for n in range(slots):
            seen = jnp.int32(0)
            for e in range(entries):
                entry = list_ref[b, e]
                hit = (entry >= n * STRIDE) & (entry < (n + 1) * STRIDE)
                hit = hit & (entry <= d * nb + b - LOCAL)
                seen = jnp.where(hit, 1, seen)
            biases.append(jnp.where(seen > 0, 0.0, NEG))
        for g in range(groups):
            cols = slice(g * HEAD_DIM, (g + 1) * HEAD_DIM)
            q = qs[b, g]
            near_peak = max_ref[b, g]
            scores = []
            top = None
            for n in range(slots):
                s = lax.dot_general(q, far[0, n, :, cols], NT, preferred_element_type=jnp.float32)
                s = s + biases[n]
                scores.append(s)
                top = s if top is None else jnp.maximum(top, s)
            peak = jnp.maximum(near_peak, jnp.max(top, axis=1, keepdims=True))
            max_ref[b, g] = jnp.exp2((near_peak - peak) * SCALE)
            for n in range(slots):
                p = jnp.exp2((scores[n] - peak) * SCALE)
                pbuf[b, g, :, n * BLOCK : (n + 1) * BLOCK] = p.astype(jnp.bfloat16)
        return carry

    def distant_values(b, carry):
        base = pl.multiple_of(b * BLOCK, BLOCK)
        for g in range(groups):
            cols = slice(g * HEAD_DIM, (g + 1) * HEAD_DIM)
            both = acc_ref[b, g]
            shrink = max_ref[b, g]
            total = both[:, :HEAD_DIM] * shrink
            count = both[:, HEAD_DIM:] * shrink
            for n in range(slots):
                more = jnp.dot(
                    pbuf[b, g, :, n * BLOCK : (n + 1) * BLOCK],
                    jnp.concatenate([far[1, n, :, cols], ones[:BLOCK]], 1),
                    preferred_element_type=jnp.float32,
                )
                total = total + more[:, :HEAD_DIM]
                count = count + more[:, HEAD_DIM:]
            mixed = (total / count).astype(jnp.bfloat16)
            for h in range(per_group):
                head = g * per_group + h
                outb[pl.ds(base, BLOCK), head * HEAD_DIM : (head + 1) * HEAD_DIM] = mixed[
                    h * BLOCK : (h + 1) * BLOCK
                ]
        return carry

    lax.fori_loop(0, nb, distant_keys, 0)
    gather_wait(1)
    lax.fori_loop(0, nb, distant_values, 0)

    @pl.when(has_prev)
    def _():
        w_copy.wait_send()

    @pl.when(has_next)
    def _():
        for copy in tails:
            copy.wait_send()

    for half in range(2):
        for r in range(1, ni):
            scatter(half, r).wait_send()
            gather(half, r).wait_send()
        for r in range(1, no):
            pl.when(o + r < no)(column(half, r).wait_send)


ROWS = 4
SUMS = ({0: (1,), 2: (3,)}, {0: (2,), 1: (2,)})
SPREADS = ({1: (3, 2)}, {2: (3, 1)})
TAKEN = ((), (1,))
FIRST_ROW_STEP = 1
SITE_AFTER = (2, 2)
LATE_TAILS = False
UNROLL = 4
LATE = ((2, 3), (1, 3), (0, 2))


def dests(row, late):
    rows = {r for table in (*SUMS, *SPREADS) for r in table.get(row, ())}
    return sorted(r for r in rows if ((row, r) in LATE) == late)


def origins(row, late):
    return [r for r in range(ROWS) if row in dests(r, late)]


def paired_kernel(
    list_hbm, q_hbm, k_hbm, v_hbm, qt_hbm, kt_hbm, vt_hbm, outb,
    list_ref, qt_ref, kt_ref, vt_ref, qpad, kvpad, kvc, qs, acc_ref, max_ref, pbuf,
    flag_out, flag_in, chip, cand, rrow, rother, site, zfar, far_k, far_v,
    in_sem, own_sem, fl_s, fl_r, raw_s, raw_r, rim_s, rim_r, tail_s, tail_r,
    a_s, a_r, b_s, b_r, c_s, c_r, d_s, d_r, e_s, e_r, ready,
):
    tokens, qw = q_hbm.shape
    kvw = k_hbm.shape[1]
    groups = kvw // HEAD_DIM
    hw = kvw // 2
    quarter = hw // 2
    per_group = qw // kvw
    nb = tokens // BLOCK
    before = BLOCK + HALO
    entries = list_ref.shape[1]
    o = lax.axis_index("outer")
    i = lax.axis_index("inner")
    y = i // 2
    c = lax.rem(i, 2)
    m = o * 2 + y
    no = ROWS
    last_chip = no * 2 - 1
    d = o * 4 + i
    has_next = d < 4 * no - 1
    has_prev = d > 0
    chip_next = m < last_chip
    chip_prev = m > 0
    first_core = c == 0
    second_core = c == 1

    def chip_core(step, core):
        other = m + step
        return {"outer": other // 2, "inner": lax.rem(other, 2) * 2 + core}

    def at(row, col):
        return {"outer": row, "inner": col * 2 + c}

    peer_core = {"inner": i + 1 - 2 * c}
    peer_y = {"inner": lax.rem(i + 2, 4)}
    next_device = {"outer": (d + 1) // 4, "inner": lax.rem(d + 1, 4)}

    barrier = pltpu.get_barrier_semaphore()

    def greet(device):
        pl.semaphore_signal(barrier, inc=1, device_id=device, device_id_type=MESH)

    def call(device):
        pl.semaphore_signal(ready, inc=1, device_id=device, device_id_type=MESH)

    loads = [
        pltpu.make_async_copy(q_hbm, qpad.at[pl.ds(HALO, tokens)], in_sem.at[0]),
        pltpu.make_async_copy(k_hbm, kvpad.at[0, pl.ds(before, tokens)], in_sem.at[1]),
        pltpu.make_async_copy(v_hbm, kvpad.at[1, pl.ds(before, tokens)], in_sem.at[2]),
        pltpu.make_async_copy(list_hbm, list_ref, in_sem.at[3]),
        pltpu.make_async_copy(qt_hbm, qt_ref, in_sem.at[4]),
        pltpu.make_async_copy(kt_hbm, kt_ref, in_sem.at[5]),
        pltpu.make_async_copy(vt_hbm, vt_ref, in_sem.at[6]),
    ]
    half_cols = pl.ds(pl.multiple_of(c * hw, hw), hw)
    peer_cols = pl.ds(pl.multiple_of((1 - c) * hw, hw), hw)
    chip_rows = pl.ds(pl.multiple_of(HALO + c * tokens, HALO), tokens)
    own = [
        pltpu.make_async_copy(x.at[:, half_cols], chip.at[h, chip_rows], own_sem.at[h])
        for h, x in enumerate((k_hbm, v_hbm))
    ]
    loads[3].start()
    greet(peer_core)
    greet(peer_y)

    late_next = (y == 1) & functools.reduce(
        jnp.logical_or, [o == row for row in range(no - 1) if (row, row + 1) in LATE], o < 0
    )
    late_prev = (y == 0) & functools.reduce(
        jnp.logical_or, [o == row + 1 for row in range(no - 1) if (row, row + 1) in LATE], o < 0
    )

    @pl.when(chip_next)
    def _():
        greet(chip_core(1, 0))
        pl.when(second_core & late_next)(lambda: greet(chip_core(1, 1)))

    pl.when(chip_prev & jnp.logical_not(late_prev))(lambda: greet(chip_core(-1, 1)))
    for row in range(no):

        @pl.when(o == row)
        def _():
            for other in origins(row, False) + dests(row, True):
                greet(at(other, 0))
                greet(at(other, 1))

    for n in (1, 5, 2, 6):
        loads[n].start()
    for copy in own:
        copy.start()
    for n in (0, 4):
        loads[n].start()

    def remote(src, dst, send, recv, device):
        return pltpu.make_async_remote_copy(
            src, dst, send, recv, device_id=device, device_id_type=MESH
        )

    flag_back = [
        remote(flag_out, flag_in.at[0], fl_s.at[k], fl_r.at[0], chip_core(-1, k)) for k in range(2)
    ]
    flag_peer = remote(flag_out, flag_in.at[1], fl_s.at[2], fl_r.at[1], peer_core)
    raws = [
        remote(x.at[:, peer_cols], chip.at[h, chip_rows], raw_s.at[h], raw_r.at[h], peer_core)
        for h, x in enumerate((k_hbm, v_hbm))
    ]
    rim = pl.ds(tokens - HALO, HALO)
    rims = [
        [
            remote(
                x.at[rim, k * hw : (k + 1) * hw],
                chip.at[h, pl.ds(0, HALO)],
                rim_s.at[k, h],
                rim_r.at[h],
                chip_core(1, k),
            )
            for h, x in enumerate((k_hbm, v_hbm))
        ]
        for k in range(2)
    ]
    body_rows = pl.ds(tokens - before, BLOCK)

    def to_next(n, src, dst):
        return remote(src, dst, tail_s.at[n], tail_r.at[n], next_device)

    edges = [
        to_next(h, x.at[rim], kvpad.at[h, pl.ds(BLOCK, HALO)]) for h, x in enumerate((k_hbm, v_hbm))
    ]
    tails = [
        to_next(2 + h, x.at[body_rows], kvpad.at[h, pl.ds(0, BLOCK)])
        for h, x in enumerate((k_hbm, v_hbm))
    ] + [to_next(4, q_hbm.at[rim], qpad.at[pl.ds(0, HALO)])]

    @pl.when(jnp.logical_not(has_prev))
    def _():
        qpad[0:HALO, :] = jnp.zeros((HALO, qw), jnp.bfloat16)
        kvpad[:, 0:before, :] = jnp.zeros((2, before, kvw), jnp.bfloat16)

    @pl.when(jnp.logical_not(chip_prev))
    def _():
        chip[:, 0:HALO, :] = jnp.zeros((2, HALO, hw), jnp.bfloat16)

    far_k[...] = jnp.zeros(far_k.shape, jnp.bfloat16)

    @pl.when(jnp.logical_not(chip_next))
    def _():
        flag_in[0] = jnp.full(flag_in.shape[1:], -1, jnp.int32)

    @pl.when(second_core)
    def _():
        flag_in[1] = jnp.full(flag_in.shape[1:], -1, jnp.int32)

    expected = 2 + jnp.where(chip_prev & first_core, 2, 0)
    expected = expected + jnp.where(chip_prev & late_prev & second_core, 1, 0)
    sends_on = second_core & chip_next
    expected = expected + jnp.where(sends_on & jnp.logical_not(late_next), 2, 0)
    awaited = jnp.where(sends_on & late_next, 2, 0)
    for row in range(no):
        met = 2 * len(dests(row, False) + origins(row, True))
        expected = expected + jnp.where(o == row, met, 0)
        awaited = awaited + jnp.where(o == row, 2 * len(dests(row, True)), 0)
    pl.semaphore_wait(barrier, expected)
    pl.when(chip_prev & late_prev)(lambda: call(chip_core(-1, 1)))
    for row in range(no):
        if origins(row, True):

            @pl.when(o == row)
            def _():
                for src in origins(row, True):
                    call(at(src, 0))
                    call(at(src, 1))

    for copy in raws:
        copy.start()

    loads[3].wait()
    phase = jnp.int32(-1)
    for b in range(nb):
        for e in range(entries):
            entry = list_ref[b, e]
            distant = (entry >= 0) & (entry <= d * nb + b - LOCAL)
            phase = jnp.maximum(phase, jnp.where(distant, lax.rem(entry, STRIDE), -1))
    flag_out[...] = jnp.full(flag_out.shape, phase, jnp.int32)

    @pl.when(first_core & chip_prev)
    def _():
        for copy in flag_back:
            copy.start()

    pl.when(second_core)(flag_peer.start)
    def next_sends():
        @pl.when(sends_on)
        def _():
            for h in range(2):
                for k in range(2):
                    rims[k][h].start()

        @pl.when(has_next)
        def _():
            for copy in edges:
                copy.start()

    def tail_sends():
        @pl.when(has_next)
        def _():
            for copy in tails:
                copy.start()

    held_back = sends_on & late_next
    pl.when(jnp.logical_not(held_back))(next_sends)
    if not LATE_TAILS:
        pl.when(jnp.logical_not(held_back))(tail_sends)

    def kv_conv(b):
        rows = slice(b * BLOCK, b * BLOCK + before)
        dst = slice(b * BLOCK, (b + 1) * BLOCK)
        kvc[0, dst, :] = conv(kvpad[0, rows, :], kt_ref[...])
        kvc[1, dst, :] = conv(kvpad[1, rows, :], vt_ref[...])

    def cols_of(col):
        return slice(col * quarter, (col + 1) * quarter)

    def to_peer_site(h):
        return remote(cand.at[h, 1 - y], rrow.at[h], a_s.at[h], a_r.at[h], peer_y)

    def to_site(h, row, col):
        return remote(
            cand.at[h, col], rother.at[h, o, y], b_s.at[h, row, col], b_r.at[h, o, y], at(row, col)
        )

    def at_site(h, src, col):
        return remote(
            cand.at[h, col], rother.at[h, src, col], b_s.at[h, 0, col], b_r.at[h, src, col], peer_y
        )

    def to_peer_col(h):
        return remote(site.at[h, y], site.at[h, y], c_s.at[h], c_r.at[h], peer_y)

    def from_peer_col(h):
        return remote(site.at[h, 1 - y], site.at[h, 1 - y], c_s.at[h], c_r.at[h], peer_y)

    def to_later(h, row, col):
        return remote(
            site.at[h, y], zfar.at[h, o, y], d_s.at[h, row, col], d_r.at[h, o, y], at(row, col)
        )

    def from_earlier(h, src, col):
        return remote(
            site.at[h, y], zfar.at[h, src, col], d_s.at[h, 0, 0], d_r.at[h, src, col], peer_y
        )

    def core_swap(h, core):
        if h == 0:
            part = far_k.at[core]
        else:
            part = far_v.at[pl.ds(2 * core, 2)]
        return remote(part, part, e_s.at[h], e_r.at[h], peer_core)

    def to_peer_core(h):
        return core_swap(h, c)

    def from_peer_core(h):
        return core_swap(h, 1 - c)

    def sums_own(h):
        return functools.reduce(jnp.logical_and, [o != row for row in TAKEN[h]], o >= 0)

    def candidate_step():
        pl.when(awaited > 0)(lambda: pl.semaphore_wait(ready, awaited))
        pl.when(held_back)(next_sends)

        @pl.when(chip_next)
        def _():
            remote(flag_out, flag_in.at[0], fl_s.at[0], fl_r.at[0], peer_core).wait_recv()

        @pl.when(first_core)
        def _():
            flag_peer.wait_recv()

        known = jnp.maximum(jnp.maximum(flag_in[0, 0:1, :], flag_in[1, 0:1, :]), phase)
        first = m * 2 * nb
        weights = [
            jnp.where(known == first + b, 1.0, 0.0).astype(jnp.bfloat16) for b in range(2 * nb)
        ]
        for h, taps in enumerate((kt_ref, vt_ref)):
            own[h].wait()
            raws[h].wait_recv()

            @pl.when(chip_prev)
            def _():
                rims[0][h].wait_recv()

            raw = weights[0] * chip[h, 0:before, :]
            for b in range(1, 2 * nb):
                raw = raw + weights[b] * chip[h, b * BLOCK : b * BLOCK + before, :]
            total = conv(raw, taps[:, half_cols])
            for col in range(2):
                cand[h, col] = total[:, cols_of(col)]

            for src, rows in SUMS[h].items():

                @pl.when(o == src)
                def _():
                    for row in rows:
                        for col in range(2):
                            to_site(h, row, col).start()

            pl.when(sums_own(h))(to_peer_site(h).start)

        if LATE_TAILS:
            tail_sends()
        else:
            pl.when(held_back)(tail_sends)

    def site_step(h):
        pl.when(sums_own(h))(functools.partial(own_site_step, h))

    def own_site_step(h):
        to_peer_site(h).wait_recv()
        site[h, y] = cand[h, y] + rrow[h]
        for row in range(no):
            sources = [src for src, rows in SUMS[h].items() if row in rows]
            if sources:

                @pl.when(o == row)
                def _():
                    for src in sources:
                        for col in range(2):
                            at_site(h, src, col).wait_recv()
                            site[h, y] = site[h, y] + rother[h, src, col]

        for src, rows in SPREADS[h].items():

            @pl.when(o == src)
            def _():
                for row in rows:
                    for col in range(2):
                        to_later(h, row, col).start()

        to_peer_col(h).start()

    def final_step(h):
        pl.when(sums_own(h))(from_peer_col(h).wait_recv)
        for src, rows in SPREADS[h].items():
            for row in rows:

                @pl.when(o == row)
                def _():
                    for col in range(2):
                        from_earlier(h, src, col).wait_recv()
                        if row in TAKEN[h]:
                            zfar[h, o, col] = zfar[h, src, col]
                        else:
                            zfar[h, o, col] = zfar[h, src, col] + site[h, col]

        gets = functools.reduce(
            jnp.logical_or, [o == row for rows in SPREADS[h].values() for row in rows]
        )

        def place(source):
            for col in range(2):
                if h == 0:
                    far_k[c, cols_of(col), cols_of(col)] = source(col)
                else:
                    far_v[2 * c + col] = source(col)

        pl.when(gets)(lambda: place(lambda col: zfar[h, o, col]))
        pl.when(jnp.logical_not(gets))(lambda: place(lambda col: site[h, col]))
        to_peer_core(h).start()

    for n in (1, 5, 2, 6):
        loads[n].wait()
    for b in range(2, nb + 1):
        kv_conv(b)
    loads[0].wait()
    loads[4].wait()

    row_ids = lax.broadcasted_iota(jnp.int32, (BLOCK, BLOCK), 0)
    col_ids = lax.broadcasted_iota(jnp.int32, (BLOCK, BLOCK), 1)
    causal = jnp.concatenate([row_ids >= col_ids] * per_group, 0)
    ones = jnp.ones((LOCAL * BLOCK, HEAD_DIM), jnp.bfloat16)

    def near(step, carry):
        b = jnp.where(step < nb - 2, step + 2, nb - 1 - step)

        @pl.when(b == 1)
        def _():
            @pl.when(has_prev)
            def _():
                for copy in edges:
                    copy.wait_recv()

            kv_conv(1)

        @pl.when(b == 0)
        def _():
            @pl.when(has_prev)
            def _():
                for copy in tails:
                    copy.wait_recv()

            kv_conv(0)

        bias = jnp.where((b == 0) & (d == 0), NEG, 0.0)
        base = pl.multiple_of(b * BLOCK, BLOCK)
        for g in range(groups):
            wide = slice(g * per_group * HEAD_DIM, (g + 1) * per_group * HEAD_DIM)
            cols = slice(g * HEAD_DIM, (g + 1) * HEAD_DIM)
            q = conv(qpad[pl.ds(base, BLOCK + HALO), wide], qt_ref[:, wide])
            q = jnp.concatenate(
                [q[:, h * HEAD_DIM : (h + 1) * HEAD_DIM] for h in range(per_group)], 0
            )
            qs[b, g // 2, :, cols_of(g % 2)] = q
            k = kvc[0, pl.ds(base, LOCAL * BLOCK), cols]
            v = kvc[1, pl.ds(base, LOCAL * BLOCK), cols]
            s = lax.dot_general(q, k, NT, preferred_element_type=jnp.float32)
            prev = s[:, :BLOCK] + bias
            mine = jnp.where(causal, s[:, BLOCK:], NEG)
            peak = jnp.max(jnp.maximum(prev, mine), axis=1, keepdims=True)
            p = jnp.concatenate(
                [jnp.exp2((prev - peak) * SCALE), jnp.exp2((mine - peak) * SCALE)], 1
            ).astype(jnp.bfloat16)
            acc_ref[b, g] = jnp.dot(
                p, jnp.concatenate([v, ones], 1), preferred_element_type=jnp.float32
            )
            max_ref[b, g] = jnp.broadcast_to(peak, (per_group * BLOCK, HEAD_DIM))

        pl.when(step == jnp.where(o == 0, FIRST_ROW_STEP, 0))(candidate_step)
        for h in range(2):
            if SITE_AFTER[h] is not None:
                pl.when(step == SITE_AFTER[h])(functools.partial(site_step, h))
        return carry

    lax.fori_loop(0, nb, near, 0)
    for h in range(2):
        if SITE_AFTER[h] is None:
            site_step(h)
    final_step(0)

    def distant_keys(pair, b):
        seen = jnp.int32(0)
        for e in range(entries):
            entry = list_ref[b, e]
            seen = jnp.where((entry >= 0) & (entry <= d * nb + b - LOCAL), 1, seen)
        bias = jnp.where(seen > 0, 0.0, NEG)
        both = lax.dot_general(qs[b, pair], far_k[pair], NT, preferred_element_type=jnp.float32)
        for n in range(2):
            g = 2 * pair + n
            s = both[:, cols_of(n)] + bias
            near_peak = max_ref[b, g]
            peak = jnp.maximum(near_peak, jnp.max(s, axis=1, keepdims=True))
            max_ref[b, g] = jnp.exp2((near_peak - peak) * SCALE)
            pbuf[b, g] = jnp.exp2((s - peak) * SCALE).astype(jnp.bfloat16)

    def distant_values(pair, b):
        base = pl.multiple_of(b * BLOCK, BLOCK)
        for n in range(2):
            g = 2 * pair + n
            shrink = max_ref[b, g]
            more = jnp.dot(
                pbuf[b, g],
                jnp.concatenate([far_v[g], ones[:BLOCK]], 1),
                preferred_element_type=jnp.float32,
            )
            total = acc_ref[b, g, :, :HEAD_DIM] * shrink + more[:, :HEAD_DIM]
            count = acc_ref[b, g, :, HEAD_DIM:] * shrink + more[:, HEAD_DIM:]
            inverse = pl.reciprocal(count, approx=True)
            inverse = inverse * (2.0 - count * inverse)
            mixed = (total * inverse).astype(jnp.bfloat16)
            for h in range(per_group):
                head = g * per_group + h
                outb[pl.ds(base, BLOCK), head * HEAD_DIM : (head + 1) * HEAD_DIM] = mixed[
                    h * BLOCK : (h + 1) * BLOCK
                ]

    def loop(run, pair):
        def step(b, carry):
            run(pair, b)
            return carry

        lax.fori_loop(0, nb, step, 0, unroll=UNROLL)

    def far_stage(pair):
        loop(distant_keys, pair)
        loop(distant_values, pair)
        core_swap(0, 1 - pair).wait_recv()
        loop(distant_keys, 1 - pair)
        core_swap(1, 1 - pair).wait_recv()
        loop(distant_values, 1 - pair)

    final_step(1)
    pl.when(first_core)(functools.partial(far_stage, 0))
    pl.when(second_core)(functools.partial(far_stage, 1))

    @pl.when(first_core & chip_prev)
    def _():
        for copy in flag_back:
            copy.wait_send()

    @pl.when(second_core)
    def _():
        flag_peer.wait_send()

        @pl.when(chip_next)
        def _():
            for k in range(2):
                for copy in rims[k]:
                    copy.wait_send()

    @pl.when(has_next)
    def _():
        for copy in edges + tails:
            copy.wait_send()

    for h in range(2):
        raws[h].wait_send()

        @pl.when(sums_own(h))
        def _():
            to_peer_site(h).wait_send()
            to_peer_col(h).wait_send()

        to_peer_core(h).wait_send()

        for table, copy in ((SUMS, to_site), (SPREADS, to_later)):
            for src, rows in table[h].items():

                @pl.when(o == src)
                def _():
                    for row in rows:
                        for col in range(2):
                            copy(h, row, col).wait_send()


def paired_call(arrays):
    block_list, q_proj, k_proj = arrays[:3]
    q_taps, k_taps, v_taps = arrays[4:]
    tokens, qw = q_proj.shape
    kvw = k_proj.shape[1]
    nb = tokens // BLOCK
    groups = kvw // HEAD_DIM
    rows = qw // kvw * BLOCK
    hw = kvw // 2
    piece = (BLOCK, hw // 2)
    dma = pltpu.SemaphoreType.DMA
    bf16, f32 = jnp.bfloat16, jnp.float32
    hbm_spec = pl.BlockSpec(memory_space=pltpu.HBM)
    scores = nb * groups * rows * (LOCAL + 1) * BLOCK
    return pl.pallas_call(
        paired_kernel,
        out_shape=jax.ShapeDtypeStruct((tokens, qw), bf16),
        in_specs=[hbm_spec] * 7,
        out_specs=pl.BlockSpec(memory_space=pltpu.VMEM),
        scratch_shapes=[
            pltpu.SMEM(block_list.shape, jnp.int32),
            pltpu.VMEM(q_taps.shape, f32),
            pltpu.VMEM(k_taps.shape, f32),
            pltpu.VMEM(v_taps.shape, f32),
            pltpu.VMEM((tokens + HALO, qw), bf16),
            pltpu.VMEM((2, tokens + BLOCK + HALO, kvw), bf16),
            pltpu.VMEM((2, tokens + BLOCK, kvw), bf16),
            pltpu.VMEM((nb, groups // 2, rows, 2 * HEAD_DIM), bf16),
            pltpu.VMEM((nb, groups, rows, 2 * HEAD_DIM), f32),
            pltpu.VMEM((nb, groups, rows, HEAD_DIM), f32),
            pltpu.VMEM((nb, groups, rows, BLOCK), bf16),
            pltpu.VMEM((8, hw), jnp.int32),
            pltpu.VMEM((2, 8, hw), jnp.int32),
            pltpu.VMEM((2, 2 * tokens + HALO, hw), bf16),
            pltpu.VMEM((2, 2, *piece), bf16),
            pltpu.VMEM((2, *piece), bf16),
            pltpu.VMEM((2, ROWS, 2, *piece), bf16),
            pltpu.VMEM((2, 2, *piece), bf16),
            pltpu.VMEM((2, ROWS, 2, *piece), bf16),
            pltpu.VMEM((groups // 2, 2 * BLOCK, hw), bf16),
            pltpu.VMEM((groups, BLOCK, HEAD_DIM), bf16),
            dma((7,)),
            dma((2,)),
            dma((3,)),
            dma((2,)),
            dma((2,)),
            dma((2,)),
            dma((2, 2)),
            dma((2,)),
            dma((5,)),
            dma((5,)),
            dma((2,)),
            dma((2,)),
            dma((2, ROWS, 2)),
            dma((2, ROWS, 2)),
            dma((2,)),
            dma((2,)),
            dma((2, ROWS, 2)),
            dma((2, ROWS, 2)),
            dma((2,)),
            dma((2,)),
            pltpu.SemaphoreType.REGULAR,
        ],
        compiler_params=pltpu.CompilerParams(
            collective_id=0, has_side_effects=True, vmem_limit_bytes=48 * 1024 * 1024
        ),
        cost_estimate=pl.CostEstimate(
            flops=4 * scores * HEAD_DIM,
            bytes_accessed=4 * tokens * qw + 4 * tokens * kvw,
            transcendentals=scores,
        ),
    )(*arrays)


def body(q_proj, k_proj, v_proj, q_taps, k_taps, v_taps, block_list):
    tokens, qw = q_proj.shape
    kvw = k_proj.shape[1]
    ni = lax.axis_size("inner")
    no = lax.axis_size("outer")
    nb = tokens // BLOCK
    groups = kvw // HEAD_DIM
    rows = qw // kvw * BLOCK
    slots = max(1, nb * ni * no // STRIDE)
    piece_rows = max(HALO, BLOCK // ni)
    piece_cols = BLOCK * kvw // (ni * piece_rows)
    piece = (piece_rows, piece_cols)
    dma = pltpu.SemaphoreType.DMA
    bf16, f32 = jnp.bfloat16, jnp.float32
    hbm_spec = pl.BlockSpec(memory_space=pltpu.HBM)
    scores = nb * groups * rows * (LOCAL + slots) * BLOCK
    arrays = [
        pltpu.with_memory_space_constraint(x, pltpu.HBM)
        for x in (block_list, q_proj, k_proj, v_proj, q_taps, k_taps, v_taps)
    ]
    paired = ni == 4 and no == ROWS and nb * ni * no == STRIDE and groups == 4 and nb >= 2
    if paired:
        return paired_call(arrays)
    return pl.pallas_call(
        functools.partial(kernel, ni, no),
        out_shape=jax.ShapeDtypeStruct((tokens, qw), bf16),
        in_specs=[hbm_spec] * 7,
        out_specs=pl.BlockSpec(memory_space=pltpu.VMEM),
        scratch_shapes=[
            pltpu.SMEM(block_list.shape, jnp.int32),
            pltpu.VMEM(q_taps.shape, f32),
            pltpu.VMEM(k_taps.shape, f32),
            pltpu.VMEM(v_taps.shape, f32),
            pltpu.VMEM((tokens + HALO, qw), bf16),
            pltpu.VMEM((2, tokens + BLOCK + HALO, kvw), bf16),
            pltpu.VMEM((2, tokens + BLOCK, kvw), bf16),
            pltpu.VMEM((nb, groups, rows, HEAD_DIM), bf16),
            pltpu.VMEM((nb, groups, rows, 2 * HEAD_DIM), f32),
            pltpu.VMEM((nb, groups, rows, HEAD_DIM), f32),
            pltpu.VMEM((nb, groups, rows, slots * BLOCK), bf16),
            pltpu.VMEM((max(8, nb), 128), f32),
            pltpu.VMEM((max(8, nb), 128), f32),
            pltpu.VMEM((2, BLOCK, kvw), bf16),
            pltpu.VMEM((2, ni, *piece), bf16),
            pltpu.VMEM((2, *piece), bf16),
            pltpu.VMEM((2, no, *piece), bf16),
            pltpu.VMEM((2, slots, *piece), bf16),
            pltpu.VMEM((2, slots, BLOCK, kvw), bf16),
            dma((7,)),
            dma((5,)),
            dma((5,)),
            dma,
            dma,
            dma((2, ni)),
            dma((2, ni)),
            dma((2, no)),
            dma((2, no)),
            dma((2, ni)),
            dma((2, ni)),
        ],
        compiler_params=pltpu.CompilerParams(
            collective_id=0, has_side_effects=True, vmem_limit_bytes=48 * 1024 * 1024
        ),
        cost_estimate=pl.CostEstimate(
            flops=4 * scores * HEAD_DIM,
            bytes_accessed=4 * tokens * qw + 4 * tokens * kvw,
            transcendentals=scores,
        ),
    )(*arrays)


def solution(mesh):
    rows = P(("groups", "outer", "inner"), None)
    return jax.shard_map(
        body,
        mesh=mesh,
        in_specs=(rows, rows, rows, P(), P(), P(), rows),
        out_specs=rows,
        check_vma=False,
    )
```

```python
import functools
import math

import jax
import jax.numpy as jnp
from jax import lax
from jax.experimental import pallas as pl
from jax.experimental.pallas import tpu as pltpu
from jax.sharding import PartitionSpec as P

HEAD_DIM = 128
BLOCK = 128
LOCAL = 2
STRIDE = 64
HALO = 16
NEG = -1e30
MESH = pl.DeviceIdType.MESH
SCALE = math.log2(math.e) / math.sqrt(HEAD_DIM)
NT = (((1,), (1,)), ((), ()))


def conv(padded, taps):
    wide = padded.astype(jnp.float32)
    total = taps[0:1] * wide[HALO:]
    for j in (1, 2):
        total = total + taps[j : j + 1] * pltpu.roll(wide, j, 0)[HALO:]
    return total.astype(jnp.bfloat16)


def kernel(
    ni, no, list_hbm, q_hbm, k_hbm, v_hbm, qt_hbm, kt_hbm, vt_hbm, outb,
    list_ref, qt_ref, kt_ref, vt_ref, qpad, kvpad, kvc, qs, acc_ref, max_ref, pbuf, wout, win, cand, rbuf, zpiece, zbuf,
    fsum, far, in_sem, tail_s, tail_r, w_s, w_r, sc_s, sc_r, z_s, z_r,
    g_s, g_r,
):
    tokens, qw = q_hbm.shape
    kvw = k_hbm.shape[1]
    groups = kvw // HEAD_DIM
    per_group = qw // kvw
    nb = tokens // BLOCK
    slots = far.shape[1]
    piece_rows, piece_cols = zpiece.shape[1:]
    col_parts = kvw // piece_cols
    before = BLOCK + HALO
    entries = list_ref.shape[1]
    o = lax.axis_index("outer")
    i = lax.axis_index("inner")
    d = o * ni + i
    last = ni * no - 1
    has_next = d < last
    has_prev = d > 0

    def chain(step):
        other = d + step
        return {"outer": other // ni, "inner": lax.rem(other, ni)}

    def inner_peer(r):
        return {"inner": lax.rem(i + r, ni)}

    loads = [
        pltpu.make_async_copy(q_hbm, qpad.at[pl.ds(HALO, tokens)], in_sem.at[0]),
        pltpu.make_async_copy(k_hbm, kvpad.at[0, pl.ds(before, tokens)], in_sem.at[1]),
        pltpu.make_async_copy(v_hbm, kvpad.at[1, pl.ds(before, tokens)], in_sem.at[2]),
        pltpu.make_async_copy(list_hbm, list_ref, in_sem.at[3]),
        pltpu.make_async_copy(qt_hbm, qt_ref, in_sem.at[4]),
        pltpu.make_async_copy(kt_hbm, kt_ref, in_sem.at[5]),
        pltpu.make_async_copy(vt_hbm, vt_ref, in_sem.at[6]),
    ]
    for n in (3, 1, 5, 2, 6, 0, 4):
        loads[n].start()

    barrier = pltpu.get_barrier_semaphore()
    for r in range(1, ni):
        pl.semaphore_signal(barrier, inc=1, device_id=inner_peer(r), device_id_type=MESH)
    for r in range(1, no):
        pl.semaphore_signal(
            barrier, inc=1, device_id={"outer": lax.rem(o + r, no)}, device_id_type=MESH
        )

    @pl.when(has_next)
    def _():
        pl.semaphore_signal(barrier, inc=1, device_id=chain(1), device_id_type=MESH)

    @pl.when(has_prev)
    def _():
        pl.semaphore_signal(barrier, inc=1, device_id=chain(-1), device_id_type=MESH)

    loads[3].wait()
    phase = jnp.int32(-1)
    for b in range(nb):
        for e in range(entries):
            entry = list_ref[b, e]
            distant = (entry >= 0) & (entry <= d * nb + b - LOCAL)
            phase = jnp.maximum(phase, jnp.where(distant, lax.rem(entry, STRIDE), -1))
    for b in range(nb):
        hit = lax.rem((d - 1) * nb + b + STRIDE, STRIDE) == phase
        wout[b : b + 1, :] = jnp.full((1, 128), jnp.where(hit, 1.0, 0.0), jnp.float32)
    if nb < wout.shape[0]:
        wout[nb:, :] = jnp.zeros((wout.shape[0] - nb, 128), jnp.float32)

    @pl.when(d == 0)
    def _():
        qpad[0:HALO, :] = jnp.zeros((HALO, qw), jnp.bfloat16)
        kvpad[:, 0:before, :] = jnp.zeros((2, before, kvw), jnp.bfloat16)

    @pl.when(d == last)
    def _():
        win[...] = jnp.zeros(win.shape, jnp.float32)

    fsum[...] = jnp.zeros(fsum.shape, jnp.bfloat16)

    w_copy = pltpu.make_async_remote_copy(
        wout, win, w_s, w_r, device_id=chain(-1), device_id_type=MESH
    )
    rim = pl.ds(tokens - HALO, HALO)
    body_rows = pl.ds(tokens - before, BLOCK)

    def to_next(src, dst, n):
        return pltpu.make_async_remote_copy(
            src, dst, tail_s.at[n], tail_r.at[n], device_id=chain(1), device_id_type=MESH
        )

    tails = [
        to_next(k_hbm.at[rim], kvpad.at[0, pl.ds(BLOCK, HALO)], 0),
        to_next(v_hbm.at[rim], kvpad.at[1, pl.ds(BLOCK, HALO)], 1),
        to_next(k_hbm.at[body_rows], kvpad.at[0, pl.ds(0, BLOCK)], 2),
        to_next(v_hbm.at[body_rows], kvpad.at[1, pl.ds(0, BLOCK)], 3),
        to_next(q_hbm.at[rim], qpad.at[pl.ds(0, HALO)], 4),
    ]

    def first_sends():
        pl.semaphore_wait(
            barrier,
            ni - 1 + no - 1 + jnp.where(has_next, 1, 0) + jnp.where(has_prev, 1, 0),
        )

        @pl.when(has_prev)
        def _():
            w_copy.start()

        @pl.when(has_next)
        def _():
            for copy in tails:
                copy.start()

    def kv_conv(b):
        rows = slice(b * BLOCK, b * BLOCK + before)
        dst = slice(b * BLOCK, (b + 1) * BLOCK)
        kvc[0, dst, :] = conv(kvpad[0, rows, :], kt_ref[...])
        kvc[1, dst, :] = conv(kvpad[1, rows, :], vt_ref[...])

    for n in (1, 5, 2, 6):
        loads[n].wait()
    for b in range(2, nb + 1):
        kv_conv(b)

    def candidate_step():
        @pl.when(has_prev)
        def _():
            tails[0].wait_recv()
            tails[1].wait_recv()

        kv_conv(1)

        @pl.when(has_next)
        def _():
            w_copy.wait_recv()

        for g in range(groups):
            cols = slice(g * HEAD_DIM, (g + 1) * HEAD_DIM)
            for half in range(2):
                total = jnp.zeros((BLOCK, HEAD_DIM), jnp.float32)
                for b in range(nb):
                    own = jnp.where(lax.rem(d * nb + b, STRIDE) == phase, 1.0, 0.0)
                    weight = jnp.maximum(win[b : b + 1, :], own)
                    rows = slice((b + 1) * BLOCK, (b + 2) * BLOCK)
                    total = total + weight * kvc[half, rows, cols].astype(jnp.float32)
                cand[half, :, cols] = total.astype(jnp.bfloat16)

        for half in range(2):
            for r in range(1, ni):
                scatter(half, r).start()

    def part(index):
        row = pl.multiple_of(index // col_parts * piece_rows, piece_rows)
        col = pl.multiple_of(lax.rem(index, col_parts) * piece_cols, piece_cols)
        return pl.ds(row, piece_rows), pl.ds(col, piece_cols)

    def scatter(half, r):
        return pltpu.make_async_remote_copy(
            cand.at[(half, *part(lax.rem(i + r, ni)))],
            rbuf.at[half, r],
            sc_s.at[half, r],
            sc_r.at[half, r],
            device_id=inner_peer(r),
            device_id_type=MESH,
        )

    def column(half, r):
        return pltpu.make_async_remote_copy(
            zpiece.at[half],
            zbuf.at[half, r],
            z_s.at[half, r],
            z_r.at[half, r],
            device_id={"outer": lax.rem(o + r, no)},
            device_id_type=MESH,
        )

    def gather(half, r):
        return pltpu.make_async_remote_copy(
            fsum.at[half],
            far.at[(half, slice(None), *part(i))],
            g_s.at[half, r],
            g_r.at[half, r],
            device_id=inner_peer(r),
            device_id_type=MESH,
        )

    def column_step(half):
        total = cand[(half, *part(i))].astype(jnp.float32)
        for r in range(1, ni):
            scatter(half, r).wait_recv()
            total = total + rbuf[half, r].astype(jnp.float32)
        zpiece[half] = total.astype(jnp.bfloat16)
        for r in range(1, no):
            pl.when(o + r < no)(column(half, r).start)

    def slot_of(row):
        return lax.rem(row * (ni * nb) // STRIDE, slots)

    def gather_step(half):
        fsum[half, slot_of(o)] = zpiece[half]
        for r in range(1, no):

            @pl.when(o >= r)
            def _():
                column(half, r).wait_recv()
                at = slot_of(o - r)
                fsum[half, at] = (
                    fsum[half, at].astype(jnp.float32) + zbuf[half, r].astype(jnp.float32)
                ).astype(jnp.bfloat16)

        for r in range(1, ni):
            gather(half, r).start()
        far[(half, slice(None), *part(i))] = fsum[half]

    def gather_wait(half):
        for r in range(1, ni):
            gather(half, r).wait_recv()

    loads[0].wait()
    loads[4].wait()

    row_ids = lax.broadcasted_iota(jnp.int32, (BLOCK, BLOCK), 0)
    col_ids = lax.broadcasted_iota(jnp.int32, (BLOCK, BLOCK), 1)
    causal = jnp.concatenate([row_ids >= col_ids] * per_group, 0)
    ones = jnp.ones((LOCAL * BLOCK, HEAD_DIM), jnp.bfloat16)

    def near(step, carry):
        b = jnp.where(step < nb - 2, step + 2, nb - 1 - step)

        @pl.when(b == 0)
        def _():
            @pl.when(has_prev)
            def _():
                tails[2].wait_recv()
                tails[3].wait_recv()
                tails[4].wait_recv()

            kv_conv(0)

        bias = jnp.where((b == 0) & (d == 0), NEG, 0.0)
        base = pl.multiple_of(b * BLOCK, BLOCK)
        for g in range(groups):
            wide = slice(g * per_group * HEAD_DIM, (g + 1) * per_group * HEAD_DIM)
            cols = slice(g * HEAD_DIM, (g + 1) * HEAD_DIM)
            q = conv(qpad[pl.ds(base, BLOCK + HALO), wide], qt_ref[:, wide])
            q = jnp.concatenate(
                [q[:, h * HEAD_DIM : (h + 1) * HEAD_DIM] for h in range(per_group)], 0
            )
            qs[b, g] = q
            k = kvc[0, pl.ds(base, LOCAL * BLOCK), cols]
            v = kvc[1, pl.ds(base, LOCAL * BLOCK), cols]
            s = lax.dot_general(q, k, NT, preferred_element_type=jnp.float32)
            prev = s[:, :BLOCK] + bias
            own = jnp.where(causal, s[:, BLOCK:], NEG)
            peak = jnp.max(jnp.maximum(prev, own), axis=1, keepdims=True)
            p = jnp.concatenate(
                [jnp.exp2((prev - peak) * SCALE), jnp.exp2((own - peak) * SCALE)], 1
            ).astype(jnp.bfloat16)
            acc_ref[b, g] = jnp.dot(
                p, jnp.concatenate([v, ones], 1), preferred_element_type=jnp.float32
            )
            max_ref[b, g] = jnp.broadcast_to(peak, (per_group * BLOCK, HEAD_DIM))

        pl.when(step == 0)(first_sends)
        pl.when(step == 1)(candidate_step)

        @pl.when(step == 2)
        def _():
            column_step(0)
            column_step(1)

        return carry

    lax.fori_loop(0, nb, near, 0)
    gather_step(0)
    gather_step(1)
    gather_wait(0)

    def distant_keys(b, carry):
        biases = []
        for n in range(slots):
            seen = jnp.int32(0)
            for e in range(entries):
                entry = list_ref[b, e]
                hit = (entry >= n * STRIDE) & (entry < (n + 1) * STRIDE)
                hit = hit & (entry <= d * nb + b - LOCAL)
                seen = jnp.where(hit, 1, seen)
            biases.append(jnp.where(seen > 0, 0.0, NEG))
        for g in range(groups):
            cols = slice(g * HEAD_DIM, (g + 1) * HEAD_DIM)
            q = qs[b, g]
            near_peak = max_ref[b, g]
            scores = []
            top = None
            for n in range(slots):
                s = lax.dot_general(q, far[0, n, :, cols], NT, preferred_element_type=jnp.float32)
                s = s + biases[n]
                scores.append(s)
                top = s if top is None else jnp.maximum(top, s)
            peak = jnp.maximum(near_peak, jnp.max(top, axis=1, keepdims=True))
            max_ref[b, g] = jnp.exp2((near_peak - peak) * SCALE)
            for n in range(slots):
                p = jnp.exp2((scores[n] - peak) * SCALE)
                pbuf[b, g, :, n * BLOCK : (n + 1) * BLOCK] = p.astype(jnp.bfloat16)
        return carry

    def distant_values(b, carry):
        base = pl.multiple_of(b * BLOCK, BLOCK)
        for g in range(groups):
            cols = slice(g * HEAD_DIM, (g + 1) * HEAD_DIM)
            both = acc_ref[b, g]
            shrink = max_ref[b, g]
            total = both[:, :HEAD_DIM] * shrink
            count = both[:, HEAD_DIM:] * shrink
            for n in range(slots):
                more = jnp.dot(
                    pbuf[b, g, :, n * BLOCK : (n + 1) * BLOCK],
                    jnp.concatenate([far[1, n, :, cols], ones[:BLOCK]], 1),
                    preferred_element_type=jnp.float32,
                )
                total = total + more[:, :HEAD_DIM]
                count = count + more[:, HEAD_DIM:]
            mixed = (total / count).astype(jnp.bfloat16)
            for h in range(per_group):
                head = g * per_group + h
                outb[pl.ds(base, BLOCK), head * HEAD_DIM : (head + 1) * HEAD_DIM] = mixed[
                    h * BLOCK : (h + 1) * BLOCK
                ]
        return carry

    lax.fori_loop(0, nb, distant_keys, 0)
    gather_wait(1)
    lax.fori_loop(0, nb, distant_values, 0)

    @pl.when(has_prev)
    def _():
        w_copy.wait_send()

    @pl.when(has_next)
    def _():
        for copy in tails:
            copy.wait_send()

    for half in range(2):
        for r in range(1, ni):
            scatter(half, r).wait_send()
            gather(half, r).wait_send()
        for r in range(1, no):
            pl.when(o + r < no)(column(half, r).wait_send)


ROWS = 4
SUMS = ({0: (1,), 2: (3,)}, {0: (2,), 1: (2,)})
SPREADS = ({1: (3, 2)}, {2: (3, 1)})
TAKEN = ((), (1,))
FIRST_ROW_STEP = 1
SITE_AFTER = (2, 2)
LATE_TAILS = False
LATE = ((2, 3), (1, 3), (0, 2))


def dests(row, late):
    rows = {r for table in (*SUMS, *SPREADS) for r in table.get(row, ())}
    return sorted(r for r in rows if ((row, r) in LATE) == late)


def origins(row, late):
    return [r for r in range(ROWS) if row in dests(r, late)]


def distant_keys(qs, peaks, max_ref, pbuf, far_k, bias_ref, pair, b):
    both = lax.dot_general(qs[b, pair], far_k[pair], NT, preferred_element_type=jnp.float32)
    bias = bias_ref[b : b + 1, :]
    for n in range(2):
        g = 2 * pair + n
        s = both[:, n * BLOCK : (n + 1) * BLOCK] + bias
        near_peak = peaks[b, g]
        peak = jnp.maximum(near_peak, jnp.max(s, axis=1, keepdims=True))
        max_ref[b, g] = jnp.exp2((near_peak - peak) * SCALE)
        pbuf[b, g] = jnp.exp2((s - peak) * SCALE).astype(jnp.bfloat16)


def distant_values(acc_ref, max_ref, pbuf, far_v, pair, b, dst, first_head):
    per_group = acc_ref.shape[2] // BLOCK
    ones = jnp.ones((BLOCK, HEAD_DIM), jnp.bfloat16)
    for n in range(2):
        g = 2 * pair + n
        shrink = max_ref[b, g]
        more = jnp.dot(
            pbuf[b, g],
            jnp.concatenate([far_v[g], ones], 1),
            preferred_element_type=jnp.float32,
        )
        total = acc_ref[b, g, :, :HEAD_DIM] * shrink + more[:, :HEAD_DIM]
        count = acc_ref[b, g, :, HEAD_DIM:] * shrink + more[:, HEAD_DIM:]
        inverse = pl.reciprocal(count, approx=True)
        inverse = inverse * (2.0 - count * inverse)
        mixed = (total * inverse).astype(jnp.bfloat16)
        for h in range(per_group):
            head = first_head + n * per_group + h
            dst[b * BLOCK : (b + 1) * BLOCK, head * HEAD_DIM : (head + 1) * HEAD_DIM] = mixed[
                h * BLOCK : (h + 1) * BLOCK
            ]


def other_half_kernel(
    own_out, qs, acc_ref, peaks, far_k, far_v, bias_ref, out, max_ref, pbuf, half_out, own_sem, out_sem
):
    nb = qs.shape[0]
    tokens, qw = own_out.shape
    wide = qw // 2
    c = lax.rem(lax.axis_index("inner"), 2)

    def half(pair):
        own_cols = pl.ds((1 - pair) * wide, wide)
        cols = pl.ds(pair * wide, wide)
        own_copy = pltpu.make_async_copy(own_out.at[:, own_cols], out.at[:, own_cols], own_sem)
        own_copy.start()
        for b in range(nb):
            distant_keys(qs, peaks, max_ref, pbuf, far_k, bias_ref, pair, b)
        copies = []
        for b in range(nb):
            rows = pl.ds(b * BLOCK, BLOCK)
            distant_values(acc_ref, max_ref, pbuf, far_v, pair, b, half_out, 0)
            copies.append(
                pltpu.make_async_copy(half_out.at[rows], out.at[rows, cols], out_sem.at[b])
            )
            copies[-1].start()
        for copy in copies:
            copy.wait()
        own_copy.wait()

    pl.when(c == 0)(lambda: half(1))
    pl.when(c == 1)(lambda: half(0))


def paired_kernel(
    list_hbm, q_hbm, k_hbm, v_hbm, qt_hbm, kt_hbm, vt_hbm,
    outb, qs, acc_ref, max_ref, far_k, far_v, bias_ref,
    list_ref, qt_ref, kt_ref, vt_ref, qpad, kvpad, kvc, pbuf,
    flag_out, flag_in, chip, cand, rrow, rother, site, zfar,
    in_sem, own_sem, fl_s, fl_r, raw_s, raw_r, rim_s, rim_r, tail_s, tail_r,
    a_s, a_r, b_s, b_r, c_s, c_r, d_s, d_r, e_s, e_r, ready,
):
    tokens, qw = q_hbm.shape
    kvw = k_hbm.shape[1]
    groups = kvw // HEAD_DIM
    hw = kvw // 2
    quarter = hw // 2
    per_group = qw // kvw
    nb = tokens // BLOCK
    before = BLOCK + HALO
    entries = list_ref.shape[1]
    o = lax.axis_index("outer")
    i = lax.axis_index("inner")
    y = i // 2
    c = lax.rem(i, 2)
    m = o * 2 + y
    no = ROWS
    last_chip = no * 2 - 1
    d = o * 4 + i
    has_next = d < 4 * no - 1
    has_prev = d > 0
    chip_next = m < last_chip
    chip_prev = m > 0
    first_core = c == 0
    second_core = c == 1

    def chip_core(step, core):
        other = m + step
        return {"outer": other // 2, "inner": lax.rem(other, 2) * 2 + core}

    def at(row, col):
        return {"outer": row, "inner": col * 2 + c}

    peer_core = {"inner": i + 1 - 2 * c}
    peer_y = {"inner": lax.rem(i + 2, 4)}
    next_device = {"outer": (d + 1) // 4, "inner": lax.rem(d + 1, 4)}

    barrier = pltpu.get_barrier_semaphore()

    def greet(device):
        pl.semaphore_signal(barrier, inc=1, device_id=device, device_id_type=MESH)

    def call(device):
        pl.semaphore_signal(ready, inc=1, device_id=device, device_id_type=MESH)

    loads = [
        pltpu.make_async_copy(q_hbm, qpad.at[pl.ds(HALO, tokens)], in_sem.at[0]),
        pltpu.make_async_copy(k_hbm, kvpad.at[0, pl.ds(before, tokens)], in_sem.at[1]),
        pltpu.make_async_copy(v_hbm, kvpad.at[1, pl.ds(before, tokens)], in_sem.at[2]),
        pltpu.make_async_copy(list_hbm, list_ref, in_sem.at[3]),
        pltpu.make_async_copy(qt_hbm, qt_ref, in_sem.at[4]),
        pltpu.make_async_copy(kt_hbm, kt_ref, in_sem.at[5]),
        pltpu.make_async_copy(vt_hbm, vt_ref, in_sem.at[6]),
    ]
    half_cols = pl.ds(pl.multiple_of(c * hw, hw), hw)
    peer_cols = pl.ds(pl.multiple_of((1 - c) * hw, hw), hw)
    chip_rows = pl.ds(pl.multiple_of(HALO + c * tokens, HALO), tokens)
    own = [
        pltpu.make_async_copy(x.at[:, half_cols], chip.at[h, chip_rows], own_sem.at[h])
        for h, x in enumerate((k_hbm, v_hbm))
    ]
    loads[3].start()
    greet(peer_core)
    greet(peer_y)

    late_next = (y == 1) & functools.reduce(
        jnp.logical_or, [o == row for row in range(no - 1) if (row, row + 1) in LATE], o < 0
    )
    late_prev = (y == 0) & functools.reduce(
        jnp.logical_or, [o == row + 1 for row in range(no - 1) if (row, row + 1) in LATE], o < 0
    )

    @pl.when(chip_next)
    def _():
        greet(chip_core(1, 0))
        pl.when(second_core & late_next)(lambda: greet(chip_core(1, 1)))

    pl.when(chip_prev & jnp.logical_not(late_prev))(lambda: greet(chip_core(-1, 1)))
    for row in range(no):

        @pl.when(o == row)
        def _():
            for other in origins(row, False) + dests(row, True):
                greet(at(other, 0))
                greet(at(other, 1))

    for n in (1, 5, 2, 6):
        loads[n].start()
    for copy in own:
        copy.start()
    for n in (0, 4):
        loads[n].start()

    def remote(src, dst, send, recv, device):
        return pltpu.make_async_remote_copy(
            src, dst, send, recv, device_id=device, device_id_type=MESH
        )

    flag_back = [
        remote(flag_out, flag_in.at[0], fl_s.at[k], fl_r.at[0], chip_core(-1, k)) for k in range(2)
    ]
    flag_peer = remote(flag_out, flag_in.at[1], fl_s.at[2], fl_r.at[1], peer_core)
    raws = [
        remote(x.at[:, peer_cols], chip.at[h, chip_rows], raw_s.at[h], raw_r.at[h], peer_core)
        for h, x in enumerate((k_hbm, v_hbm))
    ]
    rim = pl.ds(tokens - HALO, HALO)
    rims = [
        [
            remote(
                x.at[rim, k * hw : (k + 1) * hw],
                chip.at[h, pl.ds(0, HALO)],
                rim_s.at[k, h],
                rim_r.at[h],
                chip_core(1, k),
            )
            for h, x in enumerate((k_hbm, v_hbm))
        ]
        for k in range(2)
    ]
    body_rows = pl.ds(tokens - before, BLOCK)

    def to_next(n, src, dst):
        return remote(src, dst, tail_s.at[n], tail_r.at[n], next_device)

    edges = [
        to_next(h, x.at[rim], kvpad.at[h, pl.ds(BLOCK, HALO)]) for h, x in enumerate((k_hbm, v_hbm))
    ]
    tails = [
        to_next(2 + h, x.at[body_rows], kvpad.at[h, pl.ds(0, BLOCK)])
        for h, x in enumerate((k_hbm, v_hbm))
    ] + [to_next(4, q_hbm.at[rim], qpad.at[pl.ds(0, HALO)])]

    @pl.when(jnp.logical_not(has_prev))
    def _():
        qpad[0:HALO, :] = jnp.zeros((HALO, qw), jnp.bfloat16)
        kvpad[:, 0:before, :] = jnp.zeros((2, before, kvw), jnp.bfloat16)

    @pl.when(jnp.logical_not(chip_prev))
    def _():
        chip[:, 0:HALO, :] = jnp.zeros((2, HALO, hw), jnp.bfloat16)

    far_k[...] = jnp.zeros(far_k.shape, jnp.bfloat16)

    @pl.when(jnp.logical_not(chip_next))
    def _():
        flag_in[0] = jnp.full(flag_in.shape[1:], -1, jnp.int32)

    @pl.when(second_core)
    def _():
        flag_in[1] = jnp.full(flag_in.shape[1:], -1, jnp.int32)

    expected = 2 + jnp.where(chip_prev & first_core, 2, 0)
    expected = expected + jnp.where(chip_prev & late_prev & second_core, 1, 0)
    sends_on = second_core & chip_next
    expected = expected + jnp.where(sends_on & jnp.logical_not(late_next), 2, 0)
    awaited = jnp.where(sends_on & late_next, 2, 0)
    for row in range(no):
        met = 2 * len(dests(row, False) + origins(row, True))
        expected = expected + jnp.where(o == row, met, 0)
        awaited = awaited + jnp.where(o == row, 2 * len(dests(row, True)), 0)
    pl.semaphore_wait(barrier, expected)
    pl.when(chip_prev & late_prev)(lambda: call(chip_core(-1, 1)))
    for row in range(no):
        if origins(row, True):

            @pl.when(o == row)
            def _():
                for src in origins(row, True):
                    call(at(src, 0))
                    call(at(src, 1))

    for copy in raws:
        copy.start()

    loads[3].wait()
    phase = jnp.int32(-1)
    for b in range(nb):
        for e in range(entries):
            entry = list_ref[b, e]
            distant = (entry >= 0) & (entry <= d * nb + b - LOCAL)
            phase = jnp.maximum(phase, jnp.where(distant, lax.rem(entry, STRIDE), -1))
    flag_out[...] = jnp.full(flag_out.shape, phase, jnp.int32)

    @pl.when(first_core & chip_prev)
    def _():
        for copy in flag_back:
            copy.start()

    pl.when(second_core)(flag_peer.start)
    def next_sends():
        @pl.when(sends_on)
        def _():
            for h in range(2):
                for k in range(2):
                    rims[k][h].start()

        @pl.when(has_next)
        def _():
            for copy in edges:
                copy.start()

    def tail_sends():
        @pl.when(has_next)
        def _():
            for copy in tails:
                copy.start()

    held_back = sends_on & late_next
    pl.when(jnp.logical_not(held_back))(next_sends)
    if not LATE_TAILS:
        pl.when(jnp.logical_not(held_back))(tail_sends)

    def kv_conv(b):
        rows = slice(b * BLOCK, b * BLOCK + before)
        dst = slice(b * BLOCK, (b + 1) * BLOCK)
        kvc[0, dst, :] = conv(kvpad[0, rows, :], kt_ref[...])
        kvc[1, dst, :] = conv(kvpad[1, rows, :], vt_ref[...])

    def cols_of(col):
        return slice(col * quarter, (col + 1) * quarter)

    def to_peer_site(h):
        return remote(cand.at[h, 1 - y], rrow.at[h], a_s.at[h], a_r.at[h], peer_y)

    def to_site(h, row, col):
        return remote(
            cand.at[h, col], rother.at[h, o, y], b_s.at[h, row, col], b_r.at[h, o, y], at(row, col)
        )

    def at_site(h, src, col):
        return remote(
            cand.at[h, col], rother.at[h, src, col], b_s.at[h, 0, col], b_r.at[h, src, col], peer_y
        )

    def to_peer_col(h):
        return remote(site.at[h, y], site.at[h, y], c_s.at[h], c_r.at[h], peer_y)

    def from_peer_col(h):
        return remote(site.at[h, 1 - y], site.at[h, 1 - y], c_s.at[h], c_r.at[h], peer_y)

    def to_later(h, row, col):
        return remote(
            site.at[h, y], zfar.at[h, o, y], d_s.at[h, row, col], d_r.at[h, o, y], at(row, col)
        )

    def from_earlier(h, src, col):
        return remote(
            site.at[h, y], zfar.at[h, src, col], d_s.at[h, 0, 0], d_r.at[h, src, col], peer_y
        )

    def core_swap(h, core):
        if h == 0:
            part = far_k.at[core]
        else:
            part = far_v.at[pl.ds(2 * core, 2)]
        return remote(part, part, e_s.at[h], e_r.at[h], peer_core)

    def to_peer_core(h):
        return core_swap(h, c)

    def from_peer_core(h):
        return core_swap(h, 1 - c)

    def sums_own(h):
        return functools.reduce(jnp.logical_and, [o != row for row in TAKEN[h]], o >= 0)

    def candidate_step():
        pl.when(awaited > 0)(lambda: pl.semaphore_wait(ready, awaited))
        pl.when(held_back)(next_sends)

        @pl.when(chip_next)
        def _():
            remote(flag_out, flag_in.at[0], fl_s.at[0], fl_r.at[0], peer_core).wait_recv()

        @pl.when(first_core)
        def _():
            flag_peer.wait_recv()

        known = jnp.maximum(jnp.maximum(flag_in[0, 0:1, :], flag_in[1, 0:1, :]), phase)
        first = m * 2 * nb
        weights = [
            jnp.where(known == first + b, 1.0, 0.0).astype(jnp.bfloat16) for b in range(2 * nb)
        ]
        for h, taps in enumerate((kt_ref, vt_ref)):
            own[h].wait()
            raws[h].wait_recv()

            @pl.when(chip_prev)
            def _():
                rims[0][h].wait_recv()

            raw = weights[0] * chip[h, 0:before, :]
            for b in range(1, 2 * nb):
                raw = raw + weights[b] * chip[h, b * BLOCK : b * BLOCK + before, :]
            total = conv(raw, taps[:, half_cols])
            for col in range(2):
                cand[h, col] = total[:, cols_of(col)]

            for src, rows in SUMS[h].items():

                @pl.when(o == src)
                def _():
                    for row in rows:
                        for col in range(2):
                            to_site(h, row, col).start()

            pl.when(sums_own(h))(to_peer_site(h).start)

        if LATE_TAILS:
            tail_sends()
        else:
            pl.when(held_back)(tail_sends)

    def site_step(h):
        pl.when(sums_own(h))(functools.partial(own_site_step, h))

    def own_site_step(h):
        to_peer_site(h).wait_recv()
        site[h, y] = cand[h, y] + rrow[h]
        for row in range(no):
            sources = [src for src, rows in SUMS[h].items() if row in rows]
            if sources:

                @pl.when(o == row)
                def _():
                    for src in sources:
                        for col in range(2):
                            at_site(h, src, col).wait_recv()
                            site[h, y] = site[h, y] + rother[h, src, col]

        for src, rows in SPREADS[h].items():

            @pl.when(o == src)
            def _():
                for row in rows:
                    for col in range(2):
                        to_later(h, row, col).start()

        to_peer_col(h).start()

    def final_step(h):
        pl.when(sums_own(h))(from_peer_col(h).wait_recv)
        for src, rows in SPREADS[h].items():
            for row in rows:

                @pl.when(o == row)
                def _():
                    for col in range(2):
                        from_earlier(h, src, col).wait_recv()
                        if row in TAKEN[h]:
                            zfar[h, o, col] = zfar[h, src, col]
                        else:
                            zfar[h, o, col] = zfar[h, src, col] + site[h, col]

        gets = functools.reduce(
            jnp.logical_or, [o == row for rows in SPREADS[h].values() for row in rows]
        )

        def place(source):
            for col in range(2):
                if h == 0:
                    far_k[c, cols_of(col), cols_of(col)] = source(col)
                else:
                    far_v[2 * c + col] = source(col)

        pl.when(gets)(lambda: place(lambda col: zfar[h, o, col]))
        pl.when(jnp.logical_not(gets))(lambda: place(lambda col: site[h, col]))
        to_peer_core(h).start()

    for n in (1, 5, 2, 6):
        loads[n].wait()
    for b in range(2, nb + 1):
        kv_conv(b)
    loads[0].wait()
    loads[4].wait()

    row_ids = lax.broadcasted_iota(jnp.int32, (BLOCK, BLOCK), 0)
    col_ids = lax.broadcasted_iota(jnp.int32, (BLOCK, BLOCK), 1)
    causal = jnp.concatenate([row_ids >= col_ids] * per_group, 0)
    ones = jnp.ones((LOCAL * BLOCK, HEAD_DIM), jnp.bfloat16)

    def near(step, carry):
        b = jnp.where(step < nb - 2, step + 2, nb - 1 - step)

        @pl.when(b == 1)
        def _():
            @pl.when(has_prev)
            def _():
                for copy in edges:
                    copy.wait_recv()

            kv_conv(1)

        @pl.when(b == 0)
        def _():
            @pl.when(has_prev)
            def _():
                for copy in tails:
                    copy.wait_recv()

            kv_conv(0)

        bias = jnp.where((b == 0) & (d == 0), NEG, 0.0)
        base = pl.multiple_of(b * BLOCK, BLOCK)
        for g in range(groups):
            wide = slice(g * per_group * HEAD_DIM, (g + 1) * per_group * HEAD_DIM)
            cols = slice(g * HEAD_DIM, (g + 1) * HEAD_DIM)
            q = conv(qpad[pl.ds(base, BLOCK + HALO), wide], qt_ref[:, wide])
            q = jnp.concatenate(
                [q[:, h * HEAD_DIM : (h + 1) * HEAD_DIM] for h in range(per_group)], 0
            )
            qs[b, g // 2, :, cols_of(g % 2)] = q
            k = kvc[0, pl.ds(base, LOCAL * BLOCK), cols]
            v = kvc[1, pl.ds(base, LOCAL * BLOCK), cols]
            s = lax.dot_general(q, k, NT, preferred_element_type=jnp.float32)
            prev = s[:, :BLOCK] + bias
            mine = jnp.where(causal, s[:, BLOCK:], NEG)
            peak = jnp.max(jnp.maximum(prev, mine), axis=1, keepdims=True)
            p = jnp.concatenate(
                [jnp.exp2((prev - peak) * SCALE), jnp.exp2((mine - peak) * SCALE)], 1
            ).astype(jnp.bfloat16)
            acc_ref[b, g] = jnp.dot(
                p, jnp.concatenate([v, ones], 1), preferred_element_type=jnp.float32
            )
            max_ref[b, g] = jnp.broadcast_to(peak, (per_group * BLOCK, HEAD_DIM))

        pl.when(step == jnp.where(o == 0, FIRST_ROW_STEP, 0))(candidate_step)
        for h in range(2):
            if SITE_AFTER[h] is not None:
                pl.when(step == SITE_AFTER[h])(functools.partial(site_step, h))
        return carry

    lax.fori_loop(0, nb, near, 0)
    for h in range(2):
        if SITE_AFTER[h] is None:
            site_step(h)
    final_step(0)

    for b in range(nb):
        seen = jnp.int32(0)
        for e in range(entries):
            entry = list_ref[b, e]
            seen = jnp.where((entry >= 0) & (entry <= d * nb + b - LOCAL), 1, seen)
        bias_ref[b : b + 1, :] = jnp.full((1, 128), jnp.where(seen > 0, 0.0, NEG), jnp.float32)
    if nb < bias_ref.shape[0]:
        bias_ref[nb:, :] = jnp.zeros((bias_ref.shape[0] - nb, 128), jnp.float32)

    def far_stage(pair):
        for b in range(nb):
            distant_keys(qs, max_ref, max_ref, pbuf, far_k, bias_ref, pair, b)
        for b in range(nb):
            distant_values(acc_ref, max_ref, pbuf, far_v, pair, b, outb, 2 * pair * per_group)

    final_step(1)
    pl.when(first_core)(functools.partial(far_stage, 0))
    pl.when(second_core)(functools.partial(far_stage, 1))
    for h in range(2):
        from_peer_core(h).wait_recv()

    @pl.when(first_core & chip_prev)
    def _():
        for copy in flag_back:
            copy.wait_send()

    @pl.when(second_core)
    def _():
        flag_peer.wait_send()

        @pl.when(chip_next)
        def _():
            for k in range(2):
                for copy in rims[k]:
                    copy.wait_send()

    @pl.when(has_next)
    def _():
        for copy in edges + tails:
            copy.wait_send()

    for h in range(2):
        raws[h].wait_send()

        @pl.when(sums_own(h))
        def _():
            to_peer_site(h).wait_send()
            to_peer_col(h).wait_send()

        to_peer_core(h).wait_send()

        for table, copy in ((SUMS, to_site), (SPREADS, to_later)):
            for src, rows in table[h].items():

                @pl.when(o == src)
                def _():
                    for row in rows:
                        for col in range(2):
                            copy(h, row, col).wait_send()


def paired_call(arrays):
    block_list, q_proj, k_proj = arrays[:3]
    q_taps, k_taps, v_taps = arrays[4:]
    tokens, qw = q_proj.shape
    kvw = k_proj.shape[1]
    nb = tokens // BLOCK
    groups = kvw // HEAD_DIM
    rows = qw // kvw * BLOCK
    hw = kvw // 2
    piece = (BLOCK, hw // 2)
    dma = pltpu.SemaphoreType.DMA
    bf16, f32 = jnp.bfloat16, jnp.float32
    hbm_spec = pl.BlockSpec(memory_space=pltpu.HBM)
    scores = nb * groups * rows * (LOCAL + 1) * BLOCK
    vmem_spec = pl.BlockSpec(memory_space=pltpu.VMEM)
    partial_shapes = [
        ((tokens, qw), bf16),
        ((nb, groups // 2, rows, 2 * HEAD_DIM), bf16),
        ((nb, groups, rows, 2 * HEAD_DIM), f32),
        ((nb, groups, rows, HEAD_DIM), f32),
        ((groups // 2, 2 * BLOCK, hw), bf16),
        ((groups, BLOCK, HEAD_DIM), bf16),
        ((max(8, nb), 128), f32),
    ]
    partial = pl.pallas_call(
        paired_kernel,
        out_shape=[jax.ShapeDtypeStruct(*x) for x in partial_shapes],
        in_specs=[hbm_spec] * 7,
        out_specs=[vmem_spec] * 7,
        scratch_shapes=[
            pltpu.SMEM(block_list.shape, jnp.int32),
            pltpu.VMEM(q_taps.shape, f32),
            pltpu.VMEM(k_taps.shape, f32),
            pltpu.VMEM(v_taps.shape, f32),
            pltpu.VMEM((tokens + HALO, qw), bf16),
            pltpu.VMEM((2, tokens + BLOCK + HALO, kvw), bf16),
            pltpu.VMEM((2, tokens + BLOCK, kvw), bf16),
            pltpu.VMEM((nb, groups, rows, BLOCK), bf16),
            pltpu.VMEM((8, hw), jnp.int32),
            pltpu.VMEM((2, 8, hw), jnp.int32),
            pltpu.VMEM((2, 2 * tokens + HALO, hw), bf16),
            pltpu.VMEM((2, 2, *piece), bf16),
            pltpu.VMEM((2, *piece), bf16),
            pltpu.VMEM((2, ROWS, 2, *piece), bf16),
            pltpu.VMEM((2, 2, *piece), bf16),
            pltpu.VMEM((2, ROWS, 2, *piece), bf16),
            dma((7,)),
            dma((2,)),
            dma((3,)),
            dma((2,)),
            dma((2,)),
            dma((2,)),
            dma((2, 2)),
            dma((2,)),
            dma((5,)),
            dma((5,)),
            dma((2,)),
            dma((2,)),
            dma((2, ROWS, 2)),
            dma((2, ROWS, 2)),
            dma((2,)),
            dma((2,)),
            dma((2, ROWS, 2)),
            dma((2, ROWS, 2)),
            dma((2,)),
            dma((2,)),
            pltpu.SemaphoreType.REGULAR,
        ],
        compiler_params=pltpu.CompilerParams(
            collective_id=0, has_side_effects=True, vmem_limit_bytes=36 * 1024 * 1024
        ),
        cost_estimate=pl.CostEstimate(
            flops=4 * scores * HEAD_DIM,
            bytes_accessed=4 * tokens * qw + 4 * tokens * kvw,
            transcendentals=scores,
        ),
    )(*arrays)
    return pl.pallas_call(
        other_half_kernel,
        out_shape=jax.ShapeDtypeStruct((tokens, qw), bf16),
        in_specs=[vmem_spec] * 7,
        out_specs=hbm_spec,
        scratch_shapes=[
            pltpu.VMEM((nb, groups, rows, HEAD_DIM), f32),
            pltpu.VMEM((nb, groups, rows, BLOCK), bf16),
            pltpu.VMEM((tokens, qw // 2), bf16),
            dma,
            dma((nb,)),
        ],
        compiler_params=pltpu.CompilerParams(vmem_limit_bytes=36 * 1024 * 1024),
        cost_estimate=pl.CostEstimate(
            flops=scores * HEAD_DIM, bytes_accessed=2 * tokens * qw, transcendentals=scores // 6
        ),
    )(*partial)


def body(q_proj, k_proj, v_proj, q_taps, k_taps, v_taps, block_list):
    tokens, qw = q_proj.shape
    kvw = k_proj.shape[1]
    ni = lax.axis_size("inner")
    no = lax.axis_size("outer")
    nb = tokens // BLOCK
    groups = kvw // HEAD_DIM
    rows = qw // kvw * BLOCK
    slots = max(1, nb * ni * no // STRIDE)
    piece_rows = max(HALO, BLOCK // ni)
    piece_cols = BLOCK * kvw // (ni * piece_rows)
    piece = (piece_rows, piece_cols)
    dma = pltpu.SemaphoreType.DMA
    bf16, f32 = jnp.bfloat16, jnp.float32
    hbm_spec = pl.BlockSpec(memory_space=pltpu.HBM)
    scores = nb * groups * rows * (LOCAL + slots) * BLOCK
    arrays = [
        pltpu.with_memory_space_constraint(x, pltpu.HBM)
        for x in (block_list, q_proj, k_proj, v_proj, q_taps, k_taps, v_taps)
    ]
    paired = ni == 4 and no == ROWS and nb * ni * no == STRIDE and groups == 4 and nb >= 2
    if paired:
        return paired_call(arrays)
    return pl.pallas_call(
        functools.partial(kernel, ni, no),
        out_shape=jax.ShapeDtypeStruct((tokens, qw), bf16),
        in_specs=[hbm_spec] * 7,
        out_specs=pl.BlockSpec(memory_space=pltpu.VMEM),
        scratch_shapes=[
            pltpu.SMEM(block_list.shape, jnp.int32),
            pltpu.VMEM(q_taps.shape, f32),
            pltpu.VMEM(k_taps.shape, f32),
            pltpu.VMEM(v_taps.shape, f32),
            pltpu.VMEM((tokens + HALO, qw), bf16),
            pltpu.VMEM((2, tokens + BLOCK + HALO, kvw), bf16),
            pltpu.VMEM((2, tokens + BLOCK, kvw), bf16),
            pltpu.VMEM((nb, groups, rows, HEAD_DIM), bf16),
            pltpu.VMEM((nb, groups, rows, 2 * HEAD_DIM), f32),
            pltpu.VMEM((nb, groups, rows, HEAD_DIM), f32),
            pltpu.VMEM((nb, groups, rows, slots * BLOCK), bf16),
            pltpu.VMEM((max(8, nb), 128), f32),
            pltpu.VMEM((max(8, nb), 128), f32),
            pltpu.VMEM((2, BLOCK, kvw), bf16),
            pltpu.VMEM((2, ni, *piece), bf16),
            pltpu.VMEM((2, *piece), bf16),
            pltpu.VMEM((2, no, *piece), bf16),
            pltpu.VMEM((2, slots, *piece), bf16),
            pltpu.VMEM((2, slots, BLOCK, kvw), bf16),
            dma((7,)),
            dma((5,)),
            dma((5,)),
            dma,
            dma,
            dma((2, ni)),
            dma((2, ni)),
            dma((2, no)),
            dma((2, no)),
            dma((2, ni)),
            dma((2, ni)),
        ],
        compiler_params=pltpu.CompilerParams(
            collective_id=0, has_side_effects=True, vmem_limit_bytes=48 * 1024 * 1024
        ),
        cost_estimate=pl.CostEstimate(
            flops=4 * scores * HEAD_DIM,
            bytes_accessed=4 * tokens * qw + 4 * tokens * kvw,
            transcendentals=scores,
        ),
    )(*arrays)


def solution(mesh):
    rows = P(("groups", "outer", "inner"), None)
    return jax.shard_map(
        body,
        mesh=mesh,
        in_specs=(rows, rows, rows, P(), P(), P(), rows),
        out_specs=rows,
        check_vma=False,
    )
```

```python
import functools
import math

import jax
import jax.numpy as jnp
from jax import lax
from jax.experimental import pallas as pl
from jax.experimental.pallas import tpu as pltpu
from jax.sharding import PartitionSpec as P

HEAD_DIM = 128
BLOCK = 128
LOCAL = 2
STRIDE = 64
HALO = 16
NEG = -1e30
MESH = pl.DeviceIdType.MESH
SCALE = math.log2(math.e) / math.sqrt(HEAD_DIM)
NT = (((1,), (1,)), ((), ()))


def conv(padded, taps):
    wide = padded.astype(jnp.float32)
    total = taps[0:1] * wide[HALO:]
    for j in (1, 2):
        total = total + taps[j : j + 1] * pltpu.roll(wide, j, 0)[HALO:]
    return total.astype(jnp.bfloat16)


def kernel(
    ni, no, list_hbm, q_hbm, k_hbm, v_hbm, qt_hbm, kt_hbm, vt_hbm, outb,
    list_ref, qt_ref, kt_ref, vt_ref, qpad, kvpad, kvc, qs, acc_ref, max_ref, pbuf, wout, win, cand, rbuf, zpiece, zbuf,
    fsum, far, in_sem, tail_s, tail_r, w_s, w_r, sc_s, sc_r, z_s, z_r,
    g_s, g_r,
):
    tokens, qw = q_hbm.shape
    kvw = k_hbm.shape[1]
    groups = kvw // HEAD_DIM
    per_group = qw // kvw
    nb = tokens // BLOCK
    slots = far.shape[1]
    piece_rows, piece_cols = zpiece.shape[1:]
    col_parts = kvw // piece_cols
    before = BLOCK + HALO
    entries = list_ref.shape[1]
    o = lax.axis_index("outer")
    i = lax.axis_index("inner")
    d = o * ni + i
    last = ni * no - 1
    has_next = d < last
    has_prev = d > 0

    def chain(step):
        other = d + step
        return {"outer": other // ni, "inner": lax.rem(other, ni)}

    def inner_peer(r):
        return {"inner": lax.rem(i + r, ni)}

    loads = [
        pltpu.make_async_copy(q_hbm, qpad.at[pl.ds(HALO, tokens)], in_sem.at[0]),
        pltpu.make_async_copy(k_hbm, kvpad.at[0, pl.ds(before, tokens)], in_sem.at[1]),
        pltpu.make_async_copy(v_hbm, kvpad.at[1, pl.ds(before, tokens)], in_sem.at[2]),
        pltpu.make_async_copy(list_hbm, list_ref, in_sem.at[3]),
        pltpu.make_async_copy(qt_hbm, qt_ref, in_sem.at[4]),
        pltpu.make_async_copy(kt_hbm, kt_ref, in_sem.at[5]),
        pltpu.make_async_copy(vt_hbm, vt_ref, in_sem.at[6]),
    ]
    for n in (3, 1, 5, 2, 6, 0, 4):
        loads[n].start()

    barrier = pltpu.get_barrier_semaphore()
    for r in range(1, ni):
        pl.semaphore_signal(barrier, inc=1, device_id=inner_peer(r), device_id_type=MESH)
    for r in range(1, no):
        pl.semaphore_signal(
            barrier, inc=1, device_id={"outer": lax.rem(o + r, no)}, device_id_type=MESH
        )

    @pl.when(has_next)
    def _():
        pl.semaphore_signal(barrier, inc=1, device_id=chain(1), device_id_type=MESH)

    @pl.when(has_prev)
    def _():
        pl.semaphore_signal(barrier, inc=1, device_id=chain(-1), device_id_type=MESH)

    loads[3].wait()
    phase = jnp.int32(-1)
    for b in range(nb):
        for e in range(entries):
            entry = list_ref[b, e]
            distant = (entry >= 0) & (entry <= d * nb + b - LOCAL)
            phase = jnp.maximum(phase, jnp.where(distant, lax.rem(entry, STRIDE), -1))
    for b in range(nb):
        hit = lax.rem((d - 1) * nb + b + STRIDE, STRIDE) == phase
        wout[b : b + 1, :] = jnp.full((1, 128), jnp.where(hit, 1.0, 0.0), jnp.float32)
    if nb < wout.shape[0]:
        wout[nb:, :] = jnp.zeros((wout.shape[0] - nb, 128), jnp.float32)

    @pl.when(d == 0)
    def _():
        qpad[0:HALO, :] = jnp.zeros((HALO, qw), jnp.bfloat16)
        kvpad[:, 0:before, :] = jnp.zeros((2, before, kvw), jnp.bfloat16)

    @pl.when(d == last)
    def _():
        win[...] = jnp.zeros(win.shape, jnp.float32)

    fsum[...] = jnp.zeros(fsum.shape, jnp.bfloat16)

    w_copy = pltpu.make_async_remote_copy(
        wout, win, w_s, w_r, device_id=chain(-1), device_id_type=MESH
    )
    rim = pl.ds(tokens - HALO, HALO)
    body_rows = pl.ds(tokens - before, BLOCK)

    def to_next(src, dst, n):
        return pltpu.make_async_remote_copy(
            src, dst, tail_s.at[n], tail_r.at[n], device_id=chain(1), device_id_type=MESH
        )

    tails = [
        to_next(k_hbm.at[rim], kvpad.at[0, pl.ds(BLOCK, HALO)], 0),
        to_next(v_hbm.at[rim], kvpad.at[1, pl.ds(BLOCK, HALO)], 1),
        to_next(k_hbm.at[body_rows], kvpad.at[0, pl.ds(0, BLOCK)], 2),
        to_next(v_hbm.at[body_rows], kvpad.at[1, pl.ds(0, BLOCK)], 3),
        to_next(q_hbm.at[rim], qpad.at[pl.ds(0, HALO)], 4),
    ]

    def first_sends():
        pl.semaphore_wait(
            barrier,
            ni - 1 + no - 1 + jnp.where(has_next, 1, 0) + jnp.where(has_prev, 1, 0),
        )

        @pl.when(has_prev)
        def _():
            w_copy.start()

        @pl.when(has_next)
        def _():
            for copy in tails:
                copy.start()

    def kv_conv(b):
        rows = slice(b * BLOCK, b * BLOCK + before)
        dst = slice(b * BLOCK, (b + 1) * BLOCK)
        kvc[0, dst, :] = conv(kvpad[0, rows, :], kt_ref[...])
        kvc[1, dst, :] = conv(kvpad[1, rows, :], vt_ref[...])

    for n in (1, 5, 2, 6):
        loads[n].wait()
    for b in range(2, nb + 1):
        kv_conv(b)

    def candidate_step():
        @pl.when(has_prev)
        def _():
            tails[0].wait_recv()
            tails[1].wait_recv()

        kv_conv(1)

        @pl.when(has_next)
        def _():
            w_copy.wait_recv()

        for g in range(groups):
            cols = slice(g * HEAD_DIM, (g + 1) * HEAD_DIM)
            for half in range(2):
                total = jnp.zeros((BLOCK, HEAD_DIM), jnp.float32)
                for b in range(nb):
                    own = jnp.where(lax.rem(d * nb + b, STRIDE) == phase, 1.0, 0.0)
                    weight = jnp.maximum(win[b : b + 1, :], own)
                    rows = slice((b + 1) * BLOCK, (b + 2) * BLOCK)
                    total = total + weight * kvc[half, rows, cols].astype(jnp.float32)
                cand[half, :, cols] = total.astype(jnp.bfloat16)

        for half in range(2):
            for r in range(1, ni):
                scatter(half, r).start()

    def part(index):
        row = pl.multiple_of(index // col_parts * piece_rows, piece_rows)
        col = pl.multiple_of(lax.rem(index, col_parts) * piece_cols, piece_cols)
        return pl.ds(row, piece_rows), pl.ds(col, piece_cols)

    def scatter(half, r):
        return pltpu.make_async_remote_copy(
            cand.at[(half, *part(lax.rem(i + r, ni)))],
            rbuf.at[half, r],
            sc_s.at[half, r],
            sc_r.at[half, r],
            device_id=inner_peer(r),
            device_id_type=MESH,
        )

    def column(half, r):
        return pltpu.make_async_remote_copy(
            zpiece.at[half],
            zbuf.at[half, r],
            z_s.at[half, r],
            z_r.at[half, r],
            device_id={"outer": lax.rem(o + r, no)},
            device_id_type=MESH,
        )

    def gather(half, r):
        return pltpu.make_async_remote_copy(
            fsum.at[half],
            far.at[(half, slice(None), *part(i))],
            g_s.at[half, r],
            g_r.at[half, r],
            device_id=inner_peer(r),
            device_id_type=MESH,
        )

    def column_step(half):
        total = cand[(half, *part(i))].astype(jnp.float32)
        for r in range(1, ni):
            scatter(half, r).wait_recv()
            total = total + rbuf[half, r].astype(jnp.float32)
        zpiece[half] = total.astype(jnp.bfloat16)
        for r in range(1, no):
            pl.when(o + r < no)(column(half, r).start)

    def slot_of(row):
        return lax.rem(row * (ni * nb) // STRIDE, slots)

    def gather_step(half):
        fsum[half, slot_of(o)] = zpiece[half]
        for r in range(1, no):

            @pl.when(o >= r)
            def _():
                column(half, r).wait_recv()
                at = slot_of(o - r)
                fsum[half, at] = (
                    fsum[half, at].astype(jnp.float32) + zbuf[half, r].astype(jnp.float32)
                ).astype(jnp.bfloat16)

        for r in range(1, ni):
            gather(half, r).start()
        far[(half, slice(None), *part(i))] = fsum[half]

    def gather_wait(half):
        for r in range(1, ni):
            gather(half, r).wait_recv()

    loads[0].wait()
    loads[4].wait()

    row_ids = lax.broadcasted_iota(jnp.int32, (BLOCK, BLOCK), 0)
    col_ids = lax.broadcasted_iota(jnp.int32, (BLOCK, BLOCK), 1)
    causal = jnp.concatenate([row_ids >= col_ids] * per_group, 0)
    ones = jnp.ones((LOCAL * BLOCK, HEAD_DIM), jnp.bfloat16)

    def near(step, carry):
        b = jnp.where(step < nb - 2, step + 2, nb - 1 - step)

        @pl.when(b == 0)
        def _():
            @pl.when(has_prev)
            def _():
                tails[2].wait_recv()
                tails[3].wait_recv()
                tails[4].wait_recv()

            kv_conv(0)

        bias = jnp.where((b == 0) & (d == 0), NEG, 0.0)
        base = pl.multiple_of(b * BLOCK, BLOCK)
        for g in range(groups):
            wide = slice(g * per_group * HEAD_DIM, (g + 1) * per_group * HEAD_DIM)
            cols = slice(g * HEAD_DIM, (g + 1) * HEAD_DIM)
            q = conv(qpad[pl.ds(base, BLOCK + HALO), wide], qt_ref[:, wide])
            q = jnp.concatenate(
                [q[:, h * HEAD_DIM : (h + 1) * HEAD_DIM] for h in range(per_group)], 0
            )
            qs[b, g] = q
            k = kvc[0, pl.ds(base, LOCAL * BLOCK), cols]
            v = kvc[1, pl.ds(base, LOCAL * BLOCK), cols]
            s = lax.dot_general(q, k, NT, preferred_element_type=jnp.float32)
            prev = s[:, :BLOCK] + bias
            own = jnp.where(causal, s[:, BLOCK:], NEG)
            peak = jnp.max(jnp.maximum(prev, own), axis=1, keepdims=True)
            p = jnp.concatenate(
                [jnp.exp2((prev - peak) * SCALE), jnp.exp2((own - peak) * SCALE)], 1
            ).astype(jnp.bfloat16)
            acc_ref[b, g] = jnp.dot(
                p, jnp.concatenate([v, ones], 1), preferred_element_type=jnp.float32
            )
            max_ref[b, g] = jnp.broadcast_to(peak, (per_group * BLOCK, HEAD_DIM))

        pl.when(step == 0)(first_sends)
        pl.when(step == 1)(candidate_step)

        @pl.when(step == 2)
        def _():
            column_step(0)
            column_step(1)

        return carry

    lax.fori_loop(0, nb, near, 0)
    gather_step(0)
    gather_step(1)
    gather_wait(0)

    def distant_keys(b, carry):
        biases = []
        for n in range(slots):
            seen = jnp.int32(0)
            for e in range(entries):
                entry = list_ref[b, e]
                hit = (entry >= n * STRIDE) & (entry < (n + 1) * STRIDE)
                hit = hit & (entry <= d * nb + b - LOCAL)
                seen = jnp.where(hit, 1, seen)
            biases.append(jnp.where(seen > 0, 0.0, NEG))
        for g in range(groups):
            cols = slice(g * HEAD_DIM, (g + 1) * HEAD_DIM)
            q = qs[b, g]
            near_peak = max_ref[b, g]
            scores = []
            top = None
            for n in range(slots):
                s = lax.dot_general(q, far[0, n, :, cols], NT, preferred_element_type=jnp.float32)
                s = s + biases[n]
                scores.append(s)
                top = s if top is None else jnp.maximum(top, s)
            peak = jnp.maximum(near_peak, jnp.max(top, axis=1, keepdims=True))
            max_ref[b, g] = jnp.exp2((near_peak - peak) * SCALE)
            for n in range(slots):
                p = jnp.exp2((scores[n] - peak) * SCALE)
                pbuf[b, g, :, n * BLOCK : (n + 1) * BLOCK] = p.astype(jnp.bfloat16)
        return carry

    def distant_values(b, carry):
        base = pl.multiple_of(b * BLOCK, BLOCK)
        for g in range(groups):
            cols = slice(g * HEAD_DIM, (g + 1) * HEAD_DIM)
            both = acc_ref[b, g]
            shrink = max_ref[b, g]
            total = both[:, :HEAD_DIM] * shrink
            count = both[:, HEAD_DIM:] * shrink
            for n in range(slots):
                more = jnp.dot(
                    pbuf[b, g, :, n * BLOCK : (n + 1) * BLOCK],
                    jnp.concatenate([far[1, n, :, cols], ones[:BLOCK]], 1),
                    preferred_element_type=jnp.float32,
                )
                total = total + more[:, :HEAD_DIM]
                count = count + more[:, HEAD_DIM:]
            mixed = (total / count).astype(jnp.bfloat16)
            for h in range(per_group):
                head = g * per_group + h
                outb[pl.ds(base, BLOCK), head * HEAD_DIM : (head + 1) * HEAD_DIM] = mixed[
                    h * BLOCK : (h + 1) * BLOCK
                ]
        return carry

    lax.fori_loop(0, nb, distant_keys, 0)
    gather_wait(1)
    lax.fori_loop(0, nb, distant_values, 0)

    @pl.when(has_prev)
    def _():
        w_copy.wait_send()

    @pl.when(has_next)
    def _():
        for copy in tails:
            copy.wait_send()

    for half in range(2):
        for r in range(1, ni):
            scatter(half, r).wait_send()
            gather(half, r).wait_send()
        for r in range(1, no):
            pl.when(o + r < no)(column(half, r).wait_send)


ROWS = 4
SUMS = ({0: (1,), 2: (3,)}, {0: (2,), 1: (2,)})
SPREADS = ({1: (3, 2)}, {2: (3, 1)})
TAKEN = ((), (1,))
FIRST_ROW_STEP = 1
SITE_AFTER = (2, 2)
LATE_TAILS = False
LATE = ((2, 3), (1, 3), (0, 2))


def dests(row, late):
    rows = {r for table in (*SUMS, *SPREADS) for r in table.get(row, ())}
    return sorted(r for r in rows if ((row, r) in LATE) == late)


def origins(row, late):
    return [r for r in range(ROWS) if row in dests(r, late)]


def distant_keys(qs, peaks, max_ref, pbuf, far_k, bias_ref, pair, b):
    both = lax.dot_general(qs[b, pair], far_k[pair], NT, preferred_element_type=jnp.float32)
    bias = bias_ref[b : b + 1, :]
    for n in range(2):
        g = 2 * pair + n
        s = both[:, n * BLOCK : (n + 1) * BLOCK] + bias
        near_peak = peaks[b, g]
        peak = jnp.maximum(near_peak, jnp.max(s, axis=1, keepdims=True))
        max_ref[b, g] = jnp.exp2((near_peak - peak) * SCALE)
        pbuf[b, g] = jnp.exp2((s - peak) * SCALE).astype(jnp.bfloat16)


def distant_values(acc_ref, max_ref, pbuf, far_v, pair, b, dst, first_head):
    per_group = acc_ref.shape[2] // BLOCK
    ones = jnp.ones((BLOCK, HEAD_DIM), jnp.bfloat16)
    for n in range(2):
        g = 2 * pair + n
        shrink = max_ref[b, g]
        more = jnp.dot(
            pbuf[b, g],
            jnp.concatenate([far_v[g], ones], 1),
            preferred_element_type=jnp.float32,
        )
        total = acc_ref[b, g, :, :HEAD_DIM] * shrink + more[:, :HEAD_DIM]
        count = acc_ref[b, g, :, HEAD_DIM:] * shrink + more[:, HEAD_DIM:]
        inverse = pl.reciprocal(count, approx=True)
        inverse = inverse * (2.0 - count * inverse)
        mixed = (total * inverse).astype(jnp.bfloat16)
        for h in range(per_group):
            head = first_head + n * per_group + h
            dst[b * BLOCK : (b + 1) * BLOCK, head * HEAD_DIM : (head + 1) * HEAD_DIM] = mixed[
                h * BLOCK : (h + 1) * BLOCK
            ]


def other_half_kernel(
    own_out, qs, acc_ref, peaks, far_k, far_v, bias_ref, out, max_ref, pbuf, half_out, own_sem, out_sem
):
    nb = qs.shape[0]
    tokens, qw = own_out.shape
    wide = qw // 2
    c = lax.rem(lax.axis_index("inner"), 2)

    def half(pair):
        own_cols = pl.ds((1 - pair) * wide, wide)
        cols = pl.ds(pair * wide, wide)
        own_copy = pltpu.make_async_copy(own_out.at[:, own_cols], out.at[:, own_cols], own_sem)
        own_copy.start()
        for b in range(nb):
            distant_keys(qs, peaks, max_ref, pbuf, far_k, bias_ref, pair, b)
        copies = []
        for b in range(nb):
            rows = pl.ds(b * BLOCK, BLOCK)
            distant_values(acc_ref, max_ref, pbuf, far_v, pair, b, half_out, 0)
            copies.append(
                pltpu.make_async_copy(half_out.at[rows], out.at[rows, cols], out_sem.at[b])
            )
            copies[-1].start()
        for copy in copies:
            copy.wait()
        own_copy.wait()

    pl.when(c == 0)(lambda: half(1))
    pl.when(c == 1)(lambda: half(0))


def paired_kernel(
    list_hbm, q_hbm, k_hbm, v_hbm, qt_hbm, kt_hbm, vt_hbm,
    outb, qs, acc_ref, max_ref, far_k, far_v, bias_ref,
    list_ref, qt_ref, kt_ref, vt_ref, qpad, kvpad, kvc, pbuf,
    flag_out, flag_in, chip, cand, rrow, rother, site, zfar,
    in_sem, own_sem, fl_s, fl_r, raw_s, raw_r, rim_s, rim_r, tail_s, tail_r,
    a_s, a_r, b_s, b_r, c_s, c_r, d_s, d_r, e_s, e_r, ready,
):
    tokens, qw = q_hbm.shape
    kvw = k_hbm.shape[1]
    groups = kvw // HEAD_DIM
    hw = kvw // 2
    quarter = hw // 2
    per_group = qw // kvw
    nb = tokens // BLOCK
    before = BLOCK + HALO
    entries = list_ref.shape[1]
    o = lax.axis_index("outer")
    i = lax.axis_index("inner")
    y = i // 2
    c = lax.rem(i, 2)
    m = o * 2 + y
    no = ROWS
    last_chip = no * 2 - 1
    d = o * 4 + i
    has_next = d < 4 * no - 1
    has_prev = d > 0
    chip_next = m < last_chip
    chip_prev = m > 0
    first_core = c == 0
    second_core = c == 1

    def chip_core(step, core):
        other = m + step
        return {"outer": other // 2, "inner": lax.rem(other, 2) * 2 + core}

    def at(row, col):
        return {"outer": row, "inner": col * 2 + c}

    peer_core = {"inner": i + 1 - 2 * c}
    peer_y = {"inner": lax.rem(i + 2, 4)}
    next_device = {"outer": (d + 1) // 4, "inner": lax.rem(d + 1, 4)}

    barrier = pltpu.get_barrier_semaphore()

    def greet(device):
        pl.semaphore_signal(barrier, inc=1, device_id=device, device_id_type=MESH)

    def call(device):
        pl.semaphore_signal(ready, inc=1, device_id=device, device_id_type=MESH)

    loads = [
        pltpu.make_async_copy(q_hbm, qpad.at[pl.ds(HALO, tokens)], in_sem.at[0]),
        pltpu.make_async_copy(k_hbm, kvpad.at[0, pl.ds(before, tokens)], in_sem.at[1]),
        pltpu.make_async_copy(v_hbm, kvpad.at[1, pl.ds(before, tokens)], in_sem.at[2]),
        pltpu.make_async_copy(list_hbm, list_ref, in_sem.at[3]),
        pltpu.make_async_copy(qt_hbm, qt_ref, in_sem.at[4]),
        pltpu.make_async_copy(kt_hbm, kt_ref, in_sem.at[5]),
        pltpu.make_async_copy(vt_hbm, vt_ref, in_sem.at[6]),
    ]
    half_cols = pl.ds(pl.multiple_of(c * hw, hw), hw)
    peer_cols = pl.ds(pl.multiple_of((1 - c) * hw, hw), hw)
    chip_rows = pl.ds(pl.multiple_of(HALO + c * tokens, HALO), tokens)
    own = [
        pltpu.make_async_copy(x.at[:, half_cols], chip.at[h, chip_rows], own_sem.at[h])
        for h, x in enumerate((k_hbm, v_hbm))
    ]
    loads[3].start()
    greet(peer_core)
    greet(peer_y)

    late_next = (y == 1) & functools.reduce(
        jnp.logical_or, [o == row for row in range(no - 1) if (row, row + 1) in LATE], o < 0
    )
    late_prev = (y == 0) & functools.reduce(
        jnp.logical_or, [o == row + 1 for row in range(no - 1) if (row, row + 1) in LATE], o < 0
    )

    @pl.when(chip_next)
    def _():
        greet(chip_core(1, 0))
        pl.when(second_core & late_next)(lambda: greet(chip_core(1, 1)))

    pl.when(chip_prev & jnp.logical_not(late_prev))(lambda: greet(chip_core(-1, 1)))
    for row in range(no):

        @pl.when(o == row)
        def _():
            for other in origins(row, False) + dests(row, True):
                greet(at(other, 0))
                greet(at(other, 1))

    for n in (1, 5, 2, 6):
        loads[n].start()
    for copy in own:
        copy.start()
    for n in (0, 4):
        loads[n].start()

    def remote(src, dst, send, recv, device):
        return pltpu.make_async_remote_copy(
            src, dst, send, recv, device_id=device, device_id_type=MESH
        )

    flag_back = [
        remote(flag_out, flag_in.at[0], fl_s.at[k], fl_r.at[0], chip_core(-1, k)) for k in range(2)
    ]
    flag_peer = remote(flag_out, flag_in.at[1], fl_s.at[2], fl_r.at[1], peer_core)
    raws = [
        remote(x.at[:, peer_cols], chip.at[h, chip_rows], raw_s.at[h], raw_r.at[h], peer_core)
        for h, x in enumerate((k_hbm, v_hbm))
    ]
    rim = pl.ds(tokens - HALO, HALO)
    rims = [
        [
            remote(
                x.at[rim, k * hw : (k + 1) * hw],
                chip.at[h, pl.ds(0, HALO)],
                rim_s.at[k, h],
                rim_r.at[h],
                chip_core(1, k),
            )
            for h, x in enumerate((k_hbm, v_hbm))
        ]
        for k in range(2)
    ]
    body_rows = pl.ds(tokens - before, BLOCK)

    def to_next(n, src, dst):
        return remote(src, dst, tail_s.at[n], tail_r.at[n], next_device)

    edges = [
        to_next(h, x.at[rim], kvpad.at[h, pl.ds(BLOCK, HALO)]) for h, x in enumerate((k_hbm, v_hbm))
    ]
    tails = [
        to_next(2 + h, x.at[body_rows], kvpad.at[h, pl.ds(0, BLOCK)])
        for h, x in enumerate((k_hbm, v_hbm))
    ] + [to_next(4, q_hbm.at[rim], qpad.at[pl.ds(0, HALO)])]

    @pl.when(jnp.logical_not(has_prev))
    def _():
        qpad[0:HALO, :] = jnp.zeros((HALO, qw), jnp.bfloat16)
        kvpad[:, 0:before, :] = jnp.zeros((2, before, kvw), jnp.bfloat16)

    @pl.when(jnp.logical_not(chip_prev))
    def _():
        chip[:, 0:HALO, :] = jnp.zeros((2, HALO, hw), jnp.bfloat16)

    far_k[...] = jnp.zeros(far_k.shape, jnp.bfloat16)

    @pl.when(jnp.logical_not(chip_next))
    def _():
        flag_in[0] = jnp.full(flag_in.shape[1:], -1, jnp.int32)

    @pl.when(second_core)
    def _():
        flag_in[1] = jnp.full(flag_in.shape[1:], -1, jnp.int32)

    expected = 2 + jnp.where(chip_prev & first_core, 2, 0)
    expected = expected + jnp.where(chip_prev & late_prev & second_core, 1, 0)
    sends_on = second_core & chip_next
    expected = expected + jnp.where(sends_on & jnp.logical_not(late_next), 2, 0)
    awaited = jnp.where(sends_on & late_next, 2, 0)
    for row in range(no):
        met = 2 * len(dests(row, False) + origins(row, True))
        expected = expected + jnp.where(o == row, met, 0)
        awaited = awaited + jnp.where(o == row, 2 * len(dests(row, True)), 0)
    pl.semaphore_wait(barrier, expected)
    pl.when(chip_prev & late_prev)(lambda: call(chip_core(-1, 1)))
    for row in range(no):
        if origins(row, True):

            @pl.when(o == row)
            def _():
                for src in origins(row, True):
                    call(at(src, 0))
                    call(at(src, 1))

    for copy in raws:
        copy.start()

    loads[3].wait()
    phase = jnp.int32(-1)
    for b in range(nb):
        for e in range(entries):
            entry = list_ref[b, e]
            distant = (entry >= 0) & (entry <= d * nb + b - LOCAL)
            phase = jnp.maximum(phase, jnp.where(distant, lax.rem(entry, STRIDE), -1))
    flag_out[...] = jnp.full(flag_out.shape, phase, jnp.int32)

    @pl.when(first_core & chip_prev)
    def _():
        for copy in flag_back:
            copy.start()

    pl.when(second_core)(flag_peer.start)
    def next_sends():
        @pl.when(sends_on)
        def _():
            for h in range(2):
                for k in range(2):
                    rims[k][h].start()

        @pl.when(has_next)
        def _():
            for copy in edges:
                copy.start()

    def tail_sends():
        @pl.when(has_next)
        def _():
            for copy in tails:
                copy.start()

    held_back = sends_on & late_next
    pl.when(jnp.logical_not(held_back))(next_sends)
    if not LATE_TAILS:
        pl.when(jnp.logical_not(held_back))(tail_sends)

    def kv_conv(b):
        rows = slice(b * BLOCK, b * BLOCK + before)
        dst = slice(b * BLOCK, (b + 1) * BLOCK)
        kvc[0, dst, :] = conv(kvpad[0, rows, :], kt_ref[...])
        kvc[1, dst, :] = conv(kvpad[1, rows, :], vt_ref[...])

    def cols_of(col):
        return slice(col * quarter, (col + 1) * quarter)

    def to_peer_site(h):
        return remote(cand.at[h, 1 - y], rrow.at[h], a_s.at[h], a_r.at[h], peer_y)

    def to_site(h, row, col):
        return remote(
            cand.at[h, col], rother.at[h, o, y], b_s.at[h, row, col], b_r.at[h, o, y], at(row, col)
        )

    def at_site(h, src, col):
        return remote(
            cand.at[h, col], rother.at[h, src, col], b_s.at[h, 0, col], b_r.at[h, src, col], peer_y
        )

    def to_peer_col(h):
        return remote(site.at[h, y], site.at[h, y], c_s.at[h], c_r.at[h], peer_y)

    def from_peer_col(h):
        return remote(site.at[h, 1 - y], site.at[h, 1 - y], c_s.at[h], c_r.at[h], peer_y)

    def to_later(h, row, col):
        return remote(
            site.at[h, y], zfar.at[h, o, y], d_s.at[h, row, col], d_r.at[h, o, y], at(row, col)
        )

    def from_earlier(h, src, col):
        return remote(
            site.at[h, y], zfar.at[h, src, col], d_s.at[h, 0, 0], d_r.at[h, src, col], peer_y
        )

    def core_swap(h, core):
        if h == 0:
            part = far_k.at[core]
        else:
            part = far_v.at[pl.ds(2 * core, 2)]
        return remote(part, part, e_s.at[h], e_r.at[h], peer_core)

    def to_peer_core(h):
        return core_swap(h, c)

    def from_peer_core(h):
        return core_swap(h, 1 - c)

    def sums_own(h):
        return functools.reduce(jnp.logical_and, [o != row for row in TAKEN[h]], o >= 0)

    def candidate_step():
        pl.when(awaited > 0)(lambda: pl.semaphore_wait(ready, awaited))
        pl.when(held_back)(next_sends)

        @pl.when(chip_next)
        def _():
            remote(flag_out, flag_in.at[0], fl_s.at[0], fl_r.at[0], peer_core).wait_recv()

        @pl.when(first_core)
        def _():
            flag_peer.wait_recv()

        known = jnp.maximum(jnp.maximum(flag_in[0, 0:1, :], flag_in[1, 0:1, :]), phase)
        first = m * 2 * nb
        weights = [
            jnp.where(known == first + b, 1.0, 0.0).astype(jnp.bfloat16) for b in range(2 * nb)
        ]
        for h, taps in enumerate((kt_ref, vt_ref)):
            own[h].wait()
            raws[h].wait_recv()

            @pl.when(chip_prev)
            def _():
                rims[0][h].wait_recv()

            raw = weights[0] * chip[h, 0:before, :]
            for b in range(1, 2 * nb):
                raw = raw + weights[b] * chip[h, b * BLOCK : b * BLOCK + before, :]
            total = conv(raw, taps[:, half_cols])
            for col in range(2):
                cand[h, col] = total[:, cols_of(col)]

            for src, rows in SUMS[h].items():

                @pl.when(o == src)
                def _():
                    for row in rows:
                        for col in range(2):
                            to_site(h, row, col).start()

            pl.when(sums_own(h))(to_peer_site(h).start)

        if LATE_TAILS:
            tail_sends()
        else:
            pl.when(held_back)(tail_sends)

    def site_step(h):
        pl.when(sums_own(h))(functools.partial(own_site_step, h))

    def own_site_step(h):
        to_peer_site(h).wait_recv()
        site[h, y] = cand[h, y] + rrow[h]
        for row in range(no):
            sources = [src for src, rows in SUMS[h].items() if row in rows]
            if sources:

                @pl.when(o == row)
                def _():
                    for src in sources:
                        for col in range(2):
                            at_site(h, src, col).wait_recv()
                            site[h, y] = site[h, y] + rother[h, src, col]

        for src, rows in SPREADS[h].items():

            @pl.when(o == src)
            def _():
                for row in rows:
                    for col in range(2):
                        to_later(h, row, col).start()

        to_peer_col(h).start()

    def final_step(h):
        pl.when(sums_own(h))(from_peer_col(h).wait_recv)
        for src, rows in SPREADS[h].items():
            for row in rows:

                @pl.when(o == row)
                def _():
                    for col in range(2):
                        from_earlier(h, src, col).wait_recv()
                        if row in TAKEN[h]:
                            zfar[h, o, col] = zfar[h, src, col]
                        else:
                            zfar[h, o, col] = zfar[h, src, col] + site[h, col]

        gets = functools.reduce(
            jnp.logical_or, [o == row for rows in SPREADS[h].values() for row in rows]
        )

        def place(source):
            for col in range(2):
                if h == 0:
                    far_k[c, cols_of(col), cols_of(col)] = source(col)
                else:
                    far_v[2 * c + col] = source(col)

        pl.when(gets)(lambda: place(lambda col: zfar[h, o, col]))
        pl.when(jnp.logical_not(gets))(lambda: place(lambda col: site[h, col]))
        to_peer_core(h).start()

    for n in (1, 5, 2, 6):
        loads[n].wait()
    for b in range(2, nb + 1):
        kv_conv(b)
    loads[0].wait()
    loads[4].wait()

    row_ids = lax.broadcasted_iota(jnp.int32, (BLOCK, BLOCK), 0)
    col_ids = lax.broadcasted_iota(jnp.int32, (BLOCK, BLOCK), 1)
    causal = jnp.concatenate([row_ids >= col_ids] * per_group, 0)
    ones = jnp.ones((LOCAL * BLOCK, HEAD_DIM), jnp.bfloat16)

    def near(step, carry):
        b = jnp.where(step < nb - 2, step + 2, nb - 1 - step)

        @pl.when(b == 1)
        def _():
            @pl.when(has_prev)
            def _():
                for copy in edges:
                    copy.wait_recv()

            kv_conv(1)

        @pl.when(b == 0)
        def _():
            @pl.when(has_prev)
            def _():
                for copy in tails:
                    copy.wait_recv()

            kv_conv(0)

        bias = jnp.where((b == 0) & (d == 0), NEG, 0.0)
        base = pl.multiple_of(b * BLOCK, BLOCK)
        for g in range(groups):
            wide = slice(g * per_group * HEAD_DIM, (g + 1) * per_group * HEAD_DIM)
            cols = slice(g * HEAD_DIM, (g + 1) * HEAD_DIM)
            q = conv(qpad[pl.ds(base, BLOCK + HALO), wide], qt_ref[:, wide])
            q = jnp.concatenate(
                [q[:, h * HEAD_DIM : (h + 1) * HEAD_DIM] for h in range(per_group)], 0
            )
            qs[b, g // 2, :, cols_of(g % 2)] = q
            k = kvc[0, pl.ds(base, LOCAL * BLOCK), cols]
            v = kvc[1, pl.ds(base, LOCAL * BLOCK), cols]
            s = lax.dot_general(q, k, NT, preferred_element_type=jnp.float32)
            prev = s[:, :BLOCK] + bias
            mine = jnp.where(causal, s[:, BLOCK:], NEG)
            peak = jnp.max(jnp.maximum(prev, mine), axis=1, keepdims=True)
            p = jnp.concatenate(
                [jnp.exp2((prev - peak) * SCALE), jnp.exp2((mine - peak) * SCALE)], 1
            ).astype(jnp.bfloat16)
            acc_ref[b, g] = jnp.dot(
                p, jnp.concatenate([v, ones], 1), preferred_element_type=jnp.float32
            )
            max_ref[b, g] = jnp.broadcast_to(peak, (per_group * BLOCK, HEAD_DIM))

        pl.when(step == jnp.where(o == 0, FIRST_ROW_STEP, 0))(candidate_step)
        for h in range(2):
            if SITE_AFTER[h] is not None:
                pl.when(step == SITE_AFTER[h])(functools.partial(site_step, h))
        return carry

    lax.fori_loop(0, nb, near, 0)
    for h in range(2):
        if SITE_AFTER[h] is None:
            site_step(h)
    final_step(0)

    for b in range(nb):
        seen = jnp.int32(0)
        for e in range(entries):
            entry = list_ref[b, e]
            seen = jnp.where((entry >= 0) & (entry <= d * nb + b - LOCAL), 1, seen)
        bias_ref[b : b + 1, :] = jnp.full((1, 128), jnp.where(seen > 0, 0.0, NEG), jnp.float32)
    if nb < bias_ref.shape[0]:
        bias_ref[nb:, :] = jnp.zeros((bias_ref.shape[0] - nb, 128), jnp.float32)

    def far_stage(pair):
        for b in range(nb):
            distant_keys(qs, max_ref, max_ref, pbuf, far_k, bias_ref, pair, b)
        final_step(1)
        for b in range(nb):
            distant_values(acc_ref, max_ref, pbuf, far_v, pair, b, outb, 2 * pair * per_group)

    pl.when(first_core)(functools.partial(far_stage, 0))
    pl.when(second_core)(functools.partial(far_stage, 1))
    for h in range(2):
        from_peer_core(h).wait_recv()

    @pl.when(first_core & chip_prev)
    def _():
        for copy in flag_back:
            copy.wait_send()

    @pl.when(second_core)
    def _():
        flag_peer.wait_send()

        @pl.when(chip_next)
        def _():
            for k in range(2):
                for copy in rims[k]:
                    copy.wait_send()

    @pl.when(has_next)
    def _():
        for copy in edges + tails:
            copy.wait_send()

    for h in range(2):
        raws[h].wait_send()

        @pl.when(sums_own(h))
        def _():
            to_peer_site(h).wait_send()
            to_peer_col(h).wait_send()

        to_peer_core(h).wait_send()

        for table, copy in ((SUMS, to_site), (SPREADS, to_later)):
            for src, rows in table[h].items():

                @pl.when(o == src)
                def _():
                    for row in rows:
                        for col in range(2):
                            copy(h, row, col).wait_send()


def paired_call(arrays):
    block_list, q_proj, k_proj = arrays[:3]
    q_taps, k_taps, v_taps = arrays[4:]
    tokens, qw = q_proj.shape
    kvw = k_proj.shape[1]
    nb = tokens // BLOCK
    groups = kvw // HEAD_DIM
    rows = qw // kvw * BLOCK
    hw = kvw // 2
    piece = (BLOCK, hw // 2)
    dma = pltpu.SemaphoreType.DMA
    bf16, f32 = jnp.bfloat16, jnp.float32
    hbm_spec = pl.BlockSpec(memory_space=pltpu.HBM)
    scores = nb * groups * rows * (LOCAL + 1) * BLOCK
    vmem_spec = pl.BlockSpec(memory_space=pltpu.VMEM)
    partial_shapes = [
        ((tokens, qw), bf16),
        ((nb, groups // 2, rows, 2 * HEAD_DIM), bf16),
        ((nb, groups, rows, 2 * HEAD_DIM), f32),
        ((nb, groups, rows, HEAD_DIM), f32),
        ((groups // 2, 2 * BLOCK, hw), bf16),
        ((groups, BLOCK, HEAD_DIM), bf16),
        ((max(8, nb), 128), f32),
    ]
    partial = pl.pallas_call(
        paired_kernel,
        out_shape=[jax.ShapeDtypeStruct(*x) for x in partial_shapes],
        in_specs=[hbm_spec] * 7,
        out_specs=[vmem_spec] * 7,
        scratch_shapes=[
            pltpu.SMEM(block_list.shape, jnp.int32),
            pltpu.VMEM(q_taps.shape, f32),
            pltpu.VMEM(k_taps.shape, f32),
            pltpu.VMEM(v_taps.shape, f32),
            pltpu.VMEM((tokens + HALO, qw), bf16),
            pltpu.VMEM((2, tokens + BLOCK + HALO, kvw), bf16),
            pltpu.VMEM((2, tokens + BLOCK, kvw), bf16),
            pltpu.VMEM((nb, groups, rows, BLOCK), bf16),
            pltpu.VMEM((8, hw), jnp.int32),
            pltpu.VMEM((2, 8, hw), jnp.int32),
            pltpu.VMEM((2, 2 * tokens + HALO, hw), bf16),
            pltpu.VMEM((2, 2, *piece), bf16),
            pltpu.VMEM((2, *piece), bf16),
            pltpu.VMEM((2, ROWS, 2, *piece), bf16),
            pltpu.VMEM((2, 2, *piece), bf16),
            pltpu.VMEM((2, ROWS, 2, *piece), bf16),
            dma((7,)),
            dma((2,)),
            dma((3,)),
            dma((2,)),
            dma((2,)),
            dma((2,)),
            dma((2, 2)),
            dma((2,)),
            dma((5,)),
            dma((5,)),
            dma((2,)),
            dma((2,)),
            dma((2, ROWS, 2)),
            dma((2, ROWS, 2)),
            dma((2,)),
            dma((2,)),
            dma((2, ROWS, 2)),
            dma((2, ROWS, 2)),
            dma((2,)),
            dma((2,)),
            pltpu.SemaphoreType.REGULAR,
        ],
        compiler_params=pltpu.CompilerParams(
            collective_id=0, has_side_effects=True, vmem_limit_bytes=36 * 1024 * 1024
        ),
        cost_estimate=pl.CostEstimate(
            flops=4 * scores * HEAD_DIM,
            bytes_accessed=4 * tokens * qw + 4 * tokens * kvw,
            transcendentals=scores,
        ),
    )(*arrays)
    return pl.pallas_call(
        other_half_kernel,
        out_shape=jax.ShapeDtypeStruct((tokens, qw), bf16),
        in_specs=[vmem_spec] * 7,
        out_specs=hbm_spec,
        scratch_shapes=[
            pltpu.VMEM((nb, groups, rows, HEAD_DIM), f32),
            pltpu.VMEM((nb, groups, rows, BLOCK), bf16),
            pltpu.VMEM((tokens, qw // 2), bf16),
            dma,
            dma((nb,)),
        ],
        compiler_params=pltpu.CompilerParams(vmem_limit_bytes=36 * 1024 * 1024),
        cost_estimate=pl.CostEstimate(
            flops=scores * HEAD_DIM, bytes_accessed=2 * tokens * qw, transcendentals=scores // 6
        ),
    )(*partial)


def body(q_proj, k_proj, v_proj, q_taps, k_taps, v_taps, block_list):
    tokens, qw = q_proj.shape
    kvw = k_proj.shape[1]
    ni = lax.axis_size("inner")
    no = lax.axis_size("outer")
    nb = tokens // BLOCK
    groups = kvw // HEAD_DIM
    rows = qw // kvw * BLOCK
    slots = max(1, nb * ni * no // STRIDE)
    piece_rows = max(HALO, BLOCK // ni)
    piece_cols = BLOCK * kvw // (ni * piece_rows)
    piece = (piece_rows, piece_cols)
    dma = pltpu.SemaphoreType.DMA
    bf16, f32 = jnp.bfloat16, jnp.float32
    hbm_spec = pl.BlockSpec(memory_space=pltpu.HBM)
    scores = nb * groups * rows * (LOCAL + slots) * BLOCK
    arrays = [
        pltpu.with_memory_space_constraint(x, pltpu.HBM)
        for x in (block_list, q_proj, k_proj, v_proj, q_taps, k_taps, v_taps)
    ]
    paired = ni == 4 and no == ROWS and nb * ni * no == STRIDE and groups == 4 and nb >= 2
    if paired:
        return paired_call(arrays)
    return pl.pallas_call(
        functools.partial(kernel, ni, no),
        out_shape=jax.ShapeDtypeStruct((tokens, qw), bf16),
        in_specs=[hbm_spec] * 7,
        out_specs=pl.BlockSpec(memory_space=pltpu.VMEM),
        scratch_shapes=[
            pltpu.SMEM(block_list.shape, jnp.int32),
            pltpu.VMEM(q_taps.shape, f32),
            pltpu.VMEM(k_taps.shape, f32),
            pltpu.VMEM(v_taps.shape, f32),
            pltpu.VMEM((tokens + HALO, qw), bf16),
            pltpu.VMEM((2, tokens + BLOCK + HALO, kvw), bf16),
            pltpu.VMEM((2, tokens + BLOCK, kvw), bf16),
            pltpu.VMEM((nb, groups, rows, HEAD_DIM), bf16),
            pltpu.VMEM((nb, groups, rows, 2 * HEAD_DIM), f32),
            pltpu.VMEM((nb, groups, rows, HEAD_DIM), f32),
            pltpu.VMEM((nb, groups, rows, slots * BLOCK), bf16),
            pltpu.VMEM((max(8, nb), 128), f32),
            pltpu.VMEM((max(8, nb), 128), f32),
            pltpu.VMEM((2, BLOCK, kvw), bf16),
            pltpu.VMEM((2, ni, *piece), bf16),
            pltpu.VMEM((2, *piece), bf16),
            pltpu.VMEM((2, no, *piece), bf16),
            pltpu.VMEM((2, slots, *piece), bf16),
            pltpu.VMEM((2, slots, BLOCK, kvw), bf16),
            dma((7,)),
            dma((5,)),
            dma((5,)),
            dma,
            dma,
            dma((2, ni)),
            dma((2, ni)),
            dma((2, no)),
            dma((2, no)),
            dma((2, ni)),
            dma((2, ni)),
        ],
        compiler_params=pltpu.CompilerParams(
            collective_id=0, has_side_effects=True, vmem_limit_bytes=48 * 1024 * 1024
        ),
        cost_estimate=pl.CostEstimate(
            flops=4 * scores * HEAD_DIM,
            bytes_accessed=4 * tokens * qw + 4 * tokens * kvw,
            transcendentals=scores,
        ),
    )(*arrays)


def solution(mesh):
    rows = P(("groups", "outer", "inner"), None)
    return jax.shard_map(
        body,
        mesh=mesh,
        in_specs=(rows, rows, rows, P(), P(), P(), rows),
        out_specs=rows,
        check_vma=False,
    )
```

```python
import functools
import math

import jax
import jax.numpy as jnp
from jax import lax
from jax.experimental import pallas as pl
from jax.experimental.pallas import tpu as pltpu
from jax.sharding import PartitionSpec as P

HEAD_DIM = 128
BLOCK = 128
LOCAL = 2
STRIDE = 64
HALO = 16
NEG = -1e30
MESH = pl.DeviceIdType.MESH
SCALE = math.log2(math.e) / math.sqrt(HEAD_DIM)
NT = (((1,), (1,)), ((), ()))


def conv(padded, taps):
    wide = padded.astype(jnp.float32)
    total = taps[0:1] * wide[HALO:]
    for j in (1, 2):
        total = total + taps[j : j + 1] * pltpu.roll(wide, j, 0)[HALO:]
    return total.astype(jnp.bfloat16)


def kernel(
    ni, no, list_hbm, q_hbm, k_hbm, v_hbm, qt_hbm, kt_hbm, vt_hbm, outb,
    list_ref, qt_ref, kt_ref, vt_ref, qpad, kvpad, kvc, qs, acc_ref, max_ref, pbuf, wout, win, cand, rbuf, zpiece, zbuf,
    fsum, far, in_sem, tail_s, tail_r, w_s, w_r, sc_s, sc_r, z_s, z_r,
    g_s, g_r,
):
    tokens, qw = q_hbm.shape
    kvw = k_hbm.shape[1]
    groups = kvw // HEAD_DIM
    per_group = qw // kvw
    nb = tokens // BLOCK
    slots = far.shape[1]
    piece_rows, piece_cols = zpiece.shape[1:]
    col_parts = kvw // piece_cols
    before = BLOCK + HALO
    entries = list_ref.shape[1]
    o = lax.axis_index("outer")
    i = lax.axis_index("inner")
    d = o * ni + i
    last = ni * no - 1
    has_next = d < last
    has_prev = d > 0

    def chain(step):
        other = d + step
        return {"outer": other // ni, "inner": lax.rem(other, ni)}

    def inner_peer(r):
        return {"inner": lax.rem(i + r, ni)}

    loads = [
        pltpu.make_async_copy(q_hbm, qpad.at[pl.ds(HALO, tokens)], in_sem.at[0]),
        pltpu.make_async_copy(k_hbm, kvpad.at[0, pl.ds(before, tokens)], in_sem.at[1]),
        pltpu.make_async_copy(v_hbm, kvpad.at[1, pl.ds(before, tokens)], in_sem.at[2]),
        pltpu.make_async_copy(list_hbm, list_ref, in_sem.at[3]),
        pltpu.make_async_copy(qt_hbm, qt_ref, in_sem.at[4]),
        pltpu.make_async_copy(kt_hbm, kt_ref, in_sem.at[5]),
        pltpu.make_async_copy(vt_hbm, vt_ref, in_sem.at[6]),
    ]
    for n in (3, 1, 5, 2, 6, 0, 4):
        loads[n].start()

    barrier = pltpu.get_barrier_semaphore()
    for r in range(1, ni):
        pl.semaphore_signal(barrier, inc=1, device_id=inner_peer(r), device_id_type=MESH)
    for r in range(1, no):
        pl.semaphore_signal(
            barrier, inc=1, device_id={"outer": lax.rem(o + r, no)}, device_id_type=MESH
        )

    @pl.when(has_next)
    def _():
        pl.semaphore_signal(barrier, inc=1, device_id=chain(1), device_id_type=MESH)

    @pl.when(has_prev)
    def _():
        pl.semaphore_signal(barrier, inc=1, device_id=chain(-1), device_id_type=MESH)

    loads[3].wait()
    phase = jnp.int32(-1)
    for b in range(nb):
        for e in range(entries):
            entry = list_ref[b, e]
            distant = (entry >= 0) & (entry <= d * nb + b - LOCAL)
            phase = jnp.maximum(phase, jnp.where(distant, lax.rem(entry, STRIDE), -1))
    for b in range(nb):
        hit = lax.rem((d - 1) * nb + b + STRIDE, STRIDE) == phase
        wout[b : b + 1, :] = jnp.full((1, 128), jnp.where(hit, 1.0, 0.0), jnp.float32)
    if nb < wout.shape[0]:
        wout[nb:, :] = jnp.zeros((wout.shape[0] - nb, 128), jnp.float32)

    @pl.when(d == 0)
    def _():
        qpad[0:HALO, :] = jnp.zeros((HALO, qw), jnp.bfloat16)
        kvpad[:, 0:before, :] = jnp.zeros((2, before, kvw), jnp.bfloat16)

    @pl.when(d == last)
    def _():
        win[...] = jnp.zeros(win.shape, jnp.float32)

    fsum[...] = jnp.zeros(fsum.shape, jnp.bfloat16)

    w_copy = pltpu.make_async_remote_copy(
        wout, win, w_s, w_r, device_id=chain(-1), device_id_type=MESH
    )
    rim = pl.ds(tokens - HALO, HALO)
    body_rows = pl.ds(tokens - before, BLOCK)

    def to_next(src, dst, n):
        return pltpu.make_async_remote_copy(
            src, dst, tail_s.at[n], tail_r.at[n], device_id=chain(1), device_id_type=MESH
        )

    tails = [
        to_next(k_hbm.at[rim], kvpad.at[0, pl.ds(BLOCK, HALO)], 0),
        to_next(v_hbm.at[rim], kvpad.at[1, pl.ds(BLOCK, HALO)], 1),
        to_next(k_hbm.at[body_rows], kvpad.at[0, pl.ds(0, BLOCK)], 2),
        to_next(v_hbm.at[body_rows], kvpad.at[1, pl.ds(0, BLOCK)], 3),
        to_next(q_hbm.at[rim], qpad.at[pl.ds(0, HALO)], 4),
    ]

    def first_sends():
        pl.semaphore_wait(
            barrier,
            ni - 1 + no - 1 + jnp.where(has_next, 1, 0) + jnp.where(has_prev, 1, 0),
        )

        @pl.when(has_prev)
        def _():
            w_copy.start()

        @pl.when(has_next)
        def _():
            for copy in tails:
                copy.start()

    def kv_conv(b):
        rows = slice(b * BLOCK, b * BLOCK + before)
        dst = slice(b * BLOCK, (b + 1) * BLOCK)
        kvc[0, dst, :] = conv(kvpad[0, rows, :], kt_ref[...])
        kvc[1, dst, :] = conv(kvpad[1, rows, :], vt_ref[...])

    for n in (1, 5, 2, 6):
        loads[n].wait()
    for b in range(2, nb + 1):
        kv_conv(b)

    def candidate_step():
        @pl.when(has_prev)
        def _():
            tails[0].wait_recv()
            tails[1].wait_recv()

        kv_conv(1)

        @pl.when(has_next)
        def _():
            w_copy.wait_recv()

        for g in range(groups):
            cols = slice(g * HEAD_DIM, (g + 1) * HEAD_DIM)
            for half in range(2):
                total = jnp.zeros((BLOCK, HEAD_DIM), jnp.float32)
                for b in range(nb):
                    own = jnp.where(lax.rem(d * nb + b, STRIDE) == phase, 1.0, 0.0)
                    weight = jnp.maximum(win[b : b + 1, :], own)
                    rows = slice((b + 1) * BLOCK, (b + 2) * BLOCK)
                    total = total + weight * kvc[half, rows, cols].astype(jnp.float32)
                cand[half, :, cols] = total.astype(jnp.bfloat16)

        for half in range(2):
            for r in range(1, ni):
                scatter(half, r).start()

    def part(index):
        row = pl.multiple_of(index // col_parts * piece_rows, piece_rows)
        col = pl.multiple_of(lax.rem(index, col_parts) * piece_cols, piece_cols)
        return pl.ds(row, piece_rows), pl.ds(col, piece_cols)

    def scatter(half, r):
        return pltpu.make_async_remote_copy(
            cand.at[(half, *part(lax.rem(i + r, ni)))],
            rbuf.at[half, r],
            sc_s.at[half, r],
            sc_r.at[half, r],
            device_id=inner_peer(r),
            device_id_type=MESH,
        )

    def column(half, r):
        return pltpu.make_async_remote_copy(
            zpiece.at[half],
            zbuf.at[half, r],
            z_s.at[half, r],
            z_r.at[half, r],
            device_id={"outer": lax.rem(o + r, no)},
            device_id_type=MESH,
        )

    def gather(half, r):
        return pltpu.make_async_remote_copy(
            fsum.at[half],
            far.at[(half, slice(None), *part(i))],
            g_s.at[half, r],
            g_r.at[half, r],
            device_id=inner_peer(r),
            device_id_type=MESH,
        )

    def column_step(half):
        total = cand[(half, *part(i))].astype(jnp.float32)
        for r in range(1, ni):
            scatter(half, r).wait_recv()
            total = total + rbuf[half, r].astype(jnp.float32)
        zpiece[half] = total.astype(jnp.bfloat16)
        for r in range(1, no):
            pl.when(o + r < no)(column(half, r).start)

    def slot_of(row):
        return lax.rem(row * (ni * nb) // STRIDE, slots)

    def gather_step(half):
        fsum[half, slot_of(o)] = zpiece[half]
        for r in range(1, no):

            @pl.when(o >= r)
            def _():
                column(half, r).wait_recv()
                at = slot_of(o - r)
                fsum[half, at] = (
                    fsum[half, at].astype(jnp.float32) + zbuf[half, r].astype(jnp.float32)
                ).astype(jnp.bfloat16)

        for r in range(1, ni):
            gather(half, r).start()
        far[(half, slice(None), *part(i))] = fsum[half]

    def gather_wait(half):
        for r in range(1, ni):
            gather(half, r).wait_recv()

    loads[0].wait()
    loads[4].wait()

    row_ids = lax.broadcasted_iota(jnp.int32, (BLOCK, BLOCK), 0)
    col_ids = lax.broadcasted_iota(jnp.int32, (BLOCK, BLOCK), 1)
    causal = jnp.concatenate([row_ids >= col_ids] * per_group, 0)
    ones = jnp.ones((LOCAL * BLOCK, HEAD_DIM), jnp.bfloat16)

    def near(step, carry):
        b = jnp.where(step < nb - 2, step + 2, nb - 1 - step)

        @pl.when(b == 0)
        def _():
            @pl.when(has_prev)
            def _():
                tails[2].wait_recv()
                tails[3].wait_recv()
                tails[4].wait_recv()

            kv_conv(0)

        bias = jnp.where((b == 0) & (d == 0), NEG, 0.0)
        base = pl.multiple_of(b * BLOCK, BLOCK)
        for g in range(groups):
            wide = slice(g * per_group * HEAD_DIM, (g + 1) * per_group * HEAD_DIM)
            cols = slice(g * HEAD_DIM, (g + 1) * HEAD_DIM)
            q = conv(qpad[pl.ds(base, BLOCK + HALO), wide], qt_ref[:, wide])
            q = jnp.concatenate(
                [q[:, h * HEAD_DIM : (h + 1) * HEAD_DIM] for h in range(per_group)], 0
            )
            qs[b, g] = q
            k = kvc[0, pl.ds(base, LOCAL * BLOCK), cols]
            v = kvc[1, pl.ds(base, LOCAL * BLOCK), cols]
            s = lax.dot_general(q, k, NT, preferred_element_type=jnp.float32)
            prev = s[:, :BLOCK] + bias
            own = jnp.where(causal, s[:, BLOCK:], NEG)
            peak = jnp.max(jnp.maximum(prev, own), axis=1, keepdims=True)
            p = jnp.concatenate(
                [jnp.exp2((prev - peak) * SCALE), jnp.exp2((own - peak) * SCALE)], 1
            ).astype(jnp.bfloat16)
            acc_ref[b, g] = jnp.dot(
                p, jnp.concatenate([v, ones], 1), preferred_element_type=jnp.float32
            )
            max_ref[b, g] = jnp.broadcast_to(peak, (per_group * BLOCK, HEAD_DIM))

        pl.when(step == 0)(first_sends)
        pl.when(step == 1)(candidate_step)

        @pl.when(step == 2)
        def _():
            column_step(0)
            column_step(1)

        return carry

    lax.fori_loop(0, nb, near, 0)
    gather_step(0)
    gather_step(1)
    gather_wait(0)

    def distant_keys(b, carry):
        biases = []
        for n in range(slots):
            seen = jnp.int32(0)
            for e in range(entries):
                entry = list_ref[b, e]
                hit = (entry >= n * STRIDE) & (entry < (n + 1) * STRIDE)
                hit = hit & (entry <= d * nb + b - LOCAL)
                seen = jnp.where(hit, 1, seen)
            biases.append(jnp.where(seen > 0, 0.0, NEG))
        for g in range(groups):
            cols = slice(g * HEAD_DIM, (g + 1) * HEAD_DIM)
            q = qs[b, g]
            near_peak = max_ref[b, g]
            scores = []
            top = None
            for n in range(slots):
                s = lax.dot_general(q, far[0, n, :, cols], NT, preferred_element_type=jnp.float32)
                s = s + biases[n]
                scores.append(s)
                top = s if top is None else jnp.maximum(top, s)
            peak = jnp.maximum(near_peak, jnp.max(top, axis=1, keepdims=True))
            max_ref[b, g] = jnp.exp2((near_peak - peak) * SCALE)
            for n in range(slots):
                p = jnp.exp2((scores[n] - peak) * SCALE)
                pbuf[b, g, :, n * BLOCK : (n + 1) * BLOCK] = p.astype(jnp.bfloat16)
        return carry

    def distant_values(b, carry):
        base = pl.multiple_of(b * BLOCK, BLOCK)
        for g in range(groups):
            cols = slice(g * HEAD_DIM, (g + 1) * HEAD_DIM)
            both = acc_ref[b, g]
            shrink = max_ref[b, g]
            total = both[:, :HEAD_DIM] * shrink
            count = both[:, HEAD_DIM:] * shrink
            for n in range(slots):
                more = jnp.dot(
                    pbuf[b, g, :, n * BLOCK : (n + 1) * BLOCK],
                    jnp.concatenate([far[1, n, :, cols], ones[:BLOCK]], 1),
                    preferred_element_type=jnp.float32,
                )
                total = total + more[:, :HEAD_DIM]
                count = count + more[:, HEAD_DIM:]
            mixed = (total / count).astype(jnp.bfloat16)
            for h in range(per_group):
                head = g * per_group + h
                outb[pl.ds(base, BLOCK), head * HEAD_DIM : (head + 1) * HEAD_DIM] = mixed[
                    h * BLOCK : (h + 1) * BLOCK
                ]
        return carry

    lax.fori_loop(0, nb, distant_keys, 0)
    gather_wait(1)
    lax.fori_loop(0, nb, distant_values, 0)

    @pl.when(has_prev)
    def _():
        w_copy.wait_send()

    @pl.when(has_next)
    def _():
        for copy in tails:
            copy.wait_send()

    for half in range(2):
        for r in range(1, ni):
            scatter(half, r).wait_send()
            gather(half, r).wait_send()
        for r in range(1, no):
            pl.when(o + r < no)(column(half, r).wait_send)


ROWS = 4
SUMS = ({0: (1,), 2: (3,)}, {0: (2,), 1: (2,)})
SPREADS = ({1: (3, 2)}, {2: (3, 1)})
TAKEN = ((), (1,))
FIRST_ROW_STEP = 1
SITE_AFTER = (2, 2)
LATE_TAILS = False
LATE = ((2, 3), (1, 3), (0, 2))


def dests(row, late):
    rows = {r for table in (*SUMS, *SPREADS) for r in table.get(row, ())}
    return sorted(r for r in rows if ((row, r) in LATE) == late)


def origins(row, late):
    return [r for r in range(ROWS) if row in dests(r, late)]


def distant_keys(qs, peaks, max_ref, pbuf, far_k, bias_ref, pair, b):
    both = lax.dot_general(qs[b, pair], far_k[pair], NT, preferred_element_type=jnp.float32)
    bias = bias_ref[b : b + 1, :]
    for n in range(2):
        g = 2 * pair + n
        s = both[:, n * BLOCK : (n + 1) * BLOCK] + bias
        near_peak = peaks[b, g]
        peak = jnp.maximum(near_peak, jnp.max(s, axis=1, keepdims=True))
        max_ref[b, g] = jnp.exp2((near_peak - peak) * SCALE)
        pbuf[b, g] = jnp.exp2((s - peak) * SCALE).astype(jnp.bfloat16)


def distant_values(acc_ref, max_ref, pbuf, far_v, pair, b, dst, first_head):
    per_group = acc_ref.shape[2] // BLOCK
    ones = jnp.ones((BLOCK, HEAD_DIM), jnp.bfloat16)
    for n in range(2):
        g = 2 * pair + n
        shrink = max_ref[b, g]
        more = jnp.dot(
            pbuf[b, g],
            jnp.concatenate([far_v[g], ones], 1),
            preferred_element_type=jnp.float32,
        )
        total = acc_ref[b, g, :, :HEAD_DIM] * shrink + more[:, :HEAD_DIM]
        count = acc_ref[b, g, :, HEAD_DIM:] * shrink + more[:, HEAD_DIM:]
        mixed = (total / count).astype(jnp.bfloat16)
        for h in range(per_group):
            head = first_head + n * per_group + h
            dst[b * BLOCK : (b + 1) * BLOCK, head * HEAD_DIM : (head + 1) * HEAD_DIM] = mixed[
                h * BLOCK : (h + 1) * BLOCK
            ]


def other_half_kernel(
    own_out, qs, acc_ref, peaks, far_k, far_v, bias_ref, out, max_ref, pbuf, half_out, own_sem, out_sem
):
    nb = qs.shape[0]
    tokens, qw = own_out.shape
    wide = qw // 2
    c = lax.rem(lax.axis_index("inner"), 2)

    def half(pair):
        own_cols = pl.ds((1 - pair) * wide, wide)
        cols = pl.ds(pair * wide, wide)
        own_copy = pltpu.make_async_copy(own_out.at[:, own_cols], out.at[:, own_cols], own_sem)
        own_copy.start()
        for b in range(nb):
            distant_keys(qs, peaks, max_ref, pbuf, far_k, bias_ref, pair, b)
        copies = []
        for b in range(nb):
            rows = pl.ds(b * BLOCK, BLOCK)
            distant_values(acc_ref, max_ref, pbuf, far_v, pair, b, half_out, 0)
            copies.append(
                pltpu.make_async_copy(half_out.at[rows], out.at[rows, cols], out_sem.at[b])
            )
            copies[-1].start()
        for copy in copies:
            copy.wait()
        own_copy.wait()

    pl.when(c == 0)(lambda: half(1))
    pl.when(c == 1)(lambda: half(0))


def paired_kernel(
    list_hbm, q_hbm, k_hbm, v_hbm, qt_hbm, kt_hbm, vt_hbm,
    outb, qs, acc_ref, max_ref, far_k, far_v, bias_ref,
    list_ref, qt_ref, kt_ref, vt_ref, qpad, kvpad, kvc, pbuf,
    flag_out, flag_in, chip, cand, rrow, rother, site, zfar,
    in_sem, own_sem, fl_s, fl_r, raw_s, raw_r, rim_s, rim_r, tail_s, tail_r,
    a_s, a_r, b_s, b_r, c_s, c_r, d_s, d_r, e_s, e_r, ready,
):
    tokens, qw = q_hbm.shape
    kvw = k_hbm.shape[1]
    groups = kvw // HEAD_DIM
    hw = kvw // 2
    quarter = hw // 2
    per_group = qw // kvw
    nb = tokens // BLOCK
    before = BLOCK + HALO
    entries = list_ref.shape[1]
    o = lax.axis_index("outer")
    i = lax.axis_index("inner")
    y = i // 2
    c = lax.rem(i, 2)
    m = o * 2 + y
    no = ROWS
    last_chip = no * 2 - 1
    d = o * 4 + i
    has_next = d < 4 * no - 1
    has_prev = d > 0
    chip_next = m < last_chip
    chip_prev = m > 0
    first_core = c == 0
    second_core = c == 1

    def chip_core(step, core):
        other = m + step
        return {"outer": other // 2, "inner": lax.rem(other, 2) * 2 + core}

    def at(row, col):
        return {"outer": row, "inner": col * 2 + c}

    peer_core = {"inner": i + 1 - 2 * c}
    peer_y = {"inner": lax.rem(i + 2, 4)}
    next_device = {"outer": (d + 1) // 4, "inner": lax.rem(d + 1, 4)}

    barrier = pltpu.get_barrier_semaphore()

    def greet(device):
        pl.semaphore_signal(barrier, inc=1, device_id=device, device_id_type=MESH)

    def call(device):
        pl.semaphore_signal(ready, inc=1, device_id=device, device_id_type=MESH)

    loads = [
        pltpu.make_async_copy(q_hbm, qpad.at[pl.ds(HALO, tokens)], in_sem.at[0]),
        pltpu.make_async_copy(k_hbm, kvpad.at[0, pl.ds(before, tokens)], in_sem.at[1]),
        pltpu.make_async_copy(v_hbm, kvpad.at[1, pl.ds(before, tokens)], in_sem.at[2]),
        pltpu.make_async_copy(list_hbm, list_ref, in_sem.at[3]),
        pltpu.make_async_copy(qt_hbm, qt_ref, in_sem.at[4]),
        pltpu.make_async_copy(kt_hbm, kt_ref, in_sem.at[5]),
        pltpu.make_async_copy(vt_hbm, vt_ref, in_sem.at[6]),
    ]
    half_cols = pl.ds(pl.multiple_of(c * hw, hw), hw)
    peer_cols = pl.ds(pl.multiple_of((1 - c) * hw, hw), hw)
    chip_rows = pl.ds(pl.multiple_of(HALO + c * tokens, HALO), tokens)
    own = [
        pltpu.make_async_copy(x.at[:, half_cols], chip.at[h, chip_rows], own_sem.at[h])
        for h, x in enumerate((k_hbm, v_hbm))
    ]
    loads[3].start()
    greet(peer_core)
    greet(peer_y)

    late_next = (y == 1) & functools.reduce(
        jnp.logical_or, [o == row for row in range(no - 1) if (row, row + 1) in LATE], o < 0
    )
    late_prev = (y == 0) & functools.reduce(
        jnp.logical_or, [o == row + 1 for row in range(no - 1) if (row, row + 1) in LATE], o < 0
    )

    @pl.when(chip_next)
    def _():
        greet(chip_core(1, 0))
        pl.when(second_core & late_next)(lambda: greet(chip_core(1, 1)))

    pl.when(chip_prev & jnp.logical_not(late_prev))(lambda: greet(chip_core(-1, 1)))
    for row in range(no):

        @pl.when(o == row)
        def _():
            for other in origins(row, False) + dests(row, True):
                greet(at(other, 0))
                greet(at(other, 1))

    for n in (1, 5, 2, 6):
        loads[n].start()
    for copy in own:
        copy.start()
    for n in (0, 4):
        loads[n].start()

    def remote(src, dst, send, recv, device):
        return pltpu.make_async_remote_copy(
            src, dst, send, recv, device_id=device, device_id_type=MESH
        )

    flag_back = [
        remote(flag_out, flag_in.at[0], fl_s.at[k], fl_r.at[0], chip_core(-1, k)) for k in range(2)
    ]
    flag_peer = remote(flag_out, flag_in.at[1], fl_s.at[2], fl_r.at[1], peer_core)
    raws = [
        remote(x.at[:, peer_cols], chip.at[h, chip_rows], raw_s.at[h], raw_r.at[h], peer_core)
        for h, x in enumerate((k_hbm, v_hbm))
    ]
    rim = pl.ds(tokens - HALO, HALO)
    rims = [
        [
            remote(
                x.at[rim, k * hw : (k + 1) * hw],
                chip.at[h, pl.ds(0, HALO)],
                rim_s.at[k, h],
                rim_r.at[h],
                chip_core(1, k),
            )
            for h, x in enumerate((k_hbm, v_hbm))
        ]
        for k in range(2)
    ]
    body_rows = pl.ds(tokens - before, BLOCK)

    def to_next(n, src, dst):
        return remote(src, dst, tail_s.at[n], tail_r.at[n], next_device)

    edges = [
        to_next(h, x.at[rim], kvpad.at[h, pl.ds(BLOCK, HALO)]) for h, x in enumerate((k_hbm, v_hbm))
    ]
    tails = [
        to_next(2 + h, x.at[body_rows], kvpad.at[h, pl.ds(0, BLOCK)])
        for h, x in enumerate((k_hbm, v_hbm))
    ] + [to_next(4, q_hbm.at[rim], qpad.at[pl.ds(0, HALO)])]

    @pl.when(jnp.logical_not(has_prev))
    def _():
        qpad[0:HALO, :] = jnp.zeros((HALO, qw), jnp.bfloat16)
        kvpad[:, 0:before, :] = jnp.zeros((2, before, kvw), jnp.bfloat16)

    @pl.when(jnp.logical_not(chip_prev))
    def _():
        chip[:, 0:HALO, :] = jnp.zeros((2, HALO, hw), jnp.bfloat16)

    far_k[...] = jnp.zeros(far_k.shape, jnp.bfloat16)

    @pl.when(jnp.logical_not(chip_next))
    def _():
        flag_in[0] = jnp.full(flag_in.shape[1:], -1, jnp.int32)

    @pl.when(second_core)
    def _():
        flag_in[1] = jnp.full(flag_in.shape[1:], -1, jnp.int32)

    expected = 2 + jnp.where(chip_prev & first_core, 2, 0)
    expected = expected + jnp.where(chip_prev & late_prev & second_core, 1, 0)
    sends_on = second_core & chip_next
    expected = expected + jnp.where(sends_on & jnp.logical_not(late_next), 2, 0)
    awaited = jnp.where(sends_on & late_next, 2, 0)
    for row in range(no):
        met = 2 * len(dests(row, False) + origins(row, True))
        expected = expected + jnp.where(o == row, met, 0)
        awaited = awaited + jnp.where(o == row, 2 * len(dests(row, True)), 0)
    pl.semaphore_wait(barrier, expected)
    pl.when(chip_prev & late_prev)(lambda: call(chip_core(-1, 1)))
    for row in range(no):
        if origins(row, True):

            @pl.when(o == row)
            def _():
                for src in origins(row, True):
                    call(at(src, 0))
                    call(at(src, 1))

    for copy in raws:
        copy.start()

    loads[3].wait()
    phase = jnp.int32(-1)
    for b in range(nb):
        for e in range(entries):
            entry = list_ref[b, e]
            distant = (entry >= 0) & (entry <= d * nb + b - LOCAL)
            phase = jnp.maximum(phase, jnp.where(distant, lax.rem(entry, STRIDE), -1))
    flag_out[...] = jnp.full(flag_out.shape, phase, jnp.int32)

    @pl.when(first_core & chip_prev)
    def _():
        for copy in flag_back:
            copy.start()

    pl.when(second_core)(flag_peer.start)
    def next_sends():
        @pl.when(sends_on)
        def _():
            for h in range(2):
                for k in range(2):
                    rims[k][h].start()

        @pl.when(has_next)
        def _():
            for copy in edges:
                copy.start()

    def tail_sends():
        @pl.when(has_next)
        def _():
            for copy in tails:
                copy.start()

    held_back = sends_on & late_next
    pl.when(jnp.logical_not(held_back))(next_sends)
    if not LATE_TAILS:
        pl.when(jnp.logical_not(held_back))(tail_sends)

    def kv_conv(b):
        rows = slice(b * BLOCK, b * BLOCK + before)
        dst = slice(b * BLOCK, (b + 1) * BLOCK)
        kvc[0, dst, :] = conv(kvpad[0, rows, :], kt_ref[...])
        kvc[1, dst, :] = conv(kvpad[1, rows, :], vt_ref[...])

    def cols_of(col):
        return slice(col * quarter, (col + 1) * quarter)

    def to_peer_site(h):
        return remote(cand.at[h, 1 - y], rrow.at[h], a_s.at[h], a_r.at[h], peer_y)

    def to_site(h, row, col):
        return remote(
            cand.at[h, col], rother.at[h, o, y], b_s.at[h, row, col], b_r.at[h, o, y], at(row, col)
        )

    def at_site(h, src, col):
        return remote(
            cand.at[h, col], rother.at[h, src, col], b_s.at[h, 0, col], b_r.at[h, src, col], peer_y
        )

    def to_peer_col(h):
        return remote(site.at[h, y], site.at[h, y], c_s.at[h], c_r.at[h], peer_y)

    def from_peer_col(h):
        return remote(site.at[h, 1 - y], site.at[h, 1 - y], c_s.at[h], c_r.at[h], peer_y)

    def to_later(h, row, col):
        return remote(
            site.at[h, y], zfar.at[h, o, y], d_s.at[h, row, col], d_r.at[h, o, y], at(row, col)
        )

    def from_earlier(h, src, col):
        return remote(
            site.at[h, y], zfar.at[h, src, col], d_s.at[h, 0, 0], d_r.at[h, src, col], peer_y
        )

    def core_swap(h, core):
        if h == 0:
            part = far_k.at[core]
        else:
            part = far_v.at[pl.ds(2 * core, 2)]
        return remote(part, part, e_s.at[h], e_r.at[h], peer_core)

    def to_peer_core(h):
        return core_swap(h, c)

    def from_peer_core(h):
        return core_swap(h, 1 - c)

    def sums_own(h):
        return functools.reduce(jnp.logical_and, [o != row for row in TAKEN[h]], o >= 0)

    def candidate_step():
        pl.when(awaited > 0)(lambda: pl.semaphore_wait(ready, awaited))
        pl.when(held_back)(next_sends)

        @pl.when(chip_next)
        def _():
            remote(flag_out, flag_in.at[0], fl_s.at[0], fl_r.at[0], peer_core).wait_recv()

        @pl.when(first_core)
        def _():
            flag_peer.wait_recv()

        known = jnp.maximum(jnp.maximum(flag_in[0, 0:1, :], flag_in[1, 0:1, :]), phase)
        first = m * 2 * nb
        weights = [
            jnp.where(known == first + b, 1.0, 0.0).astype(jnp.bfloat16) for b in range(2 * nb)
        ]
        for h, taps in enumerate((kt_ref, vt_ref)):
            own[h].wait()
            raws[h].wait_recv()

            @pl.when(chip_prev)
            def _():
                rims[0][h].wait_recv()

            raw = weights[0] * chip[h, 0:before, :]
            for b in range(1, 2 * nb):
                raw = raw + weights[b] * chip[h, b * BLOCK : b * BLOCK + before, :]
            total = conv(raw, taps[:, half_cols])
            for col in range(2):
                cand[h, col] = total[:, cols_of(col)]

            for src, rows in SUMS[h].items():

                @pl.when(o == src)
                def _():
                    for row in rows:
                        for col in range(2):
                            to_site(h, row, col).start()

            pl.when(sums_own(h))(to_peer_site(h).start)

        if LATE_TAILS:
            tail_sends()
        else:
            pl.when(held_back)(tail_sends)

    def site_step(h):
        pl.when(sums_own(h))(functools.partial(own_site_step, h))

    def own_site_step(h):
        to_peer_site(h).wait_recv()
        site[h, y] = cand[h, y] + rrow[h]
        for row in range(no):
            sources = [src for src, rows in SUMS[h].items() if row in rows]
            if sources:

                @pl.when(o == row)
                def _():
                    for src in sources:
                        for col in range(2):
                            at_site(h, src, col).wait_recv()
                            site[h, y] = site[h, y] + rother[h, src, col]

        for src, rows in SPREADS[h].items():

            @pl.when(o == src)
            def _():
                for row in rows:
                    for col in range(2):
                        to_later(h, row, col).start()

        to_peer_col(h).start()

    def final_step(h):
        pl.when(sums_own(h))(from_peer_col(h).wait_recv)
        for src, rows in SPREADS[h].items():
            for row in rows:

                @pl.when(o == row)
                def _():
                    for col in range(2):
                        from_earlier(h, src, col).wait_recv()
                        if row in TAKEN[h]:
                            zfar[h, o, col] = zfar[h, src, col]
                        else:
                            zfar[h, o, col] = zfar[h, src, col] + site[h, col]

        gets = functools.reduce(
            jnp.logical_or, [o == row for rows in SPREADS[h].values() for row in rows]
        )

        def place(source):
            for col in range(2):
                if h == 0:
                    far_k[c, cols_of(col), cols_of(col)] = source(col)
                else:
                    far_v[2 * c + col] = source(col)

        pl.when(gets)(lambda: place(lambda col: zfar[h, o, col]))
        pl.when(jnp.logical_not(gets))(lambda: place(lambda col: site[h, col]))
        to_peer_core(h).start()

    for n in (1, 5, 2, 6):
        loads[n].wait()
    for b in range(2, nb + 1):
        kv_conv(b)
    loads[0].wait()
    loads[4].wait()

    row_ids = lax.broadcasted_iota(jnp.int32, (BLOCK, BLOCK), 0)
    col_ids = lax.broadcasted_iota(jnp.int32, (BLOCK, BLOCK), 1)
    causal = jnp.concatenate([row_ids >= col_ids] * per_group, 0)
    ones = jnp.ones((LOCAL * BLOCK, HEAD_DIM), jnp.bfloat16)

    def near(step, carry):
        b = jnp.where(step < nb - 2, step + 2, nb - 1 - step)

        @pl.when(b == 1)
        def _():
            @pl.when(has_prev)
            def _():
                for copy in edges:
                    copy.wait_recv()

            kv_conv(1)

        @pl.when(b == 0)
        def _():
            @pl.when(has_prev)
            def _():
                for copy in tails:
                    copy.wait_recv()

            kv_conv(0)

        bias = jnp.where((b == 0) & (d == 0), NEG, 0.0)
        base = pl.multiple_of(b * BLOCK, BLOCK)
        for g in range(groups):
            wide = slice(g * per_group * HEAD_DIM, (g + 1) * per_group * HEAD_DIM)
            cols = slice(g * HEAD_DIM, (g + 1) * HEAD_DIM)
            q = conv(qpad[pl.ds(base, BLOCK + HALO), wide], qt_ref[:, wide])
            q = jnp.concatenate(
                [q[:, h * HEAD_DIM : (h + 1) * HEAD_DIM] for h in range(per_group)], 0
            )
            qs[b, g // 2, :, cols_of(g % 2)] = q
            k = kvc[0, pl.ds(base, LOCAL * BLOCK), cols]
            v = kvc[1, pl.ds(base, LOCAL * BLOCK), cols]
            s = lax.dot_general(q, k, NT, preferred_element_type=jnp.float32)
            prev = s[:, :BLOCK] + bias
            mine = jnp.where(causal, s[:, BLOCK:], NEG)
            peak = jnp.max(jnp.maximum(prev, mine), axis=1, keepdims=True)
            p = jnp.concatenate(
                [jnp.exp2((prev - peak) * SCALE), jnp.exp2((mine - peak) * SCALE)], 1
            ).astype(jnp.bfloat16)
            acc_ref[b, g] = jnp.dot(
                p, jnp.concatenate([v, ones], 1), preferred_element_type=jnp.float32
            )
            max_ref[b, g] = jnp.broadcast_to(peak, (per_group * BLOCK, HEAD_DIM))

        pl.when(step == jnp.where(o == 0, FIRST_ROW_STEP, 0))(candidate_step)
        for h in range(2):
            if SITE_AFTER[h] is not None:
                pl.when(step == SITE_AFTER[h])(functools.partial(site_step, h))
        return carry

    lax.fori_loop(0, nb, near, 0)
    for h in range(2):
        if SITE_AFTER[h] is None:
            site_step(h)
    final_step(0)

    for b in range(nb):
        seen = jnp.int32(0)
        for e in range(entries):
            entry = list_ref[b, e]
            seen = jnp.where((entry >= 0) & (entry <= d * nb + b - LOCAL), 1, seen)
        bias_ref[b : b + 1, :] = jnp.full((1, 128), jnp.where(seen > 0, 0.0, NEG), jnp.float32)
    if nb < bias_ref.shape[0]:
        bias_ref[nb:, :] = jnp.zeros((bias_ref.shape[0] - nb, 128), jnp.float32)

    def far_stage(pair):
        for b in range(nb):
            distant_keys(qs, max_ref, max_ref, pbuf, far_k, bias_ref, pair, b)
        final_step(1)
        for b in range(nb):
            distant_values(acc_ref, max_ref, pbuf, far_v, pair, b, outb, 2 * pair * per_group)

    pl.when(first_core)(functools.partial(far_stage, 0))
    pl.when(second_core)(functools.partial(far_stage, 1))
    for h in range(2):
        from_peer_core(h).wait_recv()

    @pl.when(first_core & chip_prev)
    def _():
        for copy in flag_back:
            copy.wait_send()

    @pl.when(second_core)
    def _():
        flag_peer.wait_send()

        @pl.when(chip_next)
        def _():
            for k in range(2):
                for copy in rims[k]:
                    copy.wait_send()

    @pl.when(has_next)
    def _():
        for copy in edges + tails:
            copy.wait_send()

    for h in range(2):
        raws[h].wait_send()

        @pl.when(sums_own(h))
        def _():
            to_peer_site(h).wait_send()
            to_peer_col(h).wait_send()

        to_peer_core(h).wait_send()

        for table, copy in ((SUMS, to_site), (SPREADS, to_later)):
            for src, rows in table[h].items():

                @pl.when(o == src)
                def _():
                    for row in rows:
                        for col in range(2):
                            copy(h, row, col).wait_send()


def paired_call(arrays):
    block_list, q_proj, k_proj = arrays[:3]
    q_taps, k_taps, v_taps = arrays[4:]
    tokens, qw = q_proj.shape
    kvw = k_proj.shape[1]
    nb = tokens // BLOCK
    groups = kvw // HEAD_DIM
    rows = qw // kvw * BLOCK
    hw = kvw // 2
    piece = (BLOCK, hw // 2)
    dma = pltpu.SemaphoreType.DMA
    bf16, f32 = jnp.bfloat16, jnp.float32
    hbm_spec = pl.BlockSpec(memory_space=pltpu.HBM)
    scores = nb * groups * rows * (LOCAL + 1) * BLOCK
    vmem_spec = pl.BlockSpec(memory_space=pltpu.VMEM)
    partial_shapes = [
        ((tokens, qw), bf16),
        ((nb, groups // 2, rows, 2 * HEAD_DIM), bf16),
        ((nb, groups, rows, 2 * HEAD_DIM), f32),
        ((nb, groups, rows, HEAD_DIM), f32),
        ((groups // 2, 2 * BLOCK, hw), bf16),
        ((groups, BLOCK, HEAD_DIM), bf16),
        ((max(8, nb), 128), f32),
    ]
    partial = pl.pallas_call(
        paired_kernel,
        out_shape=[jax.ShapeDtypeStruct(*x) for x in partial_shapes],
        in_specs=[hbm_spec] * 7,
        out_specs=[vmem_spec] * 7,
        scratch_shapes=[
            pltpu.SMEM(block_list.shape, jnp.int32),
            pltpu.VMEM(q_taps.shape, f32),
            pltpu.VMEM(k_taps.shape, f32),
            pltpu.VMEM(v_taps.shape, f32),
            pltpu.VMEM((tokens + HALO, qw), bf16),
            pltpu.VMEM((2, tokens + BLOCK + HALO, kvw), bf16),
            pltpu.VMEM((2, tokens + BLOCK, kvw), bf16),
            pltpu.VMEM((nb, groups, rows, BLOCK), bf16),
            pltpu.VMEM((8, hw), jnp.int32),
            pltpu.VMEM((2, 8, hw), jnp.int32),
            pltpu.VMEM((2, 2 * tokens + HALO, hw), bf16),
            pltpu.VMEM((2, 2, *piece), bf16),
            pltpu.VMEM((2, *piece), bf16),
            pltpu.VMEM((2, ROWS, 2, *piece), bf16),
            pltpu.VMEM((2, 2, *piece), bf16),
            pltpu.VMEM((2, ROWS, 2, *piece), bf16),
            dma((7,)),
            dma((2,)),
            dma((3,)),
            dma((2,)),
            dma((2,)),
            dma((2,)),
            dma((2, 2)),
            dma((2,)),
            dma((5,)),
            dma((5,)),
            dma((2,)),
            dma((2,)),
            dma((2, ROWS, 2)),
            dma((2, ROWS, 2)),
            dma((2,)),
            dma((2,)),
            dma((2, ROWS, 2)),
            dma((2, ROWS, 2)),
            dma((2,)),
            dma((2,)),
            pltpu.SemaphoreType.REGULAR,
        ],
        compiler_params=pltpu.CompilerParams(
            collective_id=0, has_side_effects=True, vmem_limit_bytes=36 * 1024 * 1024
        ),
        cost_estimate=pl.CostEstimate(
            flops=4 * scores * HEAD_DIM,
            bytes_accessed=4 * tokens * qw + 4 * tokens * kvw,
            transcendentals=scores,
        ),
    )(*arrays)
    return pl.pallas_call(
        other_half_kernel,
        out_shape=jax.ShapeDtypeStruct((tokens, qw), bf16),
        in_specs=[vmem_spec] * 7,
        out_specs=hbm_spec,
        scratch_shapes=[
            pltpu.VMEM((nb, groups, rows, HEAD_DIM), f32),
            pltpu.VMEM((nb, groups, rows, BLOCK), bf16),
            pltpu.VMEM((tokens, qw // 2), bf16),
            dma,
            dma((nb,)),
        ],
        compiler_params=pltpu.CompilerParams(vmem_limit_bytes=36 * 1024 * 1024),
        cost_estimate=pl.CostEstimate(
            flops=scores * HEAD_DIM, bytes_accessed=2 * tokens * qw, transcendentals=scores // 6
        ),
    )(*partial)


def body(q_proj, k_proj, v_proj, q_taps, k_taps, v_taps, block_list):
    tokens, qw = q_proj.shape
    kvw = k_proj.shape[1]
    ni = lax.axis_size("inner")
    no = lax.axis_size("outer")
    nb = tokens // BLOCK
    groups = kvw // HEAD_DIM
    rows = qw // kvw * BLOCK
    slots = max(1, nb * ni * no // STRIDE)
    piece_rows = max(HALO, BLOCK // ni)
    piece_cols = BLOCK * kvw // (ni * piece_rows)
    piece = (piece_rows, piece_cols)
    dma = pltpu.SemaphoreType.DMA
    bf16, f32 = jnp.bfloat16, jnp.float32
    hbm_spec = pl.BlockSpec(memory_space=pltpu.HBM)
    scores = nb * groups * rows * (LOCAL + slots) * BLOCK
    arrays = [
        pltpu.with_memory_space_constraint(x, pltpu.HBM)
        for x in (block_list, q_proj, k_proj, v_proj, q_taps, k_taps, v_taps)
    ]
    paired = ni == 4 and no == ROWS and nb * ni * no == STRIDE and groups == 4 and nb >= 2
    if paired:
        return paired_call(arrays)
    return pl.pallas_call(
        functools.partial(kernel, ni, no),
        out_shape=jax.ShapeDtypeStruct((tokens, qw), bf16),
        in_specs=[hbm_spec] * 7,
        out_specs=pl.BlockSpec(memory_space=pltpu.VMEM),
        scratch_shapes=[
            pltpu.SMEM(block_list.shape, jnp.int32),
            pltpu.VMEM(q_taps.shape, f32),
            pltpu.VMEM(k_taps.shape, f32),
            pltpu.VMEM(v_taps.shape, f32),
            pltpu.VMEM((tokens + HALO, qw), bf16),
            pltpu.VMEM((2, tokens + BLOCK + HALO, kvw), bf16),
            pltpu.VMEM((2, tokens + BLOCK, kvw), bf16),
            pltpu.VMEM((nb, groups, rows, HEAD_DIM), bf16),
            pltpu.VMEM((nb, groups, rows, 2 * HEAD_DIM), f32),
            pltpu.VMEM((nb, groups, rows, HEAD_DIM), f32),
            pltpu.VMEM((nb, groups, rows, slots * BLOCK), bf16),
            pltpu.VMEM((max(8, nb), 128), f32),
            pltpu.VMEM((max(8, nb), 128), f32),
            pltpu.VMEM((2, BLOCK, kvw), bf16),
            pltpu.VMEM((2, ni, *piece), bf16),
            pltpu.VMEM((2, *piece), bf16),
            pltpu.VMEM((2, no, *piece), bf16),
            pltpu.VMEM((2, slots, *piece), bf16),
            pltpu.VMEM((2, slots, BLOCK, kvw), bf16),
            dma((7,)),
            dma((5,)),
            dma((5,)),
            dma,
            dma,
            dma((2, ni)),
            dma((2, ni)),
            dma((2, no)),
            dma((2, no)),
            dma((2, ni)),
            dma((2, ni)),
        ],
        compiler_params=pltpu.CompilerParams(
            collective_id=0, has_side_effects=True, vmem_limit_bytes=48 * 1024 * 1024
        ),
        cost_estimate=pl.CostEstimate(
            flops=4 * scores * HEAD_DIM,
            bytes_accessed=4 * tokens * qw + 4 * tokens * kvw,
            transcendentals=scores,
        ),
    )(*arrays)


def solution(mesh):
    rows = P(("groups", "outer", "inner"), None)
    return jax.shard_map(
        body,
        mesh=mesh,
        in_specs=(rows, rows, rows, P(), P(), P(), rows),
        out_specs=rows,
        check_vma=False,
    )
```

```python
import functools
import math

import jax
import jax.numpy as jnp
from jax import lax
from jax.experimental import pallas as pl
from jax.experimental.pallas import tpu as pltpu
from jax.sharding import PartitionSpec as P

HEAD_DIM = 128
BLOCK = 128
LOCAL = 2
STRIDE = 64
HALO = 16
NEG = -1e30
MESH = pl.DeviceIdType.MESH
SCALE = math.log2(math.e) / math.sqrt(HEAD_DIM)
NT = (((1,), (1,)), ((), ()))


def conv(padded, taps):
    wide = padded.astype(jnp.float32)
    total = taps[0:1] * wide[HALO:]
    for j in (1, 2):
        total = total + taps[j : j + 1] * pltpu.roll(wide, j, 0)[HALO:]
    return total.astype(jnp.bfloat16)


def kernel(
    ni, no, list_hbm, q_hbm, k_hbm, v_hbm, qt_hbm, kt_hbm, vt_hbm, outb,
    list_ref, qt_ref, kt_ref, vt_ref, qpad, kvpad, kvc, qs, acc_ref, max_ref, pbuf, wout, win, cand, rbuf, zpiece, zbuf,
    fsum, far, in_sem, tail_s, tail_r, w_s, w_r, sc_s, sc_r, z_s, z_r,
    g_s, g_r,
):
    tokens, qw = q_hbm.shape
    kvw = k_hbm.shape[1]
    groups = kvw // HEAD_DIM
    per_group = qw // kvw
    nb = tokens // BLOCK
    slots = far.shape[1]
    piece_rows, piece_cols = zpiece.shape[1:]
    col_parts = kvw // piece_cols
    before = BLOCK + HALO
    entries = list_ref.shape[1]
    o = lax.axis_index("outer")
    i = lax.axis_index("inner")
    d = o * ni + i
    last = ni * no - 1
    has_next = d < last
    has_prev = d > 0

    def chain(step):
        other = d + step
        return {"outer": other // ni, "inner": lax.rem(other, ni)}

    def inner_peer(r):
        return {"inner": lax.rem(i + r, ni)}

    loads = [
        pltpu.make_async_copy(q_hbm, qpad.at[pl.ds(HALO, tokens)], in_sem.at[0]),
        pltpu.make_async_copy(k_hbm, kvpad.at[0, pl.ds(before, tokens)], in_sem.at[1]),
        pltpu.make_async_copy(v_hbm, kvpad.at[1, pl.ds(before, tokens)], in_sem.at[2]),
        pltpu.make_async_copy(list_hbm, list_ref, in_sem.at[3]),
        pltpu.make_async_copy(qt_hbm, qt_ref, in_sem.at[4]),
        pltpu.make_async_copy(kt_hbm, kt_ref, in_sem.at[5]),
        pltpu.make_async_copy(vt_hbm, vt_ref, in_sem.at[6]),
    ]
    for n in (3, 1, 5, 2, 6, 0, 4):
        loads[n].start()

    barrier = pltpu.get_barrier_semaphore()
    for r in range(1, ni):
        pl.semaphore_signal(barrier, inc=1, device_id=inner_peer(r), device_id_type=MESH)
    for r in range(1, no):
        pl.semaphore_signal(
            barrier, inc=1, device_id={"outer": lax.rem(o + r, no)}, device_id_type=MESH
        )

    @pl.when(has_next)
    def _():
        pl.semaphore_signal(barrier, inc=1, device_id=chain(1), device_id_type=MESH)

    @pl.when(has_prev)
    def _():
        pl.semaphore_signal(barrier, inc=1, device_id=chain(-1), device_id_type=MESH)

    loads[3].wait()
    phase = jnp.int32(-1)
    for b in range(nb):
        for e in range(entries):
            entry = list_ref[b, e]
            distant = (entry >= 0) & (entry <= d * nb + b - LOCAL)
            phase = jnp.maximum(phase, jnp.where(distant, lax.rem(entry, STRIDE), -1))
    for b in range(nb):
        hit = lax.rem((d - 1) * nb + b + STRIDE, STRIDE) == phase
        wout[b : b + 1, :] = jnp.full((1, 128), jnp.where(hit, 1.0, 0.0), jnp.float32)
    if nb < wout.shape[0]:
        wout[nb:, :] = jnp.zeros((wout.shape[0] - nb, 128), jnp.float32)

    @pl.when(d == 0)
    def _():
        qpad[0:HALO, :] = jnp.zeros((HALO, qw), jnp.bfloat16)
        kvpad[:, 0:before, :] = jnp.zeros((2, before, kvw), jnp.bfloat16)

    @pl.when(d == last)
    def _():
        win[...] = jnp.zeros(win.shape, jnp.float32)

    fsum[...] = jnp.zeros(fsum.shape, jnp.bfloat16)

    w_copy = pltpu.make_async_remote_copy(
        wout, win, w_s, w_r, device_id=chain(-1), device_id_type=MESH
    )
    rim = pl.ds(tokens - HALO, HALO)
    body_rows = pl.ds(tokens - before, BLOCK)

    def to_next(src, dst, n):
        return pltpu.make_async_remote_copy(
            src, dst, tail_s.at[n], tail_r.at[n], device_id=chain(1), device_id_type=MESH
        )

    tails = [
        to_next(k_hbm.at[rim], kvpad.at[0, pl.ds(BLOCK, HALO)], 0),
        to_next(v_hbm.at[rim], kvpad.at[1, pl.ds(BLOCK, HALO)], 1),
        to_next(k_hbm.at[body_rows], kvpad.at[0, pl.ds(0, BLOCK)], 2),
        to_next(v_hbm.at[body_rows], kvpad.at[1, pl.ds(0, BLOCK)], 3),
        to_next(q_hbm.at[rim], qpad.at[pl.ds(0, HALO)], 4),
    ]

    def first_sends():
        pl.semaphore_wait(
            barrier,
            ni - 1 + no - 1 + jnp.where(has_next, 1, 0) + jnp.where(has_prev, 1, 0),
        )

        @pl.when(has_prev)
        def _():
            w_copy.start()

        @pl.when(has_next)
        def _():
            for copy in tails:
                copy.start()

    def kv_conv(b):
        rows = slice(b * BLOCK, b * BLOCK + before)
        dst = slice(b * BLOCK, (b + 1) * BLOCK)
        kvc[0, dst, :] = conv(kvpad[0, rows, :], kt_ref[...])
        kvc[1, dst, :] = conv(kvpad[1, rows, :], vt_ref[...])

    for n in (1, 5, 2, 6):
        loads[n].wait()
    for b in range(2, nb + 1):
        kv_conv(b)

    def candidate_step():
        @pl.when(has_prev)
        def _():
            tails[0].wait_recv()
            tails[1].wait_recv()

        kv_conv(1)

        @pl.when(has_next)
        def _():
            w_copy.wait_recv()

        for g in range(groups):
            cols = slice(g * HEAD_DIM, (g + 1) * HEAD_DIM)
            for half in range(2):
                total = jnp.zeros((BLOCK, HEAD_DIM), jnp.float32)
                for b in range(nb):
                    own = jnp.where(lax.rem(d * nb + b, STRIDE) == phase, 1.0, 0.0)
                    weight = jnp.maximum(win[b : b + 1, :], own)
                    rows = slice((b + 1) * BLOCK, (b + 2) * BLOCK)
                    total = total + weight * kvc[half, rows, cols].astype(jnp.float32)
                cand[half, :, cols] = total.astype(jnp.bfloat16)

        for half in range(2):
            for r in range(1, ni):
                scatter(half, r).start()

    def part(index):
        row = pl.multiple_of(index // col_parts * piece_rows, piece_rows)
        col = pl.multiple_of(lax.rem(index, col_parts) * piece_cols, piece_cols)
        return pl.ds(row, piece_rows), pl.ds(col, piece_cols)

    def scatter(half, r):
        return pltpu.make_async_remote_copy(
            cand.at[(half, *part(lax.rem(i + r, ni)))],
            rbuf.at[half, r],
            sc_s.at[half, r],
            sc_r.at[half, r],
            device_id=inner_peer(r),
            device_id_type=MESH,
        )

    def column(half, r):
        return pltpu.make_async_remote_copy(
            zpiece.at[half],
            zbuf.at[half, r],
            z_s.at[half, r],
            z_r.at[half, r],
            device_id={"outer": lax.rem(o + r, no)},
            device_id_type=MESH,
        )

    def gather(half, r):
        return pltpu.make_async_remote_copy(
            fsum.at[half],
            far.at[(half, slice(None), *part(i))],
            g_s.at[half, r],
            g_r.at[half, r],
            device_id=inner_peer(r),
            device_id_type=MESH,
        )

    def column_step(half):
        total = cand[(half, *part(i))].astype(jnp.float32)
        for r in range(1, ni):
            scatter(half, r).wait_recv()
            total = total + rbuf[half, r].astype(jnp.float32)
        zpiece[half] = total.astype(jnp.bfloat16)
        for r in range(1, no):
            pl.when(o + r < no)(column(half, r).start)

    def slot_of(row):
        return lax.rem(row * (ni * nb) // STRIDE, slots)

    def gather_step(half):
        fsum[half, slot_of(o)] = zpiece[half]
        for r in range(1, no):

            @pl.when(o >= r)
            def _():
                column(half, r).wait_recv()
                at = slot_of(o - r)
                fsum[half, at] = (
                    fsum[half, at].astype(jnp.float32) + zbuf[half, r].astype(jnp.float32)
                ).astype(jnp.bfloat16)

        for r in range(1, ni):
            gather(half, r).start()
        far[(half, slice(None), *part(i))] = fsum[half]

    def gather_wait(half):
        for r in range(1, ni):
            gather(half, r).wait_recv()

    loads[0].wait()
    loads[4].wait()

    row_ids = lax.broadcasted_iota(jnp.int32, (BLOCK, BLOCK), 0)
    col_ids = lax.broadcasted_iota(jnp.int32, (BLOCK, BLOCK), 1)
    causal = jnp.concatenate([row_ids >= col_ids] * per_group, 0)
    ones = jnp.ones((LOCAL * BLOCK, HEAD_DIM), jnp.bfloat16)

    def near(step, carry):
        b = jnp.where(step < nb - 2, step + 2, nb - 1 - step)

        @pl.when(b == 0)
        def _():
            @pl.when(has_prev)
            def _():
                tails[2].wait_recv()
                tails[3].wait_recv()
                tails[4].wait_recv()

            kv_conv(0)

        bias = jnp.where((b == 0) & (d == 0), NEG, 0.0)
        base = pl.multiple_of(b * BLOCK, BLOCK)
        for g in range(groups):
            wide = slice(g * per_group * HEAD_DIM, (g + 1) * per_group * HEAD_DIM)
            cols = slice(g * HEAD_DIM, (g + 1) * HEAD_DIM)
            q = conv(qpad[pl.ds(base, BLOCK + HALO), wide], qt_ref[:, wide])
            q = jnp.concatenate(
                [q[:, h * HEAD_DIM : (h + 1) * HEAD_DIM] for h in range(per_group)], 0
            )
            qs[b, g] = q
            k = kvc[0, pl.ds(base, LOCAL * BLOCK), cols]
            v = kvc[1, pl.ds(base, LOCAL * BLOCK), cols]
            s = lax.dot_general(q, k, NT, preferred_element_type=jnp.float32)
            prev = s[:, :BLOCK] + bias
            own = jnp.where(causal, s[:, BLOCK:], NEG)
            peak = jnp.max(jnp.maximum(prev, own), axis=1, keepdims=True)
            p = jnp.concatenate(
                [jnp.exp2((prev - peak) * SCALE), jnp.exp2((own - peak) * SCALE)], 1
            ).astype(jnp.bfloat16)
            acc_ref[b, g] = jnp.dot(
                p, jnp.concatenate([v, ones], 1), preferred_element_type=jnp.float32
            )
            max_ref[b, g] = jnp.broadcast_to(peak, (per_group * BLOCK, HEAD_DIM))

        pl.when(step == 0)(first_sends)
        pl.when(step == 1)(candidate_step)

        @pl.when(step == 2)
        def _():
            column_step(0)
            column_step(1)

        return carry

    lax.fori_loop(0, nb, near, 0)
    gather_step(0)
    gather_step(1)
    gather_wait(0)

    def distant_keys(b, carry):
        biases = []
        for n in range(slots):
            seen = jnp.int32(0)
            for e in range(entries):
                entry = list_ref[b, e]
                hit = (entry >= n * STRIDE) & (entry < (n + 1) * STRIDE)
                hit = hit & (entry <= d * nb + b - LOCAL)
                seen = jnp.where(hit, 1, seen)
            biases.append(jnp.where(seen > 0, 0.0, NEG))
        for g in range(groups):
            cols = slice(g * HEAD_DIM, (g + 1) * HEAD_DIM)
            q = qs[b, g]
            near_peak = max_ref[b, g]
            scores = []
            top = None
            for n in range(slots):
                s = lax.dot_general(q, far[0, n, :, cols], NT, preferred_element_type=jnp.float32)
                s = s + biases[n]
                scores.append(s)
                top = s if top is None else jnp.maximum(top, s)
            peak = jnp.maximum(near_peak, jnp.max(top, axis=1, keepdims=True))
            max_ref[b, g] = jnp.exp2((near_peak - peak) * SCALE)
            for n in range(slots):
                p = jnp.exp2((scores[n] - peak) * SCALE)
                pbuf[b, g, :, n * BLOCK : (n + 1) * BLOCK] = p.astype(jnp.bfloat16)
        return carry

    def distant_values(b, carry):
        base = pl.multiple_of(b * BLOCK, BLOCK)
        for g in range(groups):
            cols = slice(g * HEAD_DIM, (g + 1) * HEAD_DIM)
            both = acc_ref[b, g]
            shrink = max_ref[b, g]
            total = both[:, :HEAD_DIM] * shrink
            count = both[:, HEAD_DIM:] * shrink
            for n in range(slots):
                more = jnp.dot(
                    pbuf[b, g, :, n * BLOCK : (n + 1) * BLOCK],
                    jnp.concatenate([far[1, n, :, cols], ones[:BLOCK]], 1),
                    preferred_element_type=jnp.float32,
                )
                total = total + more[:, :HEAD_DIM]
                count = count + more[:, HEAD_DIM:]
            mixed = (total / count).astype(jnp.bfloat16)
            for h in range(per_group):
                head = g * per_group + h
                outb[pl.ds(base, BLOCK), head * HEAD_DIM : (head + 1) * HEAD_DIM] = mixed[
                    h * BLOCK : (h + 1) * BLOCK
                ]
        return carry

    lax.fori_loop(0, nb, distant_keys, 0)
    gather_wait(1)
    lax.fori_loop(0, nb, distant_values, 0)

    @pl.when(has_prev)
    def _():
        w_copy.wait_send()

    @pl.when(has_next)
    def _():
        for copy in tails:
            copy.wait_send()

    for half in range(2):
        for r in range(1, ni):
            scatter(half, r).wait_send()
            gather(half, r).wait_send()
        for r in range(1, no):
            pl.when(o + r < no)(column(half, r).wait_send)


ROWS = 4
SUMS = ({0: (1,), 2: (3,)}, {0: (2,), 1: (2,)})
SPREADS = ({1: (3, 2)}, {2: (3, 1)})
TAKEN = ((), (1,))
FIRST_ROW_STEP = 1
SITE_AFTER = (2, 2)
LATE_TAILS = False
LATE = ((2, 3), (1, 3), (0, 2))


def dests(row, late):
    rows = {r for table in (*SUMS, *SPREADS) for r in table.get(row, ())}
    return sorted(r for r in rows if ((row, r) in LATE) == late)


def origins(row, late):
    return [r for r in range(ROWS) if row in dests(r, late)]


def distant_keys(qs, peaks, max_ref, pbuf, far_k, bias_ref, pair, b):
    both = lax.dot_general(qs[b, pair], far_k[pair], NT, preferred_element_type=jnp.float32)
    bias = bias_ref[b : b + 1, :]
    for n in range(2):
        g = 2 * pair + n
        s = both[:, n * BLOCK : (n + 1) * BLOCK] + bias
        near_peak = peaks[b, g]
        peak = jnp.maximum(near_peak, jnp.max(s, axis=1, keepdims=True))
        max_ref[b, g] = jnp.exp2((near_peak - peak) * SCALE)
        pbuf[b, g] = jnp.exp2((s - peak) * SCALE).astype(jnp.bfloat16)


def distant_values(acc_ref, max_ref, pbuf, far_v, pair, b, dst, first_head):
    per_group = acc_ref.shape[2] // BLOCK
    ones = jnp.ones((BLOCK, HEAD_DIM), jnp.bfloat16)
    for n in range(2):
        g = 2 * pair + n
        shrink = max_ref[b, g]
        more = jnp.dot(
            pbuf[b, g],
            jnp.concatenate([far_v[g], ones], 1),
            preferred_element_type=jnp.float32,
        )
        total = acc_ref[b, g, :, :HEAD_DIM] * shrink + more[:, :HEAD_DIM]
        count = acc_ref[b, g, :, HEAD_DIM:] * shrink + more[:, HEAD_DIM:]
        mixed = (total / count).astype(jnp.bfloat16)
        for h in range(per_group):
            head = first_head + n * per_group + h
            dst[b * BLOCK : (b + 1) * BLOCK, head * HEAD_DIM : (head + 1) * HEAD_DIM] = mixed[
                h * BLOCK : (h + 1) * BLOCK
            ]


def other_half_kernel(
    own_out, qs, acc_ref, peaks, far_k, far_v, bias_ref, out, max_ref, pbuf, half_out, own_sem, out_sem
):
    nb = qs.shape[0]
    tokens, qw = own_out.shape
    wide = qw // 2
    c = lax.rem(lax.axis_index("inner"), 2)

    def half(pair):
        own_cols = pl.ds((1 - pair) * wide, wide)
        cols = pl.ds(pair * wide, wide)
        own_copy = pltpu.make_async_copy(own_out.at[:, own_cols], out.at[:, own_cols], own_sem)
        own_copy.start()
        copies = []
        distant_keys(qs, peaks, max_ref, pbuf, far_k, bias_ref, pair, 0)
        for b in range(nb):
            if b + 1 < nb:
                distant_keys(qs, peaks, max_ref, pbuf, far_k, bias_ref, pair, b + 1)
            rows = pl.ds(b * BLOCK, BLOCK)
            distant_values(acc_ref, max_ref, pbuf, far_v, pair, b, half_out, 0)
            copies.append(
                pltpu.make_async_copy(half_out.at[rows], out.at[rows, cols], out_sem.at[b])
            )
            copies[-1].start()
        for copy in copies:
            copy.wait()
        own_copy.wait()

    pl.when(c == 0)(lambda: half(1))
    pl.when(c == 1)(lambda: half(0))


def paired_kernel(
    list_hbm, q_hbm, k_hbm, v_hbm, qt_hbm, kt_hbm, vt_hbm,
    outb, qs, acc_ref, max_ref, far_k, far_v, bias_ref,
    list_ref, qt_ref, kt_ref, vt_ref, qpad, kvpad, kvc, pbuf,
    flag_out, flag_in, chip, cand, rrow, rother, site, zfar,
    in_sem, own_sem, fl_s, fl_r, raw_s, raw_r, rim_s, rim_r, tail_s, tail_r,
    a_s, a_r, b_s, b_r, c_s, c_r, d_s, d_r, e_s, e_r, ready,
):
    tokens, qw = q_hbm.shape
    kvw = k_hbm.shape[1]
    groups = kvw // HEAD_DIM
    hw = kvw // 2
    quarter = hw // 2
    per_group = qw // kvw
    nb = tokens // BLOCK
    before = BLOCK + HALO
    entries = list_ref.shape[1]
    o = lax.axis_index("outer")
    i = lax.axis_index("inner")
    y = i // 2
    c = lax.rem(i, 2)
    m = o * 2 + y
    no = ROWS
    last_chip = no * 2 - 1
    d = o * 4 + i
    has_next = d < 4 * no - 1
    has_prev = d > 0
    chip_next = m < last_chip
    chip_prev = m > 0
    first_core = c == 0
    second_core = c == 1

    def chip_core(step, core):
        other = m + step
        return {"outer": other // 2, "inner": lax.rem(other, 2) * 2 + core}

    def at(row, col):
        return {"outer": row, "inner": col * 2 + c}

    peer_core = {"inner": i + 1 - 2 * c}
    peer_y = {"inner": lax.rem(i + 2, 4)}
    next_device = {"outer": (d + 1) // 4, "inner": lax.rem(d + 1, 4)}

    barrier = pltpu.get_barrier_semaphore()

    def greet(device):
        pl.semaphore_signal(barrier, inc=1, device_id=device, device_id_type=MESH)

    def call(device):
        pl.semaphore_signal(ready, inc=1, device_id=device, device_id_type=MESH)

    loads = [
        pltpu.make_async_copy(q_hbm, qpad.at[pl.ds(HALO, tokens)], in_sem.at[0]),
        pltpu.make_async_copy(k_hbm, kvpad.at[0, pl.ds(before, tokens)], in_sem.at[1]),
        pltpu.make_async_copy(v_hbm, kvpad.at[1, pl.ds(before, tokens)], in_sem.at[2]),
        pltpu.make_async_copy(list_hbm, list_ref, in_sem.at[3]),
        pltpu.make_async_copy(qt_hbm, qt_ref, in_sem.at[4]),
        pltpu.make_async_copy(kt_hbm, kt_ref, in_sem.at[5]),
        pltpu.make_async_copy(vt_hbm, vt_ref, in_sem.at[6]),
    ]
    half_cols = pl.ds(pl.multiple_of(c * hw, hw), hw)
    peer_cols = pl.ds(pl.multiple_of((1 - c) * hw, hw), hw)
    chip_rows = pl.ds(pl.multiple_of(HALO + c * tokens, HALO), tokens)
    own = [
        pltpu.make_async_copy(x.at[:, half_cols], chip.at[h, chip_rows], own_sem.at[h])
        for h, x in enumerate((k_hbm, v_hbm))
    ]
    loads[3].start()
    greet(peer_core)
    greet(peer_y)

    late_next = (y == 1) & functools.reduce(
        jnp.logical_or, [o == row for row in range(no - 1) if (row, row + 1) in LATE], o < 0
    )
    late_prev = (y == 0) & functools.reduce(
        jnp.logical_or, [o == row + 1 for row in range(no - 1) if (row, row + 1) in LATE], o < 0
    )

    @pl.when(chip_next)
    def _():
        greet(chip_core(1, 0))
        pl.when(second_core & late_next)(lambda: greet(chip_core(1, 1)))

    pl.when(chip_prev & jnp.logical_not(late_prev))(lambda: greet(chip_core(-1, 1)))
    for row in range(no):

        @pl.when(o == row)
        def _():
            for other in origins(row, False) + dests(row, True):
                greet(at(other, 0))
                greet(at(other, 1))

    for n in (1, 5, 2, 6):
        loads[n].start()
    for copy in own:
        copy.start()
    for n in (0, 4):
        loads[n].start()

    def remote(src, dst, send, recv, device):
        return pltpu.make_async_remote_copy(
            src, dst, send, recv, device_id=device, device_id_type=MESH
        )

    flag_back = [
        remote(flag_out, flag_in.at[0], fl_s.at[k], fl_r.at[0], chip_core(-1, k)) for k in range(2)
    ]
    flag_peer = remote(flag_out, flag_in.at[1], fl_s.at[2], fl_r.at[1], peer_core)
    raws = [
        remote(x.at[:, peer_cols], chip.at[h, chip_rows], raw_s.at[h], raw_r.at[h], peer_core)
        for h, x in enumerate((k_hbm, v_hbm))
    ]
    rim = pl.ds(tokens - HALO, HALO)
    rims = [
        [
            remote(
                x.at[rim, k * hw : (k + 1) * hw],
                chip.at[h, pl.ds(0, HALO)],
                rim_s.at[k, h],
                rim_r.at[h],
                chip_core(1, k),
            )
            for h, x in enumerate((k_hbm, v_hbm))
        ]
        for k in range(2)
    ]
    body_rows = pl.ds(tokens - before, BLOCK)

    def to_next(n, src, dst):
        return remote(src, dst, tail_s.at[n], tail_r.at[n], next_device)

    edges = [
        to_next(h, x.at[rim], kvpad.at[h, pl.ds(BLOCK, HALO)]) for h, x in enumerate((k_hbm, v_hbm))
    ]
    tails = [
        to_next(2 + h, x.at[body_rows], kvpad.at[h, pl.ds(0, BLOCK)])
        for h, x in enumerate((k_hbm, v_hbm))
    ] + [to_next(4, q_hbm.at[rim], qpad.at[pl.ds(0, HALO)])]

    @pl.when(jnp.logical_not(has_prev))
    def _():
        qpad[0:HALO, :] = jnp.zeros((HALO, qw), jnp.bfloat16)
        kvpad[:, 0:before, :] = jnp.zeros((2, before, kvw), jnp.bfloat16)

    @pl.when(jnp.logical_not(chip_prev))
    def _():
        chip[:, 0:HALO, :] = jnp.zeros((2, HALO, hw), jnp.bfloat16)

    far_k[...] = jnp.zeros(far_k.shape, jnp.bfloat16)

    @pl.when(jnp.logical_not(chip_next))
    def _():
        flag_in[0] = jnp.full(flag_in.shape[1:], -1, jnp.int32)

    @pl.when(second_core)
    def _():
        flag_in[1] = jnp.full(flag_in.shape[1:], -1, jnp.int32)

    expected = 2 + jnp.where(chip_prev & first_core, 2, 0)
    expected = expected + jnp.where(chip_prev & late_prev & second_core, 1, 0)
    sends_on = second_core & chip_next
    expected = expected + jnp.where(sends_on & jnp.logical_not(late_next), 2, 0)
    awaited = jnp.where(sends_on & late_next, 2, 0)
    for row in range(no):
        met = 2 * len(dests(row, False) + origins(row, True))
        expected = expected + jnp.where(o == row, met, 0)
        awaited = awaited + jnp.where(o == row, 2 * len(dests(row, True)), 0)
    pl.semaphore_wait(barrier, expected)
    pl.when(chip_prev & late_prev)(lambda: call(chip_core(-1, 1)))
    for row in range(no):
        if origins(row, True):

            @pl.when(o == row)
            def _():
                for src in origins(row, True):
                    call(at(src, 0))
                    call(at(src, 1))

    for copy in raws:
        copy.start()

    loads[3].wait()
    phase = jnp.int32(-1)
    for b in range(nb):
        for e in range(entries):
            entry = list_ref[b, e]
            distant = (entry >= 0) & (entry <= d * nb + b - LOCAL)
            phase = jnp.maximum(phase, jnp.where(distant, lax.rem(entry, STRIDE), -1))
    flag_out[...] = jnp.full(flag_out.shape, phase, jnp.int32)

    @pl.when(first_core & chip_prev)
    def _():
        for copy in flag_back:
            copy.start()

    pl.when(second_core)(flag_peer.start)
    def next_sends():
        @pl.when(sends_on)
        def _():
            for h in range(2):
                for k in range(2):
                    rims[k][h].start()

        @pl.when(has_next)
        def _():
            for copy in edges:
                copy.start()

    def tail_sends():
        @pl.when(has_next)
        def _():
            for copy in tails:
                copy.start()

    held_back = sends_on & late_next
    pl.when(jnp.logical_not(held_back))(next_sends)
    if not LATE_TAILS:
        pl.when(jnp.logical_not(held_back))(tail_sends)

    def kv_conv(b):
        rows = slice(b * BLOCK, b * BLOCK + before)
        dst = slice(b * BLOCK, (b + 1) * BLOCK)
        kvc[0, dst, :] = conv(kvpad[0, rows, :], kt_ref[...])
        kvc[1, dst, :] = conv(kvpad[1, rows, :], vt_ref[...])

    def cols_of(col):
        return slice(col * quarter, (col + 1) * quarter)

    def to_peer_site(h):
        return remote(cand.at[h, 1 - y], rrow.at[h], a_s.at[h], a_r.at[h], peer_y)

    def to_site(h, row, col):
        return remote(
            cand.at[h, col], rother.at[h, o, y], b_s.at[h, row, col], b_r.at[h, o, y], at(row, col)
        )

    def at_site(h, src, col):
        return remote(
            cand.at[h, col], rother.at[h, src, col], b_s.at[h, 0, col], b_r.at[h, src, col], peer_y
        )

    def to_peer_col(h):
        return remote(site.at[h, y], site.at[h, y], c_s.at[h], c_r.at[h], peer_y)

    def from_peer_col(h):
        return remote(site.at[h, 1 - y], site.at[h, 1 - y], c_s.at[h], c_r.at[h], peer_y)

    def to_later(h, row, col):
        return remote(
            site.at[h, y], zfar.at[h, o, y], d_s.at[h, row, col], d_r.at[h, o, y], at(row, col)
        )

    def from_earlier(h, src, col):
        return remote(
            site.at[h, y], zfar.at[h, src, col], d_s.at[h, 0, 0], d_r.at[h, src, col], peer_y
        )

    def core_swap(h, core):
        if h == 0:
            part = far_k.at[core]
        else:
            part = far_v.at[pl.ds(2 * core, 2)]
        return remote(part, part, e_s.at[h], e_r.at[h], peer_core)

    def to_peer_core(h):
        return core_swap(h, c)

    def from_peer_core(h):
        return core_swap(h, 1 - c)

    def sums_own(h):
        return functools.reduce(jnp.logical_and, [o != row for row in TAKEN[h]], o >= 0)

    def candidate_step():
        pl.when(awaited > 0)(lambda: pl.semaphore_wait(ready, awaited))
        pl.when(held_back)(next_sends)

        @pl.when(chip_next)
        def _():
            remote(flag_out, flag_in.at[0], fl_s.at[0], fl_r.at[0], peer_core).wait_recv()

        @pl.when(first_core)
        def _():
            flag_peer.wait_recv()

        known = jnp.maximum(jnp.maximum(flag_in[0, 0:1, :], flag_in[1, 0:1, :]), phase)
        first = m * 2 * nb
        weights = [
            jnp.where(known == first + b, 1.0, 0.0).astype(jnp.bfloat16) for b in range(2 * nb)
        ]
        for h, taps in enumerate((kt_ref, vt_ref)):
            own[h].wait()
            raws[h].wait_recv()

            @pl.when(chip_prev)
            def _():
                rims[0][h].wait_recv()

            raw = weights[0] * chip[h, 0:before, :]
            for b in range(1, 2 * nb):
                raw = raw + weights[b] * chip[h, b * BLOCK : b * BLOCK + before, :]
            total = conv(raw, taps[:, half_cols])
            for col in range(2):
                cand[h, col] = total[:, cols_of(col)]

            for src, rows in SUMS[h].items():

                @pl.when(o == src)
                def _():
                    for row in rows:
                        for col in range(2):
                            to_site(h, row, col).start()

            pl.when(sums_own(h))(to_peer_site(h).start)

        if LATE_TAILS:
            tail_sends()
        else:
            pl.when(held_back)(tail_sends)

    def site_step(h):
        pl.when(sums_own(h))(functools.partial(own_site_step, h))

    def own_site_step(h):
        to_peer_site(h).wait_recv()
        site[h, y] = cand[h, y] + rrow[h]
        for row in range(no):
            sources = [src for src, rows in SUMS[h].items() if row in rows]
            if sources:

                @pl.when(o == row)
                def _():
                    for src in sources:
                        for col in range(2):
                            at_site(h, src, col).wait_recv()
                            site[h, y] = site[h, y] + rother[h, src, col]

        for src, rows in SPREADS[h].items():

            @pl.when(o == src)
            def _():
                for row in rows:
                    for col in range(2):
                        to_later(h, row, col).start()

        to_peer_col(h).start()

    def final_step(h):
        pl.when(sums_own(h))(from_peer_col(h).wait_recv)
        for src, rows in SPREADS[h].items():
            for row in rows:

                @pl.when(o == row)
                def _():
                    for col in range(2):
                        from_earlier(h, src, col).wait_recv()
                        if row in TAKEN[h]:
                            zfar[h, o, col] = zfar[h, src, col]
                        else:
                            zfar[h, o, col] = zfar[h, src, col] + site[h, col]

        gets = functools.reduce(
            jnp.logical_or, [o == row for rows in SPREADS[h].values() for row in rows]
        )

        def place(source):
            for col in range(2):
                if h == 0:
                    far_k[c, cols_of(col), cols_of(col)] = source(col)
                else:
                    far_v[2 * c + col] = source(col)

        pl.when(gets)(lambda: place(lambda col: zfar[h, o, col]))
        pl.when(jnp.logical_not(gets))(lambda: place(lambda col: site[h, col]))
        to_peer_core(h).start()

    for n in (1, 5, 2, 6):
        loads[n].wait()
    for b in range(2, nb + 1):
        kv_conv(b)
    loads[0].wait()
    loads[4].wait()

    row_ids = lax.broadcasted_iota(jnp.int32, (BLOCK, BLOCK), 0)
    col_ids = lax.broadcasted_iota(jnp.int32, (BLOCK, BLOCK), 1)
    causal = jnp.concatenate([row_ids >= col_ids] * per_group, 0)
    ones = jnp.ones((LOCAL * BLOCK, HEAD_DIM), jnp.bfloat16)

    def near(step, carry):
        b = jnp.where(step < nb - 2, step + 2, nb - 1 - step)

        @pl.when(b == 1)
        def _():
            @pl.when(has_prev)
            def _():
                for copy in edges:
                    copy.wait_recv()

            kv_conv(1)

        @pl.when(b == 0)
        def _():
            @pl.when(has_prev)
            def _():
                for copy in tails:
                    copy.wait_recv()

            kv_conv(0)

        bias = jnp.where((b == 0) & (d == 0), NEG, 0.0)
        base = pl.multiple_of(b * BLOCK, BLOCK)
        for g in range(groups):
            wide = slice(g * per_group * HEAD_DIM, (g + 1) * per_group * HEAD_DIM)
            cols = slice(g * HEAD_DIM, (g + 1) * HEAD_DIM)
            q = conv(qpad[pl.ds(base, BLOCK + HALO), wide], qt_ref[:, wide])
            q = jnp.concatenate(
                [q[:, h * HEAD_DIM : (h + 1) * HEAD_DIM] for h in range(per_group)], 0
            )
            qs[b, g // 2, :, cols_of(g % 2)] = q
            k = kvc[0, pl.ds(base, LOCAL * BLOCK), cols]
            v = kvc[1, pl.ds(base, LOCAL * BLOCK), cols]
            s = lax.dot_general(q, k, NT, preferred_element_type=jnp.float32)
            prev = s[:, :BLOCK] + bias
            mine = jnp.where(causal, s[:, BLOCK:], NEG)
            peak = jnp.max(jnp.maximum(prev, mine), axis=1, keepdims=True)
            p = jnp.concatenate(
                [jnp.exp2((prev - peak) * SCALE), jnp.exp2((mine - peak) * SCALE)], 1
            ).astype(jnp.bfloat16)
            acc_ref[b, g] = jnp.dot(
                p, jnp.concatenate([v, ones], 1), preferred_element_type=jnp.float32
            )
            max_ref[b, g] = jnp.broadcast_to(peak, (per_group * BLOCK, HEAD_DIM))

        pl.when(step == jnp.where(o == 0, FIRST_ROW_STEP, 0))(candidate_step)
        for h in range(2):
            if SITE_AFTER[h] is not None:
                pl.when(step == SITE_AFTER[h])(functools.partial(site_step, h))
        return carry

    lax.fori_loop(0, nb, near, 0)
    for h in range(2):
        if SITE_AFTER[h] is None:
            site_step(h)
    final_step(0)

    for b in range(nb):
        seen = jnp.int32(0)
        for e in range(entries):
            entry = list_ref[b, e]
            seen = jnp.where((entry >= 0) & (entry <= d * nb + b - LOCAL), 1, seen)
        bias_ref[b : b + 1, :] = jnp.full((1, 128), jnp.where(seen > 0, 0.0, NEG), jnp.float32)
    if nb < bias_ref.shape[0]:
        bias_ref[nb:, :] = jnp.zeros((bias_ref.shape[0] - nb, 128), jnp.float32)

    def far_stage(pair):
        for b in range(nb):
            distant_keys(qs, max_ref, max_ref, pbuf, far_k, bias_ref, pair, b)
        final_step(1)
        for b in range(nb):
            distant_values(acc_ref, max_ref, pbuf, far_v, pair, b, outb, 2 * pair * per_group)

    pl.when(first_core)(functools.partial(far_stage, 0))
    pl.when(second_core)(functools.partial(far_stage, 1))
    for h in range(2):
        from_peer_core(h).wait_recv()

    @pl.when(first_core & chip_prev)
    def _():
        for copy in flag_back:
            copy.wait_send()

    @pl.when(second_core)
    def _():
        flag_peer.wait_send()

        @pl.when(chip_next)
        def _():
            for k in range(2):
                for copy in rims[k]:
                    copy.wait_send()

    @pl.when(has_next)
    def _():
        for copy in edges + tails:
            copy.wait_send()

    for h in range(2):
        raws[h].wait_send()

        @pl.when(sums_own(h))
        def _():
            to_peer_site(h).wait_send()
            to_peer_col(h).wait_send()

        to_peer_core(h).wait_send()

        for table, copy in ((SUMS, to_site), (SPREADS, to_later)):
            for src, rows in table[h].items():

                @pl.when(o == src)
                def _():
                    for row in rows:
                        for col in range(2):
                            copy(h, row, col).wait_send()


def paired_call(arrays):
    block_list, q_proj, k_proj = arrays[:3]
    q_taps, k_taps, v_taps = arrays[4:]
    tokens, qw = q_proj.shape
    kvw = k_proj.shape[1]
    nb = tokens // BLOCK
    groups = kvw // HEAD_DIM
    rows = qw // kvw * BLOCK
    hw = kvw // 2
    piece = (BLOCK, hw // 2)
    dma = pltpu.SemaphoreType.DMA
    bf16, f32 = jnp.bfloat16, jnp.float32
    hbm_spec = pl.BlockSpec(memory_space=pltpu.HBM)
    scores = nb * groups * rows * (LOCAL + 1) * BLOCK
    vmem_spec = pl.BlockSpec(memory_space=pltpu.VMEM)
    partial_shapes = [
        ((tokens, qw), bf16),
        ((nb, groups // 2, rows, 2 * HEAD_DIM), bf16),
        ((nb, groups, rows, 2 * HEAD_DIM), f32),
        ((nb, groups, rows, HEAD_DIM), f32),
        ((groups // 2, 2 * BLOCK, hw), bf16),
        ((groups, BLOCK, HEAD_DIM), bf16),
        ((max(8, nb), 128), f32),
    ]
    partial = pl.pallas_call(
        paired_kernel,
        out_shape=[jax.ShapeDtypeStruct(*x) for x in partial_shapes],
        in_specs=[hbm_spec] * 7,
        out_specs=[vmem_spec] * 7,
        scratch_shapes=[
            pltpu.SMEM(block_list.shape, jnp.int32),
            pltpu.VMEM(q_taps.shape, f32),
            pltpu.VMEM(k_taps.shape, f32),
            pltpu.VMEM(v_taps.shape, f32),
            pltpu.VMEM((tokens + HALO, qw), bf16),
            pltpu.VMEM((2, tokens + BLOCK + HALO, kvw), bf16),
            pltpu.VMEM((2, tokens + BLOCK, kvw), bf16),
            pltpu.VMEM((nb, groups, rows, BLOCK), bf16),
            pltpu.VMEM((8, hw), jnp.int32),
            pltpu.VMEM((2, 8, hw), jnp.int32),
            pltpu.VMEM((2, 2 * tokens + HALO, hw), bf16),
            pltpu.VMEM((2, 2, *piece), bf16),
            pltpu.VMEM((2, *piece), bf16),
            pltpu.VMEM((2, ROWS, 2, *piece), bf16),
            pltpu.VMEM((2, 2, *piece), bf16),
            pltpu.VMEM((2, ROWS, 2, *piece), bf16),
            dma((7,)),
            dma((2,)),
            dma((3,)),
            dma((2,)),
            dma((2,)),
            dma((2,)),
            dma((2, 2)),
            dma((2,)),
            dma((5,)),
            dma((5,)),
            dma((2,)),
            dma((2,)),
            dma((2, ROWS, 2)),
            dma((2, ROWS, 2)),
            dma((2,)),
            dma((2,)),
            dma((2, ROWS, 2)),
            dma((2, ROWS, 2)),
            dma((2,)),
            dma((2,)),
            pltpu.SemaphoreType.REGULAR,
        ],
        compiler_params=pltpu.CompilerParams(
            collective_id=0, has_side_effects=True, vmem_limit_bytes=36 * 1024 * 1024
        ),
        cost_estimate=pl.CostEstimate(
            flops=4 * scores * HEAD_DIM,
            bytes_accessed=4 * tokens * qw + 4 * tokens * kvw,
            transcendentals=scores,
        ),
    )(*arrays)
    return pl.pallas_call(
        other_half_kernel,
        out_shape=jax.ShapeDtypeStruct((tokens, qw), bf16),
        in_specs=[vmem_spec] * 7,
        out_specs=hbm_spec,
        scratch_shapes=[
            pltpu.VMEM((nb, groups, rows, HEAD_DIM), f32),
            pltpu.VMEM((nb, groups, rows, BLOCK), bf16),
            pltpu.VMEM((tokens, qw // 2), bf16),
            dma,
            dma((nb,)),
        ],
        compiler_params=pltpu.CompilerParams(vmem_limit_bytes=36 * 1024 * 1024),
        cost_estimate=pl.CostEstimate(
            flops=scores * HEAD_DIM, bytes_accessed=2 * tokens * qw, transcendentals=scores // 6
        ),
    )(*partial)


def body(q_proj, k_proj, v_proj, q_taps, k_taps, v_taps, block_list):
    tokens, qw = q_proj.shape
    kvw = k_proj.shape[1]
    ni = lax.axis_size("inner")
    no = lax.axis_size("outer")
    nb = tokens // BLOCK
    groups = kvw // HEAD_DIM
    rows = qw // kvw * BLOCK
    slots = max(1, nb * ni * no // STRIDE)
    piece_rows = max(HALO, BLOCK // ni)
    piece_cols = BLOCK * kvw // (ni * piece_rows)
    piece = (piece_rows, piece_cols)
    dma = pltpu.SemaphoreType.DMA
    bf16, f32 = jnp.bfloat16, jnp.float32
    hbm_spec = pl.BlockSpec(memory_space=pltpu.HBM)
    scores = nb * groups * rows * (LOCAL + slots) * BLOCK
    arrays = [
        pltpu.with_memory_space_constraint(x, pltpu.HBM)
        for x in (block_list, q_proj, k_proj, v_proj, q_taps, k_taps, v_taps)
    ]
    paired = ni == 4 and no == ROWS and nb * ni * no == STRIDE and groups == 4 and nb >= 2
    if paired:
        return paired_call(arrays)
    return pl.pallas_call(
        functools.partial(kernel, ni, no),
        out_shape=jax.ShapeDtypeStruct((tokens, qw), bf16),
        in_specs=[hbm_spec] * 7,
        out_specs=pl.BlockSpec(memory_space=pltpu.VMEM),
        scratch_shapes=[
            pltpu.SMEM(block_list.shape, jnp.int32),
            pltpu.VMEM(q_taps.shape, f32),
            pltpu.VMEM(k_taps.shape, f32),
            pltpu.VMEM(v_taps.shape, f32),
            pltpu.VMEM((tokens + HALO, qw), bf16),
            pltpu.VMEM((2, tokens + BLOCK + HALO, kvw), bf16),
            pltpu.VMEM((2, tokens + BLOCK, kvw), bf16),
            pltpu.VMEM((nb, groups, rows, HEAD_DIM), bf16),
            pltpu.VMEM((nb, groups, rows, 2 * HEAD_DIM), f32),
            pltpu.VMEM((nb, groups, rows, HEAD_DIM), f32),
            pltpu.VMEM((nb, groups, rows, slots * BLOCK), bf16),
            pltpu.VMEM((max(8, nb), 128), f32),
            pltpu.VMEM((max(8, nb), 128), f32),
            pltpu.VMEM((2, BLOCK, kvw), bf16),
            pltpu.VMEM((2, ni, *piece), bf16),
            pltpu.VMEM((2, *piece), bf16),
            pltpu.VMEM((2, no, *piece), bf16),
            pltpu.VMEM((2, slots, *piece), bf16),
            pltpu.VMEM((2, slots, BLOCK, kvw), bf16),
            dma((7,)),
            dma((5,)),
            dma((5,)),
            dma,
            dma,
            dma((2, ni)),
            dma((2, ni)),
            dma((2, no)),
            dma((2, no)),
            dma((2, ni)),
            dma((2, ni)),
        ],
        compiler_params=pltpu.CompilerParams(
            collective_id=0, has_side_effects=True, vmem_limit_bytes=48 * 1024 * 1024
        ),
        cost_estimate=pl.CostEstimate(
            flops=4 * scores * HEAD_DIM,
            bytes_accessed=4 * tokens * qw + 4 * tokens * kvw,
            transcendentals=scores,
        ),
    )(*arrays)


def solution(mesh):
    rows = P(("groups", "outer", "inner"), None)
    return jax.shard_map(
        body,
        mesh=mesh,
        in_specs=(rows, rows, rows, P(), P(), P(), rows),
        out_specs=rows,
        check_vma=False,
    )
```
